256 devices in a mesh: gx: 32 (over z, y), col: 8 (over x, core).
Axes of the slice: x: 4, y: 4, z: 8, core: 2. Of those that a mesh axis runs over, the one named last changes fastest.
Arguments:
- propagator: float32 [8, 64, 512, 256], P('col', None, 'gx'), may hold values from -4 to 4
- complement: bfloat16 [8, 2, 64, 512, 256], P('col', None, None, 'gx'), may hold values from -0.75 to 0.75
- labels: int32 [8, 2], P('col'), may hold values from 0 to 1
- absorption: float32 [2, 512, 256], P(None, 'gx'), may hold values from 0 to 2048
- to_ordinates: float32 [64, 64], replicated, may hold values from -0.75 to 0.75
- to_modes: float32 [64, 64], replicated, may hold values from -0.75 to 0.75
- upwind: float32 [64], replicated, may hold values from 32 to 4096
- mode_decay: float32 [2, 64], replicated, may hold values from 0.3 to 1
Outputs:
- propagated: float32 [8, 64, 512, 256], P('col', None, 'gx')
- segment_density: float32 [2, 512, 256], P(None, 'gx')
The draws below stay inside these ranges and needn't reach their ends.
All inputs are finite; a program needn't handle non-finite values.
Results may differ from the reference program's by a relative error of at most 0.0003.
Values sent between devices are 32-bit elements; how exact they have to be, the bound alone decides.
A program may use at most 64 MiB of HBM per device.

```python
import math
import jax
import jax.numpy as jnp
from jax import lax

M = 64
LINES = 256
STEPS = 2
GRID_CELLS_X = 512
NSEC = 8


def draw_upwind(key, part):
    key = jax.random.fold_in(key, 11)
    rate_key, chosen_key = jax.random.split(key)
    lower_end = 32.0
    upper_end = 8.0 * GRID_CELLS_X
    uniform_part = jax.random.uniform(rate_key, (M,), jnp.float32)
    coeffs = lower_end * jnp.exp(uniform_part * jnp.log(upper_end / lower_end))
    chosen = jax.random.permutation(chosen_key, M)
    coeffs = coeffs.at[chosen[0]].set(upper_end)
    coeffs = coeffs.at[chosen[1]].set(32.0)
    return coeffs


def draw_absorption(key, part):
    key = jax.random.fold_in(key, 23)
    background_key, spike_key, plateau_key = jax.random.split(key, 3)
    background_level = 0.5 * jax.random.uniform(background_key, (2, GRID_CELLS_X, LINES), jnp.float32)
    spike_cells = jax.random.randint(spike_key, (2, 3), 0, GRID_CELLS_X)
    cell_location = jnp.arange(GRID_CELLS_X)
    is_spike_cell = jnp.any(cell_location[None, None, :] == spike_cells[:, :, None], axis=1)
    spike_magnitude = 4.0 * GRID_CELLS_X * jax.random.uniform(plateau_key, (2, GRID_CELLS_X, LINES), jnp.float32, 0.25, 1.0)
    spike_magnitude = spike_magnitude.at[:, :, 0].set(4.0 * GRID_CELLS_X)
    return jnp.where(is_spike_cell[:, :, None], spike_magnitude, background_level)


def draw_propagator(key, part):
    key = jax.random.fold_in(key, 37)
    offset_key, rough_key = jax.random.split(key)
    full_shape = (NSEC, M, GRID_CELLS_X, LINES)
    offset_part = jax.random.normal(offset_key, (NSEC, M, 1, LINES), jnp.float32)
    rough_part = 0.7 * jax.random.normal(rough_key, full_shape, jnp.float32)
    values = offset_part + rough_part
    return jnp.clip(values, -4.0, 4.0)


def set_ends(values, key, low, top_value):
    longest = values.shape.index(max(values.shape))
    spots = []
    for shift in (0, 1):
        where = [jax.random.randint(jax.random.fold_in(key, axis), (), 0, length) for axis, length in enumerate(values.shape)]
        where[longest] = (where[longest] + shift) % values.shape[longest]
        spots.append(tuple(where))
    return values.at[spots[0]].set(low).at[spots[1]].set(top_value)


def shard_levels(stream_key, shape, shards, low, high):
    gain, own = 1.0, jax.random.fold_in(stream_key, 6)
    for axis_at, parts in shards:
        heights = jnp.exp(jax.random.uniform(jax.random.fold_in(own, axis_at), (parts,), jnp.float32, low / len(shards), high / len(shards)))
        gain = gain * jnp.repeat(heights, shape[axis_at] // parts).reshape([-1 if axis == axis_at else 1 for axis in range(len(shape))])
    return gain


def scatter_about(key, dims, width, bound, cuts=(), held_as=jnp.bfloat16):
    drawn = width * jax.random.normal(key, dims, jnp.float32)
    if cuts:
        drawn = drawn * shard_levels(key, dims, cuts, -0.22, 0.18)
    return jnp.clip(drawn, -bound, bound).astype(held_as)


def setup_inputs(seed: int = 0) -> dict:
    key_of = jax.random.split(jax.random.key(seed), 9)
    propagator = draw_propagator(jax.random.fold_in(key_of[8], 71), 0)
    complement = scatter_about(key_of[1], (NSEC, STEPS, M, GRID_CELLS_X, LINES), 0.125, 0.75, ((0, 8), (3, 32)))
    labels = set_ends(jax.random.randint(key_of[2], (NSEC, STEPS), 0, 2), jax.random.fold_in(key_of[2], 1), 0, 1).astype(jnp.int32)
    absorption = draw_absorption(jax.random.fold_in(key_of[8], 71), 0)
    to_ordinates = scatter_about(key_of[4], (M, M), M ** -0.5, 0.75, (), jnp.float32)
    to_modes = scatter_about(key_of[5], (M, M), M ** -0.5, 0.75, (), jnp.float32)
    upwind = draw_upwind(jax.random.fold_in(key_of[8], 71), 0)
    mode_decay = jnp.clip(jnp.exp(jax.random.uniform(key_of[7], (2, M), jnp.float32, math.log(0.3), math.log(1.0))), 0.3, 1.0)
    return dict(propagator=propagator, complement=complement, labels=labels, absorption=absorption, to_ordinates=to_ordinates, to_modes=to_modes, upwind=upwind, mode_decay=mode_decay)


def sweep_line(ordinal, coeffs, absorb_now, reverse):
    cells_first = jnp.moveaxis(ordinal, 1, 0)
    rate_column = coeffs[:, None]

    def advance(state, item):
        source, absorb_row = item
        free_part, unit_part = state
        denominator = 1.0 + rate_column + absorb_row[None, :]
        free_part = (source + rate_column * free_part) / denominator
        unit_part = rate_column * unit_part / denominator
        return (free_part, unit_part), (free_part, unit_part)

    initial = (jnp.zeros(cells_first.shape[1:], jnp.float32), jnp.ones(cells_first.shape[1:], jnp.float32))
    _, (free_all, unit_all) = lax.scan(advance, initial, (cells_first, absorb_now), reverse=reverse)
    final_index = 0 if reverse else -1
    closure = free_all[final_index] / (1.0 - unit_all[final_index])
    solved_ord = free_all + unit_all * closure[None]
    return jnp.moveaxis(solved_ord, 0, 1)


def reference(propagator, complement, labels, absorption, to_ordinates, to_modes, upwind, mode_decay):
    half_modes = upwind.shape[0] // 2

    def one_section(density, inputs):
        section, comp_section, label_row = inputs
        for contour_step in range(STEPS):
            first_species = label_row[contour_step] == 0
            absorb_now = jnp.where(first_species, absorption[0], absorption[1])
            mode_gain = jnp.where(first_species, mode_decay[0], mode_decay[1])
            ordinal = jnp.einsum("nm,mxl->nxl", to_ordinates, section, precision=lax.Precision.HIGHEST)
            forward = sweep_line(ordinal[:half_modes], upwind[:half_modes], absorb_now, False)
            backward = sweep_line(ordinal[half_modes:], upwind[half_modes:], absorb_now, True)
            solved_all = jnp.concatenate([forward, backward], axis=0)
            section = mode_gain[:, None, None] * jnp.einsum("mn,nxl->mxl", to_modes, solved_all, precision=lax.Precision.HIGHEST)
            density_term = jnp.sum(section * comp_section[contour_step].astype(jnp.float32), axis=0)
            density = density + jnp.stack([jnp.where(first_species, density_term, 0.0), jnp.where(first_species, 0.0, density_term)])
        return density, section

    initial = jnp.zeros(absorption.shape, jnp.float32)
    density, propagated = lax.scan(one_section, initial, (propagator, complement, labels))
    return propagated, density
```

```python
import functools

import jax
import jax.numpy as jnp
from jax import lax
from jax.experimental import pallas as pl
from jax.experimental.pallas import tpu as pltpu
from jax.sharding import PartitionSpec as P

F32, BF16 = jnp.float32, jnp.bfloat16
M = 64
HALF = M // 2
X = 16
LANES = 128
HALVES = 2
STEPS = 2
TILES = M // 8


def loop(count, step, carry=None):
    if carry is None:

        def plain(i, none):
            step(i)
            return none

        lax.fori_loop(0, count, plain, 0, unroll=True)
        return None
    return lax.fori_loop(0, count, step, carry, unroll=True)


def column(row):
    wide = jnp.broadcast_to(row, (M, M))
    here = lax.broadcasted_iota(jnp.int32, (M, M), 0) == lax.broadcasted_iota(jnp.int32, (M, M), 1)
    return jnp.sum(jnp.where(here, wide, 0.0), axis=1, keepdims=True)


def split(value):
    high = value.astype(BF16)
    low = (value - high.astype(F32)).astype(BF16)
    return high, low


def left_operand(weights):
    high, low = split(weights)
    return jnp.concatenate([high, high, low], axis=1)


def product(left, value):
    high, low = split(value)
    right = jnp.concatenate([high, low, high], axis=0)
    return jnp.dot(left, right, preferred_element_type=F32)


def kernel(
    cycle,
    sections,
    prop_ref,
    comp_ref,
    labels_ref,
    absorb_ref,
    ordin_ref,
    modes_ref,
    upwind_ref,
    decay_ref,
    out_ref,
    dens_ref,
    q_in,
    q_mid,
    q_out,
    comp,
    labels,
    absorb,
    ordin,
    modes,
    upwind,
    decay,
    rate,
    absorb_now,
    left_in,
    left_mid,
    left_mid_modes,
    left_out,
    inverse,
    ratio,
    unit,
    free,
    send_map,
    recv_map,
    send_unit,
    recv_unit,
    send_free,
    recv_free,
    prefix_unit,
    prefix_free,
    send_flow,
    recv_flow,
    send_early,
    recv_early,
    send_late,
    recv_late,
    dens,
    load_sem,
    q_sem,
    comp_sem,
    map_send,
    map_recv,
    unit_send,
    unit_recv,
    free_send,
    free_recv,
    flow_send,
    flow_recv,
    early_send,
    early_recv,
    late_send,
    late_recv,
    out_sem,
    dens_sem,
):
    me = lax.axis_index("gx")
    col = lax.axis_index("col")
    core = lax.rem(col, 2)
    my_tile = me // 4
    my_half = lax.rem(me, 4) // 2
    is_owner = lax.rem(me, 2) == lax.rem(my_tile + core, 2)

    small = [
        pltpu.make_async_copy(src, dst, load_sem.at[i])
        for i, (src, dst) in enumerate(
            (
                (absorb_ref, absorb),
                (upwind_ref, upwind),
                (labels_ref, labels),
                (ordin_ref, ordin),
                (modes_ref, modes),
                (decay_ref, decay),
            )
        )
    ]
    for copy in small:
        copy.start()
    q_load = [
        pltpu.make_async_copy(prop_ref.at[:, pl.ds(LANES * h, LANES)], q_in.at[h], q_sem.at[h])
        for h in range(HALVES)
    ]
    for copy in q_load:
        copy.start()
    comp_load = pltpu.make_async_copy(comp_ref, comp, comp_sem)
    comp_load.start()

    barrier = pltpu.get_barrier_semaphore()

    def greet_cycle(k, none):
        pl.semaphore_signal(barrier, inc=1, device_id={"gx": lax.rem(me + k, cycle)}, device_id_type=pl.DeviceIdType.MESH)
        return none

    def greet_sections(k, none):
        pl.semaphore_signal(barrier, inc=1, device_id={"col": lax.rem(col + k, sections)}, device_id_type=pl.DeviceIdType.MESH)
        return none

    lax.fori_loop(1, cycle, greet_cycle, 0)
    lax.fori_loop(1, sections, greet_sections, 0)

    for copy in small:
        copy.wait()

    rate[...] = jnp.broadcast_to(column(upwind[...]), (M, LANES))
    first = [labels[0, s] == 0 for s in range(STEPS)]
    for s in range(STEPS):
        absorb_now[s] = jnp.where(first[s], absorb[0], absorb[1])
    left_in[...] = left_operand(ordin[...])

    def coefficients(s, h):
        def one(i, carry):
            up, down = carry
            lanes = pl.ds(LANES * h, LANES)
            j = X - 1 - i
            rate_up, rate_down = rate[:HALF], rate[HALF:]
            inverse_up = 1.0 / (1.0 + rate_up + absorb_now[s, pl.ds(i, 1), lanes])
            inverse_down = 1.0 / (1.0 + rate_down + absorb_now[s, pl.ds(j, 1), lanes])
            ratio_up = rate_up * inverse_up
            ratio_down = rate_down * inverse_down
            up = up * ratio_up
            down = down * ratio_down
            inverse[s, h, i, :HALF] = inverse_up
            inverse[s, h, j, HALF:] = inverse_down
            ratio[s, h, i, :HALF] = ratio_up
            ratio[s, h, j, HALF:] = ratio_down
            unit[s, h, i, :HALF] = up
            unit[s, h, j, HALF:] = down
            return up, down

        ones = jnp.ones((HALF, LANES), F32)
        return loop(X, one, (ones, ones))

    def sweep(s, h):
        def one(i, carry):
            up, down = carry
            j = X - 1 - i
            up = free[s, h, i, :HALF] + ratio[s, h, i, :HALF] * up
            down = free[s, h, j, HALF:] + ratio[s, h, j, HALF:] * down
            free[s, h, i, :HALF] = up
            free[s, h, j, HALF:] = down
            return up, down

        zeros = jnp.zeros((HALF, LANES), F32)
        return loop(X, one, (zeros, zeros))

    def owner_of(t, h):
        return 4 * t + 2 * h + lax.rem(t + core, 2)

    def to_owners(source, target, send_sem, recv_sem, h):
        def one(t):
            owner = owner_of(t, h)

            @pl.when(owner != me)
            def _():
                pltpu.make_async_remote_copy(
                    src_ref=source.at[h, t],
                    dst_ref=target.at[me],
                    send_sem=send_sem,
                    recv_sem=recv_sem,
                    device_id={"gx": owner},
                    device_id_type=pl.DeviceIdType.MESH,
                ).start()

        loop(TILES, one)

        @pl.when(jnp.logical_and(is_owner, my_half == h))
        def _():
            target[me] = source[h, my_tile]

    def tile_rows(pair, t):
        up, down = pair
        rows = up if t < TILES // 2 else down
        base = 8 * (t % (TILES // 2))
        return rows[base : base + 8]

    for h in range(HALVES):
        units = coefficients(0, h)
        for t in range(TILES):
            send_map[h, t, 0] = tile_rows(units, t)
    for h in range(HALVES):
        q_load[h].wait()

        def sources(i):
            value = jnp.concatenate(
                [q_in[h, pl.ds(2 * i, M, stride=X), :], q_in[h, pl.ds(2 * i + 1, M, stride=X), :]], axis=1
            )
            result = product(left_in[...], value)
            free[0, h, 2 * i] = result[:, :LANES] * inverse[0, h, 2 * i]
            free[0, h, 2 * i + 1] = result[:, LANES:] * inverse[0, h, 2 * i + 1]

        loop(X // 2, sources)
        frees = sweep(0, h)
        for t in range(TILES):
            send_map[h, t, 1] = tile_rows(frees, t)
        if h == 0:
            pl.semaphore_wait(barrier, cycle + sections - 2)
        to_owners(send_map, recv_map, map_send, map_recv, h)

    for h in range(HALVES):
        units = coefficients(1, h)
        for t in range(TILES):
            send_unit[h, t] = tile_rows(units, t)
        to_owners(send_unit, recv_unit, unit_send, unit_recv, h)
    gained = []
    for s in range(STEPS):
        gain = jnp.where(first[s], decay[0:1], decay[1:2])
        gained.append(column(gain) * modes[...])
    left_mid[...] = left_operand(
        jnp.dot(ordin[...], gained[0], preferred_element_type=F32, precision=lax.Precision.HIGHEST)
    )
    left_mid_modes[...] = left_operand(gained[0])
    left_out[...] = left_operand(gained[1])

    def place(k):
        return jnp.where(my_tile < TILES // 2, k, cycle - 1 - k)

    def wait_for(ref, sem):
        pltpu.make_async_copy(ref, ref, sem).wait()

    def send_inflows(s, entry):
        def one(k):
            p = place(k)
            flow = prefix_unit[s, k] * entry + prefix_free[k]
            send_flow[s, p] = flow

            @pl.when(p != me)
            def _():
                pltpu.make_async_remote_copy(
                    src_ref=send_flow.at[s, p],
                    dst_ref=recv_flow.at[s, my_half, my_tile],
                    send_sem=flow_send.at[s],
                    recv_sem=flow_recv.at[s, my_half],
                    device_id={"gx": p},
                    device_id_type=pl.DeviceIdType.MESH,
                ).start()

        loop(cycle, one)
        recv_flow[s, my_half, my_tile] = send_flow[s, me]

    @pl.when(is_owner)
    def _():
        wait_for(recv_map.at[pl.ds(0, cycle - 1)], map_recv)

        def one(k, carry):
            whole_unit, whole_free = carry
            p = place(k)
            prefix_unit[0, k] = whole_unit
            prefix_free[k] = whole_free
            step_unit = recv_map[p, 0]
            return whole_unit * step_unit, step_unit * whole_free + recv_map[p, 1]

        ones, zeros = jnp.ones((8, LANES), F32), jnp.zeros((8, LANES), F32)
        whole_unit, whole_free = loop(cycle, one, (ones, zeros))
        send_inflows(0, whole_free / (1.0 - whole_unit))

    def wait_inflows(s, h):
        owns = jnp.logical_and(is_owner, my_half == h)

        @pl.when(owns)
        def _():
            wait_for(recv_flow.at[s, h, pl.ds(0, TILES - 1)], flow_recv.at[s, h])

        @pl.when(jnp.logical_not(owns))
        def _():
            wait_for(recv_flow.at[s, h], flow_recv.at[s, h])

    def swept(s, h, i, inflow):
        return free[s, h, i] + unit[s, h, i] * inflow

    for h in range(HALVES):
        wait_inflows(0, h)
        inflow = recv_flow[0, h].reshape(M, LANES)

        def sources(i):
            a, b = swept(0, h, 2 * i, inflow), swept(0, h, 2 * i + 1, inflow)
            free[0, h, 2 * i] = a
            free[0, h, 2 * i + 1] = b
            result = product(left_mid[...], jnp.concatenate([a, b], axis=1))
            free[1, h, 2 * i] = result[:, :LANES] * inverse[1, h, 2 * i]
            free[1, h, 2 * i + 1] = result[:, LANES:] * inverse[1, h, 2 * i + 1]

        loop(X // 2, sources)
        frees = sweep(1, h)
        for t in range(TILES):
            send_free[h, t] = tile_rows(frees, t)
        to_owners(send_free, recv_free, free_send, free_recv, h)

    def density(s, h, q):
        def one(i, total):
            rows = pl.ds(8 * X * i, 8 * X)
            term = q[h, rows, :] * comp[s, rows, pl.ds(LANES * h, LANES)].astype(F32)
            return total + jnp.sum(term.reshape(8, X, LANES), axis=0)

        return loop(M // 8, one, jnp.zeros((X, LANES), F32))

    def to_sections(source, target, send_sem, recv_sem):
        def one(k):
            pltpu.make_async_remote_copy(
                src_ref=source,
                dst_ref=target,
                send_sem=send_sem,
                recv_sem=recv_sem,
                device_id={"col": lax.rem(col + 1 + k, sections)},
                device_id_type=pl.DeviceIdType.MESH,
            ).start()

        loop(sections - 1, one)

    comp_load.wait()
    for h in range(HALVES):

        def middle(i):
            value = jnp.concatenate([free[0, h, 2 * i], free[0, h, 2 * i + 1]], axis=1)
            result = product(left_mid_modes[...], value)
            q_mid[h, pl.ds(2 * i, M, stride=X), :] = result[:, :LANES]
            q_mid[h, pl.ds(2 * i + 1, M, stride=X), :] = result[:, LANES:]

        loop(X // 2, middle)
        send_early[pl.ds(X * h, X)] = density(0, h, q_mid)
    for s in range(STEPS):
        send_early[pl.ds(2 * X + 8 * s, 8)] = jnp.broadcast_to(labels[0, s].astype(F32), (8, LANES))
    to_sections(send_early, recv_early.at[col], early_send, early_recv)
    recv_early[col] = send_early[...]

    @pl.when(is_owner)
    def _():
        wait_for(recv_unit.at[pl.ds(0, cycle - 1)], unit_recv)

        def units(k, whole_unit):
            prefix_unit[1, k] = whole_unit
            return whole_unit * recv_unit[place(k)]

        whole_unit = loop(cycle, units, jnp.ones((8, LANES), F32))
        wait_for(recv_free.at[pl.ds(0, cycle - 1)], free_recv)

        def one(k, whole_free):
            p = place(k)
            prefix_free[k] = whole_free
            return recv_unit[p] * whole_free + recv_free[p]

        whole_free = loop(cycle, one, jnp.zeros((8, LANES), F32))
        send_inflows(1, whole_free / (1.0 - whole_unit))

    q_store = [
        pltpu.make_async_copy(q_out.at[h], out_ref.at[:, pl.ds(LANES * h, LANES)], out_sem.at[h])
        for h in range(HALVES)
    ]
    for h in range(HALVES):
        wait_inflows(1, h)
        inflow = recv_flow[1, h].reshape(M, LANES)

        def last(i):
            value = jnp.concatenate([swept(1, h, 2 * i, inflow), swept(1, h, 2 * i + 1, inflow)], axis=1)
            result = product(left_out[...], value)
            q_out[h, pl.ds(2 * i, M, stride=X), :] = result[:, :LANES]
            q_out[h, pl.ds(2 * i + 1, M, stride=X), :] = result[:, LANES:]

        loop(X // 2, last)
        q_store[h].start()
        send_late[h] = density(1, h, q_out)
        to_sections(send_late.at[h], recv_late.at[h, col], late_send.at[h], late_recv.at[h])
        recv_late[h, col] = send_late[h]

    wait_for(recv_early.at[pl.ds(0, sections - 1)], early_recv)
    for h in range(HALVES):
        wait_for(recv_late.at[h, pl.ds(0, sections - 1)], late_recv.at[h])

        def one(c, carry):
            total_a, total_b = carry
            terms = (recv_early[c, pl.ds(X * h, X)], recv_late[h, c])
            for s in range(STEPS):
                label = recv_early[c, pl.ds(2 * X + 8 * s, 8)]
                is_a = jnp.concatenate([label, label], axis=0) == 0.0
                total_a = total_a + jnp.where(is_a, terms[s], 0.0)
                total_b = total_b + jnp.where(is_a, 0.0, terms[s])
            return total_a, total_b

        zeros = jnp.zeros((X, LANES), F32)
        total_a, total_b = loop(sections, one, (zeros, zeros))
        dens[0, :, pl.ds(LANES * h, LANES)] = total_a
        dens[1, :, pl.ds(LANES * h, LANES)] = total_b
    dens_store = pltpu.make_async_copy(dens, dens_ref, dens_sem)
    dens_store.start()

    for h in range(HALVES):
        owns = jnp.logical_and(is_owner, my_half == h)

        for count, when in ((TILES - 1, owns), (TILES, jnp.logical_not(owns))):

            @pl.when(when)
            def _():
                wait_for(send_map.at[h, pl.ds(0, count)], map_send)
                wait_for(send_unit.at[h, pl.ds(0, count)], unit_send)
                wait_for(send_free.at[h, pl.ds(0, count)], free_send)

    @pl.when(is_owner)
    def _():
        for s in range(STEPS):
            wait_for(send_flow.at[s, pl.ds(0, cycle - 1)], flow_send.at[s])

    wait_for(recv_early.at[pl.ds(0, sections - 1)], early_send)
    for h in range(HALVES):
        wait_for(recv_late.at[h, pl.ds(0, sections - 1)], late_send.at[h])
    for copy in q_store:
        copy.wait()
    dens_store.wait()


def body(propagator, complement, labels, absorption, to_ordinates, to_modes, upwind, mode_decay):
    cycle = lax.axis_size("gx")
    sections = lax.axis_size("col")
    rows, lines = M * X, HALVES * LANES
    dma = pltpu.SemaphoreType.DMA
    anywhere = pl.BlockSpec(memory_space=pl.ANY)
    left = pltpu.VMEM((M, 3 * M), BF16)
    cells = pltpu.VMEM((STEPS, HALVES, X, M, LANES), F32)
    scratch = [
        pltpu.VMEM((HALVES, rows, LANES), F32),
        pltpu.VMEM((HALVES, rows, LANES), F32),
        pltpu.VMEM((HALVES, rows, LANES), F32),
        pltpu.VMEM((STEPS, rows, lines), BF16),
        pltpu.SMEM((1, STEPS), jnp.int32),
        pltpu.VMEM((2, X, lines), F32),
        pltpu.VMEM((M, M), F32),
        pltpu.VMEM((M, M), F32),
        pltpu.VMEM((1, M), F32),
        pltpu.VMEM((2, M), F32),
        pltpu.VMEM((M, LANES), F32),
        pltpu.VMEM((STEPS, X, lines), F32),
        left,
        left,
        left,
        left,
        cells,
        cells,
        cells,
        cells,
        pltpu.VMEM((HALVES, TILES, 2, 8, LANES), F32),
        pltpu.VMEM((cycle, 2, 8, LANES), F32),
        pltpu.VMEM((HALVES, TILES, 8, LANES), F32),
        pltpu.VMEM((cycle, 8, LANES), F32),
        pltpu.VMEM((HALVES, TILES, 8, LANES), F32),
        pltpu.VMEM((cycle, 8, LANES), F32),
        pltpu.VMEM((STEPS, cycle, 8, LANES), F32),
        pltpu.VMEM((cycle, 8, LANES), F32),
        pltpu.VMEM((STEPS, cycle, 8, LANES), F32),
        pltpu.VMEM((STEPS, HALVES, TILES, 8, LANES), F32),
        pltpu.VMEM((3 * X, LANES), F32),
        pltpu.VMEM((sections, 3 * X, LANES), F32),
        pltpu.VMEM((HALVES, X, LANES), F32),
        pltpu.VMEM((HALVES, sections, X, LANES), F32),
        pltpu.VMEM((2, X, lines), F32),
        dma((6,)),
        dma((HALVES,)),
        dma,
        dma,
        dma,
        dma,
        dma,
        dma,
        dma,
        dma((STEPS,)),
        dma((STEPS, HALVES)),
        dma,
        dma,
        dma((HALVES,)),
        dma((HALVES,)),
        dma((HALVES,)),
        dma,
    ]
    propagated, density = pl.pallas_call(
        functools.partial(kernel, cycle, sections),
        out_shape=(
            jax.ShapeDtypeStruct((rows, lines), F32),
            jax.ShapeDtypeStruct((2, X, lines), F32),
        ),
        in_specs=[anywhere] * 8,
        out_specs=(anywhere, anywhere),
        scratch_shapes=scratch,
        compiler_params=pltpu.CompilerParams(
            collective_id=0, has_side_effects=True, vmem_limit_bytes=48 * 1024 * 1024
        ),
        name="contour_steps",
    )(
        propagator.reshape(rows, lines),
        complement.reshape(STEPS, rows, lines),
        labels,
        absorption,
        to_ordinates,
        to_modes,
        upwind.reshape(1, M),
        mode_decay,
    )
    return propagated.reshape(1, M, X, lines), density


def solution(mesh):
    in_specs = (
        P("col", None, "gx", None),
        P("col", None, None, "gx", None),
        P("col", None),
        P(None, "gx", None),
        P(),
        P(),
        P(),
        P(),
    )
    out_specs = (P("col", None, "gx", None), P(None, "gx", None))
    return jax.shard_map(body, mesh=mesh, in_specs=in_specs, out_specs=out_specs, check_vma=False)
```

```python
import functools

import jax
import jax.numpy as jnp
from jax import lax
from jax.experimental import pallas as pl
from jax.experimental.pallas import tpu as pltpu
from jax.sharding import PartitionSpec as P

F32, BF16 = jnp.float32, jnp.bfloat16
M = 64
HALF = M // 2
X = 16
LANES = 128
HALVES = 2
STEPS = 2
TILES = M // 8
RING_Z, RING_Y, RING_X = 8, 4, 4
FAR_Z, FAR_Y, FAR_X = (4, 3, 5, 2, 6, 1, 7, 0), (2, 1, 3, 0), (2, 1, 3, 0)


def loop(count, step, carry=None):
    if carry is None:

        def plain(i, none):
            step(i)
            return none

        lax.fori_loop(0, count, plain, 0, unroll=True)
        return None
    return lax.fori_loop(0, count, step, carry, unroll=True)


def column(row):
    wide = jnp.broadcast_to(row, (M, M))
    here = lax.broadcasted_iota(jnp.int32, (M, M), 0) == lax.broadcasted_iota(jnp.int32, (M, M), 1)
    return jnp.sum(jnp.where(here, wide, 0.0), axis=1, keepdims=True)


def split(value):
    high = value.astype(BF16)
    low = (value - high.astype(F32)).astype(BF16)
    return high, low


def left_operand(weights):
    high, low = split(weights)
    return jnp.concatenate([high, high, low], axis=1)


def product(left, value):
    high, low = split(value)
    right = jnp.concatenate([high, low, high], axis=0)
    return jnp.dot(left, right, preferred_element_type=F32)


def kernel(
    cycle,
    sections,
    prop_ref,
    comp_ref,
    labels_ref,
    absorb_ref,
    ordin_ref,
    modes_ref,
    upwind_ref,
    decay_ref,
    out_ref,
    dens_ref,
    q_in,
    q_mid,
    q_out,
    comp,
    labels,
    absorb,
    ordin,
    modes,
    upwind,
    decay,
    rate,
    absorb_now,
    left_in,
    left_mid,
    left_mid_modes,
    left_out,
    inverse,
    ratio,
    unit,
    free,
    send_map,
    recv_map,
    send_unit,
    recv_unit,
    send_free,
    recv_free,
    prefix_unit,
    prefix_free,
    send_flow,
    recv_flow,
    send_early,
    recv_early,
    send_late,
    recv_late,
    dens,
    load_sem,
    q_sem,
    comp_sem,
    map_send,
    map_recv,
    unit_send,
    unit_recv,
    free_send,
    free_recv,
    flow_send,
    flow_recv,
    early_send,
    early_recv,
    late_send,
    late_recv,
    out_sem,
    dens_sem,
):
    me = lax.axis_index("gx")
    col = lax.axis_index("col")
    core = lax.rem(col, 2)
    my_z, my_y, my_x = me // RING_Y, lax.rem(me, RING_Y), col // 2
    is_owner = core == 1
    parity = lax.rem(my_z + my_y, 2)
    owns_here = jnp.logical_and(is_owner, parity == 1)
    owns_other = jnp.logical_and(is_owner, parity == 0)
    my_tile, my_half = my_z, my_y // 2
    owner_col = col - core + 1
    served_col = col - 1 + parity

    small = [
        pltpu.make_async_copy(src, dst, load_sem.at[i])
        for i, (src, dst) in enumerate(
            (
                (absorb_ref, absorb),
                (upwind_ref, upwind),
                (labels_ref, labels),
                (ordin_ref, ordin),
                (modes_ref, modes),
                (decay_ref, decay),
            )
        )
    ]
    for copy in small:
        copy.start()
    q_load = [
        pltpu.make_async_copy(prop_ref.at[:, pl.ds(LANES * h, LANES)], q_in.at[h], q_sem.at[h])
        for h in range(HALVES)
    ]
    for copy in q_load:
        copy.start()
    comp_load = pltpu.make_async_copy(comp_ref, comp, comp_sem)
    comp_load.start()

    barrier = pltpu.get_barrier_semaphore()

    def far_places():
        for dz in FAR_Z:
            for dy in FAR_Y:
                yield RING_Y * lax.rem(my_z + dz, RING_Z) + lax.rem(my_y + dy, RING_Y), (dz, dy) == (0, 0)

    def far_sections():
        for dx in FAR_X:
            for dc in range(2):
                if (dx, dc) != (0, 0):
                    yield 2 * lax.rem(my_x + dx, RING_X) + lax.rem(core + dc, 2)

    def far_owners(halves=range(HALVES)):
        for dz in FAR_Z:
            for h in halves:
                t = lax.rem(my_z + dz, RING_Z)
                yield t, h, RING_Y * t + 2 * h + lax.rem(t + core, 2), dz == 0

    def greet(place, section):
        pl.semaphore_signal(
            barrier, inc=1, device_id={"gx": place, "col": section}, device_id_type=pl.DeviceIdType.MESH
        )

    @pl.when(owns_here)
    def _():
        for place, here in far_places():
            if not here:
                greet(place, col)

    @pl.when(owns_other)
    def _():
        for place, here in far_places():
            greet(place, served_col)

    @pl.when(jnp.logical_not(owns_here))
    def _():
        for t, h, owner, near in far_owners():
            greet(owner, owner_col)

    for section in far_sections():
        greet(me, section)
    greeted = jnp.where(owns_here, cycle - 1, jnp.where(owns_other, cycle + 2 * TILES, 2 * TILES)) + sections - 1

    for copy in small:
        copy.wait()

    rate[...] = jnp.broadcast_to(column(upwind[...]), (M, LANES))
    first = [labels[0, s] == 0 for s in range(STEPS)]
    for s in range(STEPS):
        absorb_now[s] = jnp.where(first[s], absorb[0], absorb[1])
    left_in[...] = left_operand(ordin[...])

    def coefficients(s, h):
        def one(i, carry):
            up, down = carry
            lanes = pl.ds(LANES * h, LANES)
            j = X - 1 - i
            rate_up, rate_down = rate[:HALF], rate[HALF:]
            inverse_up = 1.0 / (1.0 + rate_up + absorb_now[s, pl.ds(i, 1), lanes])
            inverse_down = 1.0 / (1.0 + rate_down + absorb_now[s, pl.ds(j, 1), lanes])
            ratio_up = rate_up * inverse_up
            ratio_down = rate_down * inverse_down
            up = up * ratio_up
            down = down * ratio_down
            inverse[s, h, i, :HALF] = inverse_up
            inverse[s, h, j, HALF:] = inverse_down
            ratio[s, h, i, :HALF] = ratio_up
            ratio[s, h, j, HALF:] = ratio_down
            unit[s, h, i, :HALF] = up
            unit[s, h, j, HALF:] = down
            return up, down

        ones = jnp.ones((HALF, LANES), F32)
        return loop(X, one, (ones, ones))

    def sweep(s, h):
        def one(i, carry):
            up, down = carry
            j = X - 1 - i
            up = free[s, h, i, :HALF] + ratio[s, h, i, :HALF] * up
            down = free[s, h, j, HALF:] + ratio[s, h, j, HALF:] * down
            free[s, h, i, :HALF] = up
            free[s, h, j, HALF:] = down
            return up, down

        zeros = jnp.zeros((HALF, LANES), F32)
        return loop(X, one, (zeros, zeros))

    def to_owners(source, target, send_sem, recv_sem, halves):
        for t, h, owner, near in far_owners(halves):

            def send(t=t, h=h, owner=owner):
                pltpu.make_async_remote_copy(
                    src_ref=source.at[h, t],
                    dst_ref=target.at[me],
                    send_sem=send_sem,
                    recv_sem=recv_sem,
                    device_id={"gx": owner, "col": owner_col},
                    device_id_type=pl.DeviceIdType.MESH,
                ).start()

            if near:
                pl.when(jnp.logical_not(jnp.logical_and(owns_here, h == my_half)))(send)
            else:
                send()

        for h in halves:

            @pl.when(jnp.logical_and(owns_here, my_half == h))
            def _():
                target[me] = source[h, my_tile]

    def tile_rows(pair, t):
        up, down = pair
        rows = up if t < TILES // 2 else down
        base = 8 * (t % (TILES // 2))
        return rows[base : base + 8]

    for h in range(HALVES):
        units = coefficients(0, h)
        for t in range(TILES):
            send_map[h, t, 0] = tile_rows(units, t)
    for h in range(HALVES):
        units = coefficients(1, h)
        for t in range(TILES):
            send_unit[h, t] = tile_rows(units, t)
    gained = []
    for s in range(STEPS):
        gain = jnp.where(first[s], decay[0:1], decay[1:2])
        gained.append(column(gain) * modes[...])
    left_mid[...] = left_operand(
        jnp.dot(ordin[...], gained[0], preferred_element_type=F32, precision=lax.Precision.HIGHEST)
    )
    left_mid_modes[...] = left_operand(gained[0])
    left_out[...] = left_operand(gained[1])

    for h in range(HALVES):
        q_load[h].wait()

        def sources(i):
            value = jnp.concatenate(
                [q_in[h, pl.ds(2 * i, M, stride=X), :], q_in[h, pl.ds(2 * i + 1, M, stride=X), :]], axis=1
            )
            result = product(left_in[...], value)
            free[0, h, 2 * i] = result[:, :LANES] * inverse[0, h, 2 * i]
            free[0, h, 2 * i + 1] = result[:, LANES:] * inverse[0, h, 2 * i + 1]

        loop(X // 2, sources)
        frees = sweep(0, h)
        for t in range(TILES):
            send_map[h, t, 1] = tile_rows(frees, t)
    pl.semaphore_wait(barrier, greeted)
    to_owners(send_map, recv_map, map_send, map_recv, range(HALVES))
    to_owners(send_unit, recv_unit, unit_send, unit_recv, range(HALVES))

    def along(k):
        return jnp.where(my_tile < TILES // 2, k, cycle - 1 - k)

    def wait_for(ref, sem):
        pltpu.make_async_copy(ref, ref, sem).wait()

    def wait_for_tiles(ref, sem):
        @pl.when(owns_here)
        def _():
            wait_for(ref.at[pl.ds(0, cycle - 1)], sem)

        @pl.when(owns_other)
        def _():
            wait_for(ref, sem)

    def send_inflows(s, entry):
        for p, here in far_places():
            k = along(p)
            send_flow[s, p] = prefix_unit[s, k] * entry + prefix_free[k]

            def send(p=p):
                pltpu.make_async_remote_copy(
                    src_ref=send_flow.at[s, p],
                    dst_ref=recv_flow.at[s, my_half, my_tile],
                    send_sem=flow_send.at[s],
                    recv_sem=flow_recv.at[s, my_half],
                    device_id={"gx": p, "col": served_col},
                    device_id_type=pl.DeviceIdType.MESH,
                ).start()

            if here:
                pl.when(owns_other)(send)
            else:
                send()

        @pl.when(owns_here)
        def _():
            recv_flow[s, my_half, my_tile] = send_flow[s, me]

    @pl.when(is_owner)
    def _():
        wait_for_tiles(recv_map, map_recv)

        def one(k, carry):
            whole_unit, whole_free = carry
            p = along(k)
            prefix_unit[0, k] = whole_unit
            prefix_free[k] = whole_free
            step_unit = recv_map[p, 0]
            return whole_unit * step_unit, step_unit * whole_free + recv_map[p, 1]

        ones, zeros = jnp.ones((8, LANES), F32), jnp.zeros((8, LANES), F32)
        whole_unit, whole_free = loop(cycle, one, (ones, zeros))
        send_inflows(0, whole_free / (1.0 - whole_unit))

    def wait_inflows(s, h):
        owns = jnp.logical_and(owns_here, my_half == h)

        @pl.when(owns)
        def _():
            wait_for(recv_flow.at[s, h, pl.ds(0, TILES - 1)], flow_recv.at[s, h])

        @pl.when(jnp.logical_not(owns))
        def _():
            wait_for(recv_flow.at[s, h], flow_recv.at[s, h])

    def swept(s, h, i, inflow):
        return free[s, h, i] + unit[s, h, i] * inflow

    for h in range(HALVES):
        wait_inflows(0, h)
        inflow = recv_flow[0, h].reshape(M, LANES)

        def sources(i):
            a, b = swept(0, h, 2 * i, inflow), swept(0, h, 2 * i + 1, inflow)
            free[0, h, 2 * i] = a
            free[0, h, 2 * i + 1] = b
            result = product(left_mid[...], jnp.concatenate([a, b], axis=1))
            free[1, h, 2 * i] = result[:, :LANES] * inverse[1, h, 2 * i]
            free[1, h, 2 * i + 1] = result[:, LANES:] * inverse[1, h, 2 * i + 1]

        loop(X // 2, sources)
        frees = sweep(1, h)
        for t in range(TILES):
            send_free[h, t] = tile_rows(frees, t)
        to_owners(send_free, recv_free, free_send, free_recv, (h,))

    def density(s, h, q):
        def one(i, total):
            rows = pl.ds(8 * X * i, 8 * X)
            term = q[h, rows, :] * comp[s, rows, pl.ds(LANES * h, LANES)].astype(F32)
            return total + jnp.sum(term.reshape(8, X, LANES), axis=0)

        return loop(M // 8, one, jnp.zeros((X, LANES), F32))

    def to_sections(source, target, send_sem, recv_sem):
        for section in far_sections():
            pltpu.make_async_remote_copy(
                src_ref=source,
                dst_ref=target,
                send_sem=send_sem,
                recv_sem=recv_sem,
                device_id={"gx": me, "col": section},
                device_id_type=pl.DeviceIdType.MESH,
            ).start()

    comp_load.wait()
    for h in range(HALVES):

        def middle(i):
            value = jnp.concatenate([free[0, h, 2 * i], free[0, h, 2 * i + 1]], axis=1)
            result = product(left_mid_modes[...], value)
            q_mid[h, pl.ds(2 * i, M, stride=X), :] = result[:, :LANES]
            q_mid[h, pl.ds(2 * i + 1, M, stride=X), :] = result[:, LANES:]

        loop(X // 2, middle)
        send_early[pl.ds(X * h, X)] = density(0, h, q_mid)
    for s in range(STEPS):
        send_early[pl.ds(2 * X + 8 * s, 8)] = jnp.broadcast_to(labels[0, s].astype(F32), (8, LANES))
    to_sections(send_early, recv_early.at[col], early_send, early_recv)
    recv_early[col] = send_early[...]

    @pl.when(is_owner)
    def _():
        wait_for_tiles(recv_unit, unit_recv)

        def units(k, whole_unit):
            prefix_unit[1, k] = whole_unit
            return whole_unit * recv_unit[along(k)]

        whole_unit = loop(cycle, units, jnp.ones((8, LANES), F32))
        wait_for_tiles(recv_free, free_recv)

        def one(k, whole_free):
            p = along(k)
            prefix_free[k] = whole_free
            return recv_unit[p] * whole_free + recv_free[p]

        whole_free = loop(cycle, one, jnp.zeros((8, LANES), F32))
        send_inflows(1, whole_free / (1.0 - whole_unit))

    q_store = [
        pltpu.make_async_copy(q_out.at[h], out_ref.at[:, pl.ds(LANES * h, LANES)], out_sem.at[h])
        for h in range(HALVES)
    ]
    for h in range(HALVES):
        wait_inflows(1, h)
        inflow = recv_flow[1, h].reshape(M, LANES)

        def last(i):
            value = jnp.concatenate([swept(1, h, 2 * i, inflow), swept(1, h, 2 * i + 1, inflow)], axis=1)
            result = product(left_out[...], value)
            q_out[h, pl.ds(2 * i, M, stride=X), :] = result[:, :LANES]
            q_out[h, pl.ds(2 * i + 1, M, stride=X), :] = result[:, LANES:]

        loop(X // 2, last)
        q_store[h].start()
        send_late[h] = density(1, h, q_out)
        to_sections(send_late.at[h], recv_late.at[h, col], late_send.at[h], late_recv.at[h])
        recv_late[h, col] = send_late[h]

    wait_for(recv_early.at[pl.ds(0, sections - 1)], early_recv)
    for h in range(HALVES):
        wait_for(recv_late.at[h, pl.ds(0, sections - 1)], late_recv.at[h])

        def one(c, carry):
            total_a, total_b = carry
            terms = (recv_early[c, pl.ds(X * h, X)], recv_late[h, c])
            for s in range(STEPS):
                label = recv_early[c, pl.ds(2 * X + 8 * s, 8)]
                is_a = jnp.concatenate([label, label], axis=0) == 0.0
                total_a = total_a + jnp.where(is_a, terms[s], 0.0)
                total_b = total_b + jnp.where(is_a, 0.0, terms[s])
            return total_a, total_b

        zeros = jnp.zeros((X, LANES), F32)
        total_a, total_b = loop(sections, one, (zeros, zeros))
        dens[0, :, pl.ds(LANES * h, LANES)] = total_a
        dens[1, :, pl.ds(LANES * h, LANES)] = total_b
    dens_store = pltpu.make_async_copy(dens, dens_ref, dens_sem)
    dens_store.start()

    for h in range(HALVES):
        owns = jnp.logical_and(owns_here, my_half == h)

        for count, when in ((TILES - 1, owns), (TILES, jnp.logical_not(owns))):

            @pl.when(when)
            def _():
                wait_for(send_map.at[h, pl.ds(0, count)], map_send)
                wait_for(send_unit.at[h, pl.ds(0, count)], unit_send)
                wait_for(send_free.at[h, pl.ds(0, count)], free_send)

    for s in range(STEPS):
        wait_for_tiles(send_flow.at[s], flow_send.at[s])

    wait_for(recv_early.at[pl.ds(0, sections - 1)], early_send)
    for h in range(HALVES):
        wait_for(recv_late.at[h, pl.ds(0, sections - 1)], late_send.at[h])
    for copy in q_store:
        copy.wait()
    dens_store.wait()


def body(propagator, complement, labels, absorption, to_ordinates, to_modes, upwind, mode_decay):
    cycle = lax.axis_size("gx")
    sections = lax.axis_size("col")
    rows, lines = M * X, HALVES * LANES
    dma = pltpu.SemaphoreType.DMA
    anywhere = pl.BlockSpec(memory_space=pl.ANY)
    left = pltpu.VMEM((M, 3 * M), BF16)
    cells = pltpu.VMEM((STEPS, HALVES, X, M, LANES), F32)
    scratch = [
        pltpu.VMEM((HALVES, rows, LANES), F32),
        pltpu.VMEM((HALVES, rows, LANES), F32),
        pltpu.VMEM((HALVES, rows, LANES), F32),
        pltpu.VMEM((STEPS, rows, lines), BF16),
        pltpu.SMEM((1, STEPS), jnp.int32),
        pltpu.VMEM((2, X, lines), F32),
        pltpu.VMEM((M, M), F32),
        pltpu.VMEM((M, M), F32),
        pltpu.VMEM((1, M), F32),
        pltpu.VMEM((2, M), F32),
        pltpu.VMEM((M, LANES), F32),
        pltpu.VMEM((STEPS, X, lines), F32),
        left,
        left,
        left,
        left,
        cells,
        cells,
        cells,
        cells,
        pltpu.VMEM((HALVES, TILES, 2, 8, LANES), F32),
        pltpu.VMEM((cycle, 2, 8, LANES), F32),
        pltpu.VMEM((HALVES, TILES, 8, LANES), F32),
        pltpu.VMEM((cycle, 8, LANES), F32),
        pltpu.VMEM((HALVES, TILES, 8, LANES), F32),
        pltpu.VMEM((cycle, 8, LANES), F32),
        pltpu.VMEM((STEPS, cycle, 8, LANES), F32),
        pltpu.VMEM((cycle, 8, LANES), F32),
        pltpu.VMEM((STEPS, cycle, 8, LANES), F32),
        pltpu.VMEM((STEPS, HALVES, TILES, 8, LANES), F32),
        pltpu.VMEM((3 * X, LANES), F32),
        pltpu.VMEM((sections, 3 * X, LANES), F32),
        pltpu.VMEM((HALVES, X, LANES), F32),
        pltpu.VMEM((HALVES, sections, X, LANES), F32),
        pltpu.VMEM((2, X, lines), F32),
        dma((6,)),
        dma((HALVES,)),
        dma,
        dma,
        dma,
        dma,
        dma,
        dma,
        dma,
        dma((STEPS,)),
        dma((STEPS, HALVES)),
        dma,
        dma,
        dma((HALVES,)),
        dma((HALVES,)),
        dma((HALVES,)),
        dma,
    ]
    propagated, density = pl.pallas_call(
        functools.partial(kernel, cycle, sections),
        out_shape=(
            jax.ShapeDtypeStruct((rows, lines), F32),
            jax.ShapeDtypeStruct((2, X, lines), F32),
        ),
        in_specs=[anywhere] * 8,
        out_specs=(anywhere, anywhere),
        scratch_shapes=scratch,
        compiler_params=pltpu.CompilerParams(
            collective_id=0, has_side_effects=True, vmem_limit_bytes=48 * 1024 * 1024
        ),
        name="contour_steps",
    )(
        *(
            pltpu.with_memory_space_constraint(operand, pltpu.HBM)
            for operand in (
                propagator.reshape(rows, lines),
                complement.reshape(STEPS, rows, lines),
                labels,
                absorption,
                to_ordinates,
                to_modes,
                upwind.reshape(1, M),
                mode_decay,
            )
        )
    )
    return propagated.reshape(1, M, X, lines), density


def solution(mesh):
    in_specs = (
        P("col", None, "gx", None),
        P("col", None, None, "gx", None),
        P("col", None),
        P(None, "gx", None),
        P(),
        P(),
        P(),
        P(),
    )
    out_specs = (P("col", None, "gx", None), P(None, "gx", None))
    return jax.shard_map(body, mesh=mesh, in_specs=in_specs, out_specs=out_specs, check_vma=False)
```

```python
import functools

import jax
import jax.numpy as jnp
from jax import lax
from jax.experimental import pallas as pl
from jax.experimental.pallas import tpu as pltpu
from jax.sharding import PartitionSpec as P

F32, BF16 = jnp.float32, jnp.bfloat16
M = 64
HALF = M // 2
X = 16
LANES = 128
HALVES = 2
STEPS = 2
TILES = M // 8
RING_Z, RING_Y, RING_X = 8, 4, 4
FAR_Z, FAR_Y, FAR_X = (4, 3, 5, 2, 6, 1, 7, 0), (2, 1, 3, 0), (2, 1, 3, 0)


def loop(count, step, carry=None):
    if carry is None:

        def plain(i, none):
            step(i)
            return none

        lax.fori_loop(0, count, plain, 0, unroll=True)
        return None
    return lax.fori_loop(0, count, step, carry, unroll=True)


def column(row):
    wide = jnp.broadcast_to(row, (M, M))
    here = lax.broadcasted_iota(jnp.int32, (M, M), 0) == lax.broadcasted_iota(jnp.int32, (M, M), 1)
    return jnp.sum(jnp.where(here, wide, 0.0), axis=1, keepdims=True)


def split(value):
    high = value.astype(BF16)
    low = (value - high.astype(F32)).astype(BF16)
    return high, low


def left_operand(weights):
    high, low = split(weights)
    return jnp.concatenate([high, high, low], axis=1)


def product(left, value):
    high, low = split(value)
    right = jnp.concatenate([high, low, high], axis=0)
    return jnp.dot(left, right, preferred_element_type=F32)


def kernel(
    cycle,
    sections,
    prop_ref,
    comp_ref,
    labels_ref,
    absorb_ref,
    ordin_ref,
    modes_ref,
    upwind_ref,
    decay_ref,
    out_ref,
    dens_ref,
    q_in,
    q_mid,
    q_out,
    comp,
    labels,
    absorb,
    ordin,
    modes,
    upwind,
    decay,
    rate,
    absorb_now,
    left_in,
    left_mid,
    left_mid_modes,
    left_out,
    left_comp,
    inverse,
    ratio,
    unit,
    free,
    send_map,
    recv_map,
    send_unit,
    recv_unit,
    send_free,
    recv_free,
    prefix_unit,
    prefix_free,
    send_flow,
    recv_flow,
    send_early,
    recv_early,
    send_late,
    recv_late,
    weight,
    comp_wide,
    comp_ordin,
    load_sem,
    q_sem,
    comp_sem,
    map_send,
    map_recv,
    unit_send,
    unit_recv,
    free_send,
    free_recv,
    flow_send,
    flow_recv,
    early_send,
    early_recv,
    late_send,
    late_recv,
    out_sem,
):
    me = lax.axis_index("gx")
    col = lax.axis_index("col")
    core = lax.rem(col, 2)
    my_z, my_y, my_x = me // RING_Y, lax.rem(me, RING_Y), col // 2
    is_owner = core == 1
    parity = lax.rem(my_z + my_y, 2)
    owns_here = jnp.logical_and(is_owner, parity == 1)
    owns_other = jnp.logical_and(is_owner, parity == 0)
    my_tile, my_half = my_z, my_y // 2
    owner_col = col - core + 1
    served_col = col - 1 + parity

    barrier = pltpu.get_barrier_semaphore()

    def far_places():
        for dz in FAR_Z:
            for dy in FAR_Y:
                yield RING_Y * lax.rem(my_z + dz, RING_Z) + lax.rem(my_y + dy, RING_Y), (dz, dy) == (0, 0)

    def far_sections():
        for dx in FAR_X:
            for dc in range(2):
                if (dx, dc) != (0, 0):
                    yield 2 * lax.rem(my_x + dx, RING_X) + lax.rem(core + dc, 2)

    def far_owners(halves=range(HALVES)):
        for dz in FAR_Z:
            for h in halves:
                t = lax.rem(my_z + dz, RING_Z)
                yield t, h, RING_Y * t + 2 * h + lax.rem(t + core, 2), dz == 0

    def greet(place, section):
        pl.semaphore_signal(
            barrier, inc=1, device_id={"gx": place, "col": section}, device_id_type=pl.DeviceIdType.MESH
        )

    @pl.when(owns_here)
    def _():
        for place, here in far_places():
            if not here:
                greet(place, col)

    @pl.when(owns_other)
    def _():
        for place, here in far_places():
            greet(place, served_col)

    @pl.when(jnp.logical_not(owns_here))
    def _():
        for t, h, owner, near in far_owners():
            greet(owner, owner_col)

    for section in far_sections():
        greet(me, section)
    greeted = jnp.where(owns_here, cycle - 1, jnp.where(owns_other, cycle + 2 * TILES, 2 * TILES)) + sections - 1

    small = [
        pltpu.make_async_copy(src, dst, load_sem.at[i])
        for i, (src, dst) in enumerate(
            (
                (absorb_ref, absorb),
                (upwind_ref, upwind),
                (labels_ref, labels),
                (ordin_ref, ordin),
                (modes_ref, modes),
                (decay_ref, decay),
            )
        )
    ]
    for copy in small:
        copy.start()
    q_load = [
        pltpu.make_async_copy(prop_ref.at[:, pl.ds(LANES * h, LANES)], q_in.at[h], q_sem.at[h])
        for h in range(HALVES)
    ]
    for copy in q_load:
        copy.start()
    comp_load = pltpu.make_async_copy(comp_ref, comp, comp_sem)
    comp_load.start()

    for copy in small:
        copy.wait()

    rate[...] = jnp.broadcast_to(column(upwind[...]), (M, LANES))
    first = [labels[0, s] == 0 for s in range(STEPS)]
    for s in range(STEPS):
        absorb_now[s] = jnp.where(first[s], absorb[0], absorb[1])
    left_in[...] = left_operand(ordin[...])

    def coefficients(s, h):
        def one(i, carry):
            up, down = carry
            lanes = pl.ds(LANES * h, LANES)
            j = X - 1 - i
            rate_up, rate_down = rate[:HALF], rate[HALF:]
            inverse_up = 1.0 / (1.0 + rate_up + absorb_now[s, pl.ds(i, 1), lanes])
            inverse_down = 1.0 / (1.0 + rate_down + absorb_now[s, pl.ds(j, 1), lanes])
            ratio_up = rate_up * inverse_up
            ratio_down = rate_down * inverse_down
            up = up * ratio_up
            down = down * ratio_down
            inverse[s, h, i, :HALF] = inverse_up
            inverse[s, h, j, HALF:] = inverse_down
            ratio[s, h, i, :HALF] = ratio_up
            ratio[s, h, j, HALF:] = ratio_down
            unit[s, h, i, :HALF] = up
            unit[s, h, j, HALF:] = down
            return up, down

        ones = jnp.ones((HALF, LANES), F32)
        return loop(X, one, (ones, ones))

    def sweep(s, h):
        def one(i, carry):
            up, down = carry
            j = X - 1 - i
            up = free[s, h, i, :HALF] * inverse[s, h, i, :HALF] + ratio[s, h, i, :HALF] * up
            down = free[s, h, j, HALF:] * inverse[s, h, j, HALF:] + ratio[s, h, j, HALF:] * down
            free[s, h, i, :HALF] = up
            free[s, h, j, HALF:] = down
            return up, down

        zeros = jnp.zeros((HALF, LANES), F32)
        return loop(X, one, (zeros, zeros))

    def weights(h):
        def one(i, carry):
            up, down = carry
            j = X - 1 - i
            weight[h, j, :HALF] = inverse[1, h, j, :HALF] * up
            weight[h, i, HALF:] = inverse[1, h, i, HALF:] * down
            return up * ratio[1, h, j, :HALF], down * ratio[1, h, i, HALF:]

        ones = jnp.ones((HALF, LANES), F32)
        loop(X, one, (ones, ones))

    def to_owners(source, target, send_sem, recv_sem, halves):
        for t, h, owner, near in far_owners(halves):

            def send(t=t, h=h, owner=owner):
                pltpu.make_async_remote_copy(
                    src_ref=source.at[h, t],
                    dst_ref=target.at[me],
                    send_sem=send_sem,
                    recv_sem=recv_sem,
                    device_id={"gx": owner, "col": owner_col},
                    device_id_type=pl.DeviceIdType.MESH,
                ).start()

            if near:
                pl.when(jnp.logical_not(jnp.logical_and(owns_here, h == my_half)))(send)
            else:
                send()

        for h in halves:

            @pl.when(jnp.logical_and(owns_here, my_half == h))
            def _():
                target[me] = source[h, my_tile]

    def tile_rows(pair, t):
        up, down = pair
        rows = up if t < TILES // 2 else down
        base = 8 * (t % (TILES // 2))
        return rows[base : base + 8]

    for h in range(HALVES):
        units = coefficients(0, h)
        for t in range(TILES):
            send_map[h, t, 0] = tile_rows(units, t)
    for h in range(HALVES):
        units = coefficients(1, h)
        for t in range(TILES):
            send_unit[h, t] = tile_rows(units, t)
    gained = []
    for s in range(STEPS):
        gain = jnp.where(first[s], decay[0:1], decay[1:2])
        gained.append(column(gain) * modes[...])
    left_mid[...] = left_operand(
        jnp.dot(ordin[...], gained[0], preferred_element_type=F32, precision=lax.Precision.HIGHEST)
    )
    left_mid_modes[...] = left_operand(gained[0])
    left_out[...] = left_operand(gained[1])
    left_comp[...] = jnp.concatenate(split(gained[1].T), axis=1)

    for h in range(HALVES):
        q_load[h].wait()

        def sources(i):
            value = jnp.concatenate(
                [q_in[h, pl.ds(2 * i, M, stride=X), :], q_in[h, pl.ds(2 * i + 1, M, stride=X), :]], axis=1
            )
            result = product(left_in[...], value)
            free[0, h, 2 * i] = result[:, :LANES]
            free[0, h, 2 * i + 1] = result[:, LANES:]

        loop(X // 2, sources)
        frees = sweep(0, h)
        for t in range(TILES):
            send_map[h, t, 1] = tile_rows(frees, t)
    pl.semaphore_wait(barrier, greeted)
    to_owners(send_map, recv_map, map_send, map_recv, range(HALVES))
    to_owners(send_unit, recv_unit, unit_send, unit_recv, range(HALVES))

    for h in range(HALVES):
        weights(h)
    comp_load.wait()
    for h in range(HALVES):

        def widen(i):
            rows = pl.ds(8 * X * i, 8 * X)
            comp_wide[h, rows] = comp[1, rows, pl.ds(LANES * h, LANES)].astype(F32)

        loop(M // 8, widen)

        def to_ordinates(i):
            value = jnp.concatenate(
                [comp_wide[h, pl.ds(2 * i, M, stride=X), :], comp_wide[h, pl.ds(2 * i + 1, M, stride=X), :]], axis=1
            ).astype(BF16)
            result = jnp.dot(left_comp[...], jnp.concatenate([value, value], axis=0), preferred_element_type=F32)
            comp_ordin[h, 2 * i] = result[:, :LANES]
            comp_ordin[h, 2 * i + 1] = result[:, LANES:]

        loop(X // 2, to_ordinates)

    def along(k):
        return jnp.where(my_tile < TILES // 2, k, cycle - 1 - k)

    def wait_for(ref, sem):
        pltpu.make_async_copy(ref, ref, sem).wait()

    def wait_for_tiles(ref, sem):
        @pl.when(owns_here)
        def _():
            wait_for(ref.at[pl.ds(0, cycle - 1)], sem)

        @pl.when(owns_other)
        def _():
            wait_for(ref, sem)

    def send_inflows(s, entry):
        for p, here in far_places():
            k = along(p)
            send_flow[s, p] = prefix_unit[s, k] * entry + prefix_free[k]

            def send(p=p):
                pltpu.make_async_remote_copy(
                    src_ref=send_flow.at[s, p],
                    dst_ref=recv_flow.at[s, my_half, my_tile],
                    send_sem=flow_send.at[s],
                    recv_sem=flow_recv.at[s, my_half],
                    device_id={"gx": p, "col": served_col},
                    device_id_type=pl.DeviceIdType.MESH,
                ).start()

            if here:
                pl.when(owns_other)(send)
            else:
                send()

        @pl.when(owns_here)
        def _():
            recv_flow[s, my_half, my_tile] = send_flow[s, me]

    @pl.when(is_owner)
    def _():
        wait_for_tiles(recv_map, map_recv)

        def one(k, carry):
            whole_unit, whole_free = carry
            p = along(k)
            prefix_unit[0, k] = whole_unit
            prefix_free[k] = whole_free
            step_unit = recv_map[p, 0]
            return whole_unit * step_unit, step_unit * whole_free + recv_map[p, 1]

        ones, zeros = jnp.ones((8, LANES), F32), jnp.zeros((8, LANES), F32)
        whole_unit, whole_free = loop(cycle, one, (ones, zeros))
        send_inflows(0, whole_free / (1.0 - whole_unit))

    def wait_inflows(s, h):
        owns = jnp.logical_and(owns_here, my_half == h)

        @pl.when(owns)
        def _():
            wait_for(recv_flow.at[s, h, pl.ds(0, TILES - 1)], flow_recv.at[s, h])

        @pl.when(jnp.logical_not(owns))
        def _():
            wait_for(recv_flow.at[s, h], flow_recv.at[s, h])

    def swept(s, h, i, inflow):
        return free[s, h, i] + unit[s, h, i] * inflow

    for h in range(HALVES):
        wait_inflows(0, h)
        inflow = recv_flow[0, h].reshape(M, LANES)

        def sources(i, outflow):
            a, b = swept(0, h, 2 * i, inflow), swept(0, h, 2 * i + 1, inflow)
            free[0, h, 2 * i] = a
            free[0, h, 2 * i + 1] = b
            result = product(left_mid[...], jnp.concatenate([a, b], axis=1))
            a, b = result[:, :LANES], result[:, LANES:]
            free[1, h, 2 * i] = a
            free[1, h, 2 * i + 1] = b
            return outflow + weight[h, 2 * i] * a + weight[h, 2 * i + 1] * b

        outflow = loop(X // 2, sources, jnp.zeros((M, LANES), F32))
        send_free[h] = outflow.reshape(TILES, 8, LANES)
        to_owners(send_free, recv_free, free_send, free_recv, (h,))

    def density(s, h, q):
        def one(i, total):
            rows = pl.ds(8 * X * i, 8 * X)
            term = q[h, rows, :] * comp[s, rows, pl.ds(LANES * h, LANES)].astype(F32)
            return total + jnp.sum(term.reshape(8, X, LANES), axis=0)

        return loop(M // 8, one, jnp.zeros((X, LANES), F32))

    def to_sections(source, target, send_sem, recv_sem):
        for section in far_sections():
            pltpu.make_async_remote_copy(
                src_ref=source,
                dst_ref=target,
                send_sem=send_sem,
                recv_sem=recv_sem,
                device_id={"gx": me, "col": section},
                device_id_type=pl.DeviceIdType.MESH,
            ).start()

    for h in range(HALVES):
        sweep(1, h)
    for h in range(HALVES):

        def middle(i):
            value = jnp.concatenate([free[0, h, 2 * i], free[0, h, 2 * i + 1]], axis=1)
            result = product(left_mid_modes[...], value)
            q_mid[h, pl.ds(2 * i, M, stride=X), :] = result[:, :LANES]
            q_mid[h, pl.ds(2 * i + 1, M, stride=X), :] = result[:, LANES:]

        loop(X // 2, middle)
        send_early[pl.ds(X * h, X)] = density(0, h, q_mid)
    for s in range(STEPS):
        send_early[pl.ds(2 * X + 8 * s, 8)] = jnp.broadcast_to(labels[0, s].astype(F32), (8, LANES))
    to_sections(send_early, recv_early.at[col], early_send, early_recv)
    recv_early[col] = send_early[...]

    @pl.when(is_owner)
    def _():
        wait_for_tiles(recv_unit, unit_recv)

        def units(k, whole_unit):
            prefix_unit[1, k] = whole_unit
            return whole_unit * recv_unit[along(k)]

        whole_unit = loop(cycle, units, jnp.ones((8, LANES), F32))
        wait_for_tiles(recv_free, free_recv)

        def one(k, whole_free):
            p = along(k)
            prefix_free[k] = whole_free
            return recv_unit[p] * whole_free + recv_free[p]

        whole_free = loop(cycle, one, jnp.zeros((8, LANES), F32))
        send_inflows(1, whole_free / (1.0 - whole_unit))

    for h in range(HALVES):
        wait_inflows(1, h)
        inflow = recv_flow[1, h].reshape(M, LANES)

        def last_density(i):
            solved = swept(1, h, i, inflow)
            free[1, h, i] = solved
            send_late[h, pl.ds(i, 1)] = jnp.sum(solved * comp_ordin[h, i], axis=0, keepdims=True)

        loop(X, last_density)
        to_sections(send_late.at[h], recv_late.at[h, col], late_send.at[h], late_recv.at[h])
        recv_late[h, col] = send_late[h]
    q_store = [
        pltpu.make_async_copy(q_out.at[h], out_ref.at[:, pl.ds(LANES * h, LANES)], out_sem.at[h])
        for h in range(HALVES)
    ]
    for h in range(HALVES):

        def last(i):
            value = jnp.concatenate([free[1, h, 2 * i], free[1, h, 2 * i + 1]], axis=1)
            result = product(left_out[...], value)
            q_out[h, pl.ds(2 * i, M, stride=X), :] = result[:, :LANES]
            q_out[h, pl.ds(2 * i + 1, M, stride=X), :] = result[:, LANES:]

        loop(X // 2, last)
        q_store[h].start()

    wait_for(recv_early.at[pl.ds(0, sections - 1)], early_recv)

    def add_densities(carry, terms, s):
        def one(c, carry):
            total_a, total_b = carry
            label = recv_early[c, pl.ds(2 * X + 8 * s, 8)]
            is_a = jnp.concatenate([label, label], axis=0) == 0.0
            term = terms(c)
            return total_a + jnp.where(is_a, term, 0.0), total_b + jnp.where(is_a, 0.0, term)

        return loop(sections, one, carry)

    zeros = jnp.zeros((X, LANES), F32)
    early = [
        add_densities((zeros, zeros), lambda c, h=h: recv_early[c, pl.ds(X * h, X)], 0) for h in range(HALVES)
    ]
    for h in range(HALVES):
        wait_for(recv_late.at[h, pl.ds(0, sections - 1)], late_recv.at[h])
        total_a, total_b = add_densities(early[h], lambda c, h=h: recv_late[h, c], 1)
        dens_ref[0, :, pl.ds(LANES * h, LANES)] = total_a
        dens_ref[1, :, pl.ds(LANES * h, LANES)] = total_b

    for h in range(HALVES):
        owns = jnp.logical_and(owns_here, my_half == h)

        for count, when in ((TILES - 1, owns), (TILES, jnp.logical_not(owns))):

            @pl.when(when)
            def _():
                wait_for(send_map.at[h, pl.ds(0, count)], map_send)
                wait_for(send_unit.at[h, pl.ds(0, count)], unit_send)
                wait_for(send_free.at[h, pl.ds(0, count)], free_send)

    for s in range(STEPS):
        wait_for_tiles(send_flow.at[s], flow_send.at[s])

    wait_for(recv_early.at[pl.ds(0, sections - 1)], early_send)
    for h in range(HALVES):
        wait_for(recv_late.at[h, pl.ds(0, sections - 1)], late_send.at[h])
    for copy in q_store:
        copy.wait()


STORES = 4


def store(q_ref, dens_ref, q_out, dens_out, sem):
    part = M * X // STORES
    copies = [pltpu.make_async_copy(dens_ref, dens_out, sem.at[STORES])]
    for i in range(STORES):
        rows = pl.ds(part * i, part)
        copies.append(pltpu.make_async_copy(q_ref.at[rows], q_out.at[rows], sem.at[i]))
    for copy in copies:
        copy.start()
    for copy in copies:
        copy.wait()


def body(propagator, complement, labels, absorption, to_ordinates, to_modes, upwind, mode_decay):
    cycle = lax.axis_size("gx")
    sections = lax.axis_size("col")
    rows, lines = M * X, HALVES * LANES
    dma = pltpu.SemaphoreType.DMA
    anywhere = pl.BlockSpec(memory_space=pl.ANY)
    left = pltpu.VMEM((M, 3 * M), BF16)
    cells = pltpu.VMEM((STEPS, HALVES, X, M, LANES), F32)
    halves_cells = pltpu.VMEM((HALVES, X, M, LANES), F32)
    scratch = [
        pltpu.VMEM((HALVES, rows, LANES), F32),
        pltpu.VMEM((HALVES, rows, LANES), F32),
        pltpu.VMEM((HALVES, rows, LANES), F32),
        pltpu.VMEM((STEPS, rows, lines), BF16),
        pltpu.SMEM((1, STEPS), jnp.int32),
        pltpu.VMEM((2, X, lines), F32),
        pltpu.VMEM((M, M), F32),
        pltpu.VMEM((M, M), F32),
        pltpu.VMEM((1, M), F32),
        pltpu.VMEM((2, M), F32),
        pltpu.VMEM((M, LANES), F32),
        pltpu.VMEM((STEPS, X, lines), F32),
        left,
        left,
        left,
        left,
        pltpu.VMEM((M, 2 * M), BF16),
        cells,
        cells,
        cells,
        cells,
        pltpu.VMEM((HALVES, TILES, 2, 8, LANES), F32),
        pltpu.VMEM((cycle, 2, 8, LANES), F32),
        pltpu.VMEM((HALVES, TILES, 8, LANES), F32),
        pltpu.VMEM((cycle, 8, LANES), F32),
        pltpu.VMEM((HALVES, TILES, 8, LANES), F32),
        pltpu.VMEM((cycle, 8, LANES), F32),
        pltpu.VMEM((STEPS, cycle, 8, LANES), F32),
        pltpu.VMEM((cycle, 8, LANES), F32),
        pltpu.VMEM((STEPS, cycle, 8, LANES), F32),
        pltpu.VMEM((STEPS, HALVES, TILES, 8, LANES), F32),
        pltpu.VMEM((3 * X, LANES), F32),
        pltpu.VMEM((sections, 3 * X, LANES), F32),
        pltpu.VMEM((HALVES, X, LANES), F32),
        pltpu.VMEM((HALVES, sections, X, LANES), F32),
        halves_cells,
        pltpu.VMEM((HALVES, rows, LANES), F32),
        halves_cells,
        dma((6,)),
        dma((HALVES,)),
        dma,
        dma,
        dma,
        dma,
        dma,
        dma,
        dma,
        dma((STEPS,)),
        dma((STEPS, HALVES)),
        dma,
        dma,
        dma((HALVES,)),
        dma((HALVES,)),
        dma((HALVES,)),
    ]
    propagated, density = pl.pallas_call(
        functools.partial(kernel, cycle, sections),
        out_shape=(
            jax.ShapeDtypeStruct((rows, lines), F32),
            jax.ShapeDtypeStruct((2, X, lines), F32),
        ),
        in_specs=[anywhere] * 8,
        out_specs=(anywhere, pl.BlockSpec(memory_space=pltpu.VMEM)),
        scratch_shapes=scratch,
        compiler_params=pltpu.CompilerParams(
            collective_id=0, has_side_effects=True, vmem_limit_bytes=48 * 1024 * 1024
        ),
        name="contour_steps",
    )(
        *(
            pltpu.with_memory_space_constraint(operand, pltpu.HBM)
            for operand in (
                propagator.reshape(rows, lines),
                complement.reshape(STEPS, rows, lines),
                labels,
                absorption,
                to_ordinates,
                to_modes,
                upwind.reshape(1, M),
                mode_decay,
            )
        )
    )
    propagated, density = pl.pallas_call(
        store,
        out_shape=(
            jax.ShapeDtypeStruct((rows, lines), F32),
            jax.ShapeDtypeStruct((2, X, lines), F32),
        ),
        in_specs=[anywhere] * 2,
        out_specs=(anywhere, anywhere),
        scratch_shapes=[dma((STORES + 1,))],
        compiler_params=pltpu.CompilerParams(vmem_limit_bytes=1024 * 1024),
        name="store_results",
    )(propagated, density)
    return propagated.reshape(1, M, X, lines), density


def solution(mesh):
    in_specs = (
        P("col", None, "gx", None),
        P("col", None, None, "gx", None),
        P("col", None),
        P(None, "gx", None),
        P(),
        P(),
        P(),
        P(),
    )
    out_specs = (P("col", None, "gx", None), P(None, "gx", None))
    return jax.shard_map(body, mesh=mesh, in_specs=in_specs, out_specs=out_specs, check_vma=False)
```

```python
import jax
import jax.numpy as jnp
from jax import lax
from jax.experimental import pallas as pl
from jax.experimental.pallas import tpu as pltpu
from jax.sharding import PartitionSpec as P

F32, BF16 = jnp.float32, jnp.bfloat16
M = 64
HALF = M // 2
X = 16
LANES = 128
HALVES = 2
STEPS = 2
CYCLE, SECTIONS = 32, 8
OWN = 8
ROWS = CYCLE * OWN
RING_Z, RING_Y, RING_X = 8, 4, 4
FAR_Z, FAR_Y, FAR_X = (4, 3, 5, 2, 6, 1, 7, 0), (2, 1, 3, 0), (2, 1, 3, 0)
STORES = 4


def loop(count, step, carry=None):
    if carry is None:

        def plain(i, none):
            step(i)
            return none

        lax.fori_loop(0, count, plain, 0, unroll=True)
        return None
    return lax.fori_loop(0, count, step, carry, unroll=True)


def column(row):
    wide = jnp.broadcast_to(row, (M, M))
    here = lax.broadcasted_iota(jnp.int32, (M, M), 0) == lax.broadcasted_iota(jnp.int32, (M, M), 1)
    return jnp.sum(jnp.where(here, wide, 0.0), axis=1, keepdims=True)


def split(value):
    high = value.astype(BF16)
    low = (value - high.astype(F32)).astype(BF16)
    return high, low


def left_operand(weights):
    high, low = split(weights)
    return jnp.concatenate([high, high, low], axis=1)


def product(left, value):
    high, low = split(value)
    right = jnp.concatenate([high, low, high], axis=0)
    return jnp.dot(left, right, preferred_element_type=F32)


def wait_for(ref, sem):
    pltpu.make_async_copy(ref, ref, sem).wait()


def kernel(
    prop_ref,
    comp_ref,
    labels_ref,
    absorb_ref,
    ordin_ref,
    modes_ref,
    upwind_ref,
    decay_ref,
    out_ref,
    dens_ref,
    q_in,
    q_out,
    comp,
    labels,
    absorb,
    ordin,
    modes,
    upwind,
    decay,
    rate,
    absorb_now,
    left_in,
    left_mid,
    left_out,
    left_comp,
    inverse,
    ratio,
    unit,
    free,
    weight,
    comp_wide,
    comp_ordin,
    turned,
    send_absorb,
    recv_absorb,
    own_wide,
    own_absorb,
    own_inverse,
    own_ratio,
    own_unit,
    own_weight,
    send_out,
    recv_out,
    own_factor,
    prefix_unit,
    prefix_free,
    own_extra,
    send_flow,
    recv_flow,
    send_early,
    recv_early,
    send_late,
    recv_late,
    load_sem,
    q_sem,
    comp_sem,
    absorb_send,
    absorb_recv,
    out_send,
    out_recv,
    flow_send,
    flow_recv,
    early_send,
    early_recv,
    late_send,
    late_recv,
    store_sem,
):
    me = lax.axis_index("gx")
    col = lax.axis_index("col")
    core = lax.rem(col, 2)
    my_z, my_y, my_x = me // RING_Y, lax.rem(me, RING_Y), col // 2

    def far_places():
        for dz in FAR_Z:
            for dy in FAR_Y:
                if (dz, dy) != (0, 0):
                    yield RING_Y * lax.rem(my_z + dz, RING_Z) + lax.rem(my_y + dy, RING_Y)

    def far_sections():
        for dx in FAR_X:
            for dc in range(2):
                if (dx, dc) != (0, 0):
                    yield 2 * lax.rem(my_x + dx, RING_X) + lax.rem(core + dc, 2)

    barrier = pltpu.get_barrier_semaphore()

    def greet(place, section):
        pl.semaphore_signal(
            barrier, inc=1, device_id={"gx": place, "col": section}, device_id_type=pl.DeviceIdType.MESH
        )

    for place in far_places():
        greet(place, col)
    for section in far_sections():
        greet(me, section)

    small = [
        pltpu.make_async_copy(src, dst, load_sem.at[i])
        for i, (src, dst) in enumerate(
            (
                (absorb_ref, absorb),
                (upwind_ref, upwind),
                (labels_ref, labels),
                (ordin_ref, ordin),
                (modes_ref, modes),
                (decay_ref, decay),
            )
        )
    ]
    for copy in small:
        copy.start()
    q_load = [
        pltpu.make_async_copy(prop_ref.at[:, pl.ds(LANES * h, LANES)], q_in.at[h], q_sem.at[h])
        for h in range(HALVES)
    ]
    for copy in q_load:
        copy.start()
    comp_load = pltpu.make_async_copy(comp_ref, comp, comp_sem)
    comp_load.start()
    for copy in small:
        copy.wait()

    rate[...] = jnp.broadcast_to(column(upwind[...]), (M, LANES))
    first = [labels[0, s] == 0 for s in range(STEPS)]
    for s in range(STEPS):
        absorb_now[s] = jnp.where(first[s], absorb[0], absorb[1])
    left_in[...] = left_operand(ordin[...])

    def coefficients(rows, h, inverse, ratio, unit):
        def one(i, carry):
            up, down = carry
            lanes = pl.ds(LANES * h, LANES)
            j = X - 1 - i
            rate_up, rate_down = rate[:HALF], rate[HALF:]
            inverse_up = 1.0 / (1.0 + rate_up + rows[pl.ds(i, 1), lanes])
            inverse_down = 1.0 / (1.0 + rate_down + rows[pl.ds(j, 1), lanes])
            ratio_up = rate_up * inverse_up
            ratio_down = rate_down * inverse_down
            up = up * ratio_up
            down = down * ratio_down
            if inverse is not None:
                inverse[i, :HALF] = inverse_up
                inverse[j, HALF:] = inverse_down
                ratio[i, :HALF] = ratio_up
                ratio[j, HALF:] = ratio_down
            if unit is not None:
                unit[i, :HALF] = up
                unit[j, HALF:] = down
            return up, down

        ones = jnp.ones((HALF, LANES), F32)
        return jnp.concatenate(loop(X, one, (ones, ones)), axis=0)

    def weights(inverse, ratio, weight):
        def one(i, carry):
            up, down = carry
            j = X - 1 - i
            weight[j, :HALF] = inverse[j, :HALF] * up
            weight[i, HALF:] = inverse[i, HALF:] * down
            return up * ratio[j, :HALF], down * ratio[i, HALF:]

        ones = jnp.ones((HALF, LANES), F32)
        loop(X, one, (ones, ones))

    def sweep(s, h):
        def one(i, carry):
            up, down = carry
            j = X - 1 - i
            up = free[s, h, i, :HALF] * inverse[s, h, i, :HALF] + ratio[s, h, i, :HALF] * up
            down = free[s, h, j, HALF:] * inverse[s, h, j, HALF:] + ratio[s, h, j, HALF:] * down
            free[s, h, i, :HALF] = up
            free[s, h, j, HALF:] = down
            return up, down

        zeros = jnp.zeros((HALF, LANES), F32)
        return jnp.concatenate(loop(X, one, (zeros, zeros)), axis=0)

    wide = jnp.concatenate([absorb_now[0], absorb_now[1], jnp.zeros((LANES - 2 * X, 2 * LANES), F32)], axis=0)
    turned[...] = wide.T
    packed = turned[pl.ds(0, ROWS // 4, stride=4), :]
    for i in range(1, 4):
        packed = packed + pltpu.roll(turned[pl.ds(i, ROWS // 4, stride=4), :], 2 * X * i, axis=1)
    for o in range(CYCLE):
        send_absorb[o] = packed[2 * o : 2 * o + 2]

    for h in range(HALVES):
        for s in range(STEPS):
            coefficients(absorb_now.at[s], h, inverse.at[s, h], ratio.at[s, h], unit.at[s, h])
        weights(inverse.at[1, h], ratio.at[1, h], weight.at[h])
    gained = []
    for s in range(STEPS):
        gain = jnp.where(first[s], decay[0:1], decay[1:2])
        gained.append(column(gain) * modes[...])
        left_comp[s] = jnp.concatenate(split(gained[s].T), axis=1)
    left_mid[...] = left_operand(
        jnp.dot(ordin[...], gained[0], preferred_element_type=F32, precision=lax.Precision.HIGHEST)
    )
    left_out[...] = left_operand(gained[1])
    for h in range(HALVES):
        q_load[h].wait()

        def sources(i):
            value = jnp.concatenate(
                [q_in[h, pl.ds(2 * i, M, stride=X), :], q_in[h, pl.ds(2 * i + 1, M, stride=X), :]], axis=1
            )
            result = product(left_in[...], value)
            free[0, h, 2 * i] = result[:, :LANES]
            free[0, h, 2 * i + 1] = result[:, LANES:]

        loop(X // 2, sources)
        outflow = sweep(0, h)

        def sources_free(i, outflow):
            value = jnp.concatenate([free[0, h, 2 * i], free[0, h, 2 * i + 1]], axis=1)
            result = product(left_mid[...], value)
            return outflow + weight[h, 2 * i] * result[:, :LANES] + weight[h, 2 * i + 1] * result[:, LANES:]

        outflow_next = loop(X // 2, sources_free, jnp.zeros((M, LANES), F32))
        send_out[pl.ds(LANES * h, LANES)] = jnp.concatenate([outflow, outflow_next], axis=0).T

    def own_rows(p):
        return pl.ds(pl.multiple_of(OWN * p, OWN), OWN)

    def remote(source, target, send_sem, recv_sem, place, section):
        pltpu.make_async_remote_copy(
            src_ref=source,
            dst_ref=target,
            send_sem=send_sem,
            recv_sem=recv_sem,
            device_id={"gx": place, "col": section},
            device_id_type=pl.DeviceIdType.MESH,
        ).start()

    pl.semaphore_wait(barrier, CYCLE + SECTIONS - 2)
    for p in far_places():
        remote(send_absorb.at[p], recv_absorb.at[me], absorb_send, absorb_recv, p, col)
    for p in far_places():
        remote(send_out.at[own_rows(p)], recv_out.at[own_rows(me)], out_send, out_recv, p, col)
    recv_absorb[me] = send_absorb[me]
    recv_out[own_rows(me)] = send_out[own_rows(me)]

    comp_load.wait()
    for s in range(STEPS):
        for h in range(HALVES):

            def widen(i):
                rows = pl.ds(8 * X * i, 8 * X)
                comp_wide[s, h, rows] = comp[s, rows, pl.ds(LANES * h, LANES)].astype(F32)

            loop(M // 8, widen)

            def to_ordinates(i):
                value = jnp.concatenate(
                    [
                        comp_wide[s, h, pl.ds(2 * i, M, stride=X), :],
                        comp_wide[s, h, pl.ds(2 * i + 1, M, stride=X), :],
                    ],
                    axis=1,
                ).astype(BF16)
                result = jnp.dot(left_comp[s], jnp.concatenate([value, value], axis=0), preferred_element_type=F32)
                comp_ordin[s, h, 2 * i] = result[:, :LANES]
                comp_ordin[s, h, 2 * i + 1] = result[:, LANES:]

            loop(X // 2, to_ordinates)

    wait_for(recv_absorb.at[pl.ds(0, CYCLE - 1)], absorb_recv)
    for p in range(CYCLE):
        own_wide[pl.ds(2 * p, 2)] = recv_absorb[p]
    for h in range(HALVES):
        parts = [own_wide[...]] if h == 0 else [pltpu.roll(own_wide[...], LANES - 4 * X * h, axis=1)]
        parts.append(pltpu.roll(own_wide[...], LANES - 4 * X * h - 2 * X, axis=1))
        by_cell = jnp.concatenate(parts, axis=0).T
        for s in range(STEPS):
            own_absorb[s, :, pl.ds(LANES * h, LANES)] = by_cell[X * s : X * s + X]
    for h in range(HALVES):
        whole = [
            coefficients(own_absorb.at[0], h, None, None, own_unit.at[h]),
            coefficients(own_absorb.at[1], h, own_inverse.at[h], own_ratio.at[h], None),
        ]
        weights(own_inverse.at[h], own_ratio.at[h], own_weight.at[h])
        by_line = jnp.concatenate(whole, axis=0).T
        for i in range(2):
            own_factor[pl.ds(2 * h + i, M, stride=4), :] = by_line[M * i : M * i + M]

    lane = lax.broadcasted_iota(jnp.int32, (OWN, LANES), 1)
    upward = lax.rem(lane, M) < HALF
    ones, zeros = jnp.ones((OWN, LANES), F32), jnp.zeros((OWN, LANES), F32)

    def placed(ref, k):
        return jnp.where(upward, ref[OWN * k : OWN * k + OWN], ref[OWN * (CYCLE - 1 - k) : OWN * (CYCLE - k)])

    whole_unit = ones
    for k in range(CYCLE):
        prefix_unit[OWN * k : OWN * k + OWN] = whole_unit
        whole_unit = whole_unit * placed(own_factor, k)
    closing = 1.0 - whole_unit

    def solve(s, outflow):
        whole_free = zeros
        for k in range(CYCLE):
            prefix_free[OWN * k : OWN * k + OWN] = whole_free
            whole_free = placed(own_factor, k) * whole_free + outflow(k)
        entry = whole_free / closing
        for p in range(CYCLE):
            send_flow[s, OWN * p : OWN * p + OWN] = placed(prefix_unit, p) * entry + placed(prefix_free, p)
        for p in far_places():
            remote(
                send_flow.at[s, own_rows(p)], recv_flow.at[s, own_rows(me)], flow_send.at[s], flow_recv.at[s], p, col
            )
        recv_flow[s, own_rows(me)] = send_flow[s, own_rows(me)]

    wait_for(recv_out.at[pl.ds(0, ROWS - OWN)], out_recv)
    solve(0, lambda k: placed(recv_out, k))

    for h in range(HALVES):
        rows = [send_flow[0, pl.ds(2 * h + i, M, stride=4), :] for i in range(2)]
        inflow = jnp.concatenate(rows, axis=0).T[:M]

        def extra(i, outflow):
            value = jnp.concatenate([own_unit[h, 2 * i] * inflow, own_unit[h, 2 * i + 1] * inflow], axis=1)
            result = product(left_mid[...], value)
            return outflow + own_weight[h, 2 * i] * result[:, :LANES] + own_weight[h, 2 * i + 1] * result[:, LANES:]

        added = loop(X // 2, extra, jnp.zeros((M, LANES), F32))
        by_line = jnp.concatenate([jnp.zeros((M, LANES), F32), added], axis=0).T
        for i in range(2):
            own_extra[pl.ds(2 * h + i, M, stride=4), :] = by_line[M * i : M * i + M]
    solve(1, lambda k: placed(recv_out, k) + placed(own_extra, k))

    def inflows(s, h):
        return recv_flow[s, pl.ds(LANES * h, LANES)].T[M * s : M * s + M]

    def to_sections(source, target, send_sem, recv_sem):
        for section in far_sections():
            remote(source, target, send_sem, recv_sem, me, section)

    wait_for(recv_flow.at[0, pl.ds(0, ROWS - OWN)], flow_recv.at[0])
    for h in range(HALVES):
        inflow = inflows(0, h)

        def middle(i):
            solved = [free[0, h, 2 * i + j] + unit[0, h, 2 * i + j] * inflow for j in range(2)]
            for j in range(2):
                send_early[pl.ds(X * h + 2 * i + j, 1)] = jnp.sum(
                    solved[j] * comp_ordin[0, h, 2 * i + j], axis=0, keepdims=True
                )
            result = product(left_mid[...], jnp.concatenate(solved, axis=1))
            free[1, h, 2 * i] = result[:, :LANES]
            free[1, h, 2 * i + 1] = result[:, LANES:]

        loop(X // 2, middle)
    for s in range(STEPS):
        send_early[pl.ds(2 * X + 8 * s, 8)] = jnp.broadcast_to(labels[0, s].astype(F32), (8, LANES))
    to_sections(send_early, recv_early.at[col], early_send, early_recv)
    recv_early[col] = send_early[...]
    for h in range(HALVES):
        sweep(1, h)

    wait_for(recv_flow.at[1, pl.ds(0, ROWS - OWN)], flow_recv.at[1])
    for h in range(HALVES):
        inflow = inflows(1, h)

        def last_density(i):
            solved = free[1, h, i] + unit[1, h, i] * inflow
            free[1, h, i] = solved
            send_late[h, pl.ds(i, 1)] = jnp.sum(solved * comp_ordin[1, h, i], axis=0, keepdims=True)

        loop(X, last_density)
        to_sections(send_late.at[h], recv_late.at[h, col], late_send.at[h], late_recv.at[h])
        recv_late[h, col] = send_late[h]
    q_store = [
        pltpu.make_async_copy(q_out.at[h], out_ref.at[:, pl.ds(LANES * h, LANES)], store_sem.at[h])
        for h in range(HALVES)
    ]
    for h in range(HALVES):

        def last(i):
            value = jnp.concatenate([free[1, h, 2 * i], free[1, h, 2 * i + 1]], axis=1)
            result = product(left_out[...], value)
            q_out[h, pl.ds(2 * i, M, stride=X), :] = result[:, :LANES]
            q_out[h, pl.ds(2 * i + 1, M, stride=X), :] = result[:, LANES:]

        loop(X // 2, last)
        q_store[h].start()

    wait_for(recv_early.at[pl.ds(0, SECTIONS - 1)], early_recv)

    def add_densities(carry, terms, s):
        def one(c, carry):
            total_a, total_b = carry
            label = recv_early[c, pl.ds(2 * X + 8 * s, 8)]
            is_a = jnp.concatenate([label, label], axis=0) == 0.0
            term = terms(c)
            return total_a + jnp.where(is_a, term, 0.0), total_b + jnp.where(is_a, 0.0, term)

        return loop(SECTIONS, one, carry)

    none = jnp.zeros((X, LANES), F32)
    early = [add_densities((none, none), lambda c, h=h: recv_early[c, pl.ds(X * h, X)], 0) for h in range(HALVES)]
    for h in range(HALVES):
        wait_for(recv_late.at[h, pl.ds(0, SECTIONS - 1)], late_recv.at[h])
        total_a, total_b = add_densities(early[h], lambda c, h=h: recv_late[h, c], 1)
        dens_ref[0, :, pl.ds(LANES * h, LANES)] = total_a
        dens_ref[1, :, pl.ds(LANES * h, LANES)] = total_b

    wait_for(send_absorb.at[pl.ds(0, CYCLE - 1)], absorb_send)
    wait_for(send_out.at[pl.ds(0, ROWS - OWN)], out_send)
    for s in range(STEPS):
        wait_for(send_flow.at[s, pl.ds(0, ROWS - OWN)], flow_send.at[s])
    wait_for(recv_early.at[pl.ds(0, SECTIONS - 1)], early_send)
    for h in range(HALVES):
        wait_for(recv_late.at[h, pl.ds(0, SECTIONS - 1)], late_send.at[h])
    for copy in q_store:
        copy.wait()


def store(q_ref, dens_ref, q_out, dens_out, sem):
    part = M * X // STORES
    copies = [pltpu.make_async_copy(dens_ref, dens_out, sem.at[STORES])]
    for i in range(STORES):
        rows = pl.ds(part * i, part)
        copies.append(pltpu.make_async_copy(q_ref.at[rows], q_out.at[rows], sem.at[i]))
    for copy in copies:
        copy.start()
    for copy in copies:
        copy.wait()


def body(propagator, complement, labels, absorption, to_ordinates, to_modes, upwind, mode_decay):
    rows, lines = M * X, HALVES * LANES
    dma = pltpu.SemaphoreType.DMA
    anywhere = pl.BlockSpec(memory_space=pl.ANY)
    left = pltpu.VMEM((M, 3 * M), BF16)
    half_cells = pltpu.VMEM((HALVES, X, M, LANES), F32)
    cells = pltpu.VMEM((STEPS, HALVES, X, M, LANES), F32)
    by_line = pltpu.VMEM((ROWS, LANES), F32)
    flows = pltpu.VMEM((STEPS, ROWS, LANES), F32)
    pairs = pltpu.VMEM((CYCLE, 2, LANES), F32)
    scratch = [
        pltpu.VMEM((HALVES, rows, LANES), F32),
        pltpu.VMEM((HALVES, rows, LANES), F32),
        pltpu.VMEM((STEPS, rows, lines), BF16),
        pltpu.SMEM((1, STEPS), jnp.int32),
        pltpu.VMEM((2, X, lines), F32),
        pltpu.VMEM((M, M), F32),
        pltpu.VMEM((M, M), F32),
        pltpu.VMEM((1, M), F32),
        pltpu.VMEM((2, M), F32),
        pltpu.VMEM((M, LANES), F32),
        pltpu.VMEM((STEPS, X, lines), F32),
        left,
        left,
        left,
        pltpu.VMEM((STEPS, M, 2 * M), BF16),
        cells,
        cells,
        cells,
        cells,
        half_cells,
        pltpu.VMEM((STEPS, HALVES, rows, LANES), F32),
        cells,
        by_line,
        pairs,
        pairs,
        pltpu.VMEM((2 * CYCLE, LANES), F32),
        pltpu.VMEM((STEPS, X, lines), F32),
        half_cells,
        half_cells,
        half_cells,
        half_cells,
        by_line,
        by_line,
        by_line,
        by_line,
        by_line,
        by_line,
        flows,
        flows,
        pltpu.VMEM((3 * X, LANES), F32),
        pltpu.VMEM((SECTIONS, 3 * X, LANES), F32),
        pltpu.VMEM((HALVES, X, LANES), F32),
        pltpu.VMEM((HALVES, SECTIONS, X, LANES), F32),
        dma((6,)),
        dma((HALVES,)),
        dma,
        dma,
        dma,
        dma,
        dma,
        dma((STEPS,)),
        dma((STEPS,)),
        dma,
        dma,
        dma((HALVES,)),
        dma((HALVES,)),
        dma((HALVES,)),
    ]
    propagated, density = pl.pallas_call(
        kernel,
        out_shape=(
            jax.ShapeDtypeStruct((rows, lines), F32),
            jax.ShapeDtypeStruct((2, X, lines), F32),
        ),
        in_specs=[anywhere] * 8,
        out_specs=(anywhere, pl.BlockSpec(memory_space=pltpu.VMEM)),
        scratch_shapes=scratch,
        compiler_params=pltpu.CompilerParams(
            collective_id=0, has_side_effects=True, vmem_limit_bytes=48 * 1024 * 1024
        ),
        name="contour_steps",
    )(
        *(
            pltpu.with_memory_space_constraint(operand, pltpu.HBM)
            for operand in (
                propagator.reshape(rows, lines),
                complement.reshape(STEPS, rows, lines),
                labels,
                absorption,
                to_ordinates,
                to_modes,
                upwind.reshape(1, M),
                mode_decay,
            )
        )
    )
    propagated, density = pl.pallas_call(
        store,
        out_shape=(
            jax.ShapeDtypeStruct((rows, lines), F32),
            jax.ShapeDtypeStruct((2, X, lines), F32),
        ),
        in_specs=[anywhere] * 2,
        out_specs=(anywhere, anywhere),
        scratch_shapes=[dma((STORES + 1,))],
        compiler_params=pltpu.CompilerParams(vmem_limit_bytes=1024 * 1024),
        name="store_results",
    )(propagated, density)
    return propagated.reshape(1, M, X, lines), density


def solution(mesh):
    in_specs = (
        P("col", None, "gx", None),
        P("col", None, None, "gx", None),
        P("col", None),
        P(None, "gx", None),
        P(),
        P(),
        P(),
        P(),
    )
    out_specs = (P("col", None, "gx", None), P(None, "gx", None))
    return jax.shard_map(body, mesh=mesh, in_specs=in_specs, out_specs=out_specs, check_vma=False)
```

```python
import jax
import jax.numpy as jnp
from jax import lax
from jax.experimental import pallas as pl
from jax.experimental.pallas import tpu as pltpu
from jax.sharding import PartitionSpec as P

F32, BF16 = jnp.float32, jnp.bfloat16
M = 64
HALF = M // 2
X = 16
LANES = 128
HALVES = 2
STEPS = 2
CYCLE, SECTIONS = 32, 8
OWN = 4
RING_Z, RING_Y, RING_X = 8, 4, 4
FAR_Z, FAR_Y, FAR_X = (4, 3, 5, 2, 6, 1, 7, 0), (2, 1, 3, 0), (2, 1, 3, 0)
STORES = 4


def loop(count, step, carry=None):
    if carry is None:

        def plain(i, none):
            step(i)
            return none

        lax.fori_loop(0, count, plain, 0, unroll=True)
        return None
    return lax.fori_loop(0, count, step, carry, unroll=True)


def column(row):
    wide = jnp.broadcast_to(row, (M, M))
    here = lax.broadcasted_iota(jnp.int32, (M, M), 0) == lax.broadcasted_iota(jnp.int32, (M, M), 1)
    return jnp.sum(jnp.where(here, wide, 0.0), axis=1, keepdims=True)


def split(value):
    high = value.astype(BF16)
    low = (value - high.astype(F32)).astype(BF16)
    return high, low


def left_operand(weights):
    high, low = split(weights)
    return jnp.concatenate([high, high, low], axis=1)


def product(left, value):
    high, low = split(value)
    right = jnp.concatenate([high, low, high], axis=0)
    return jnp.dot(left, right, preferred_element_type=F32)


def wait_for(ref, sem):
    pltpu.make_async_copy(ref, ref, sem).wait()


def kernel(
    prop_ref,
    comp_ref,
    labels_ref,
    absorb_ref,
    ordin_ref,
    modes_ref,
    upwind_ref,
    decay_ref,
    out_ref,
    dens_ref,
    q_in,
    q_out,
    comp,
    labels,
    absorb,
    ordin,
    modes,
    upwind,
    decay,
    rate,
    absorb_now,
    left_in,
    left_mid,
    left_out,
    left_comp,
    inverse,
    ratio,
    unit,
    free,
    weight,
    comp_wide,
    comp_ordin,
    turned,
    send_absorb,
    recv_absorb,
    own_wide,
    own_absorb,
    own_inverse,
    own_ratio,
    own_unit,
    own_weight,
    send_out,
    recv_out,
    own_factor,
    prefix_unit,
    prefix_free,
    own_flow,
    own_extra,
    send_flow,
    recv_flow,
    flow,
    send_early,
    recv_early,
    send_late,
    recv_late,
    load_sem,
    q_sem,
    comp_sem,
    absorb_send,
    absorb_recv,
    out_send,
    out_recv,
    flow_send,
    flow_recv,
    early_send,
    early_recv,
    late_send,
    late_recv,
    store_sem,
):
    me = lax.axis_index("gx")
    col = lax.axis_index("col")
    core = lax.rem(col, 2)
    my_z, my_y, my_x = me // RING_Y, lax.rem(me, RING_Y), col // 2

    def far_places():
        for dz in FAR_Z:
            for dy in FAR_Y:
                if (dz, dy) != (0, 0):
                    yield RING_Y * lax.rem(my_z + dz, RING_Z) + lax.rem(my_y + dy, RING_Y)

    def far_sections():
        for dx in FAR_X:
            for dc in range(2):
                if (dx, dc) != (0, 0):
                    yield 2 * lax.rem(my_x + dx, RING_X) + lax.rem(core + dc, 2)

    barrier = pltpu.get_barrier_semaphore()

    def greet(place, section):
        pl.semaphore_signal(
            barrier, inc=1, device_id={"gx": place, "col": section}, device_id_type=pl.DeviceIdType.MESH
        )

    for place in far_places():
        greet(place, col)
    for section in far_sections():
        greet(me, section)

    small = [
        pltpu.make_async_copy(src, dst, load_sem.at[i])
        for i, (src, dst) in enumerate(
            (
                (absorb_ref, absorb),
                (upwind_ref, upwind),
                (labels_ref, labels),
                (ordin_ref, ordin),
                (modes_ref, modes),
                (decay_ref, decay),
            )
        )
    ]
    for copy in small:
        copy.start()
    q_load = [
        pltpu.make_async_copy(prop_ref.at[:, pl.ds(LANES * h, LANES)], q_in.at[h], q_sem.at[h])
        for h in range(HALVES)
    ]
    for copy in q_load:
        copy.start()
    comp_load = pltpu.make_async_copy(comp_ref, comp, comp_sem)
    comp_load.start()
    for copy in small:
        copy.wait()

    rate[...] = jnp.broadcast_to(column(upwind[...]), (M, LANES))
    first = [labels[0, s] == 0 for s in range(STEPS)]
    for s in range(STEPS):
        absorb_now[s] = jnp.where(first[s], absorb[0], absorb[1])
    left_in[...] = left_operand(ordin[...])

    def coefficients(rows, h, inverse, ratio, unit):
        def one(i, carry):
            up, down = carry
            lanes = pl.ds(LANES * h, LANES)
            j = X - 1 - i
            rate_up, rate_down = rate[:HALF], rate[HALF:]
            inverse_up = 1.0 / (1.0 + rate_up + rows[pl.ds(i, 1), lanes])
            inverse_down = 1.0 / (1.0 + rate_down + rows[pl.ds(j, 1), lanes])
            ratio_up = rate_up * inverse_up
            ratio_down = rate_down * inverse_down
            up = up * ratio_up
            down = down * ratio_down
            if inverse is not None:
                inverse[i, :HALF] = inverse_up
                inverse[j, HALF:] = inverse_down
                ratio[i, :HALF] = ratio_up
                ratio[j, HALF:] = ratio_down
            if unit is not None:
                unit[i, :HALF] = up
                unit[j, HALF:] = down
            return up, down

        ones = jnp.ones((HALF, LANES), F32)
        return jnp.concatenate(loop(X, one, (ones, ones)), axis=0)

    def weights(inverse, ratio, weight):
        def one(i, carry):
            up, down = carry
            j = X - 1 - i
            weight[j, :HALF] = inverse[j, :HALF] * up
            weight[i, HALF:] = inverse[i, HALF:] * down
            return up * ratio[j, :HALF], down * ratio[i, HALF:]

        ones = jnp.ones((HALF, LANES), F32)
        loop(X, one, (ones, ones))

    def sweep(s, h):
        def one(i, carry):
            up, down = carry
            j = X - 1 - i
            up = free[s, h, i, :HALF] * inverse[s, h, i, :HALF] + ratio[s, h, i, :HALF] * up
            down = free[s, h, j, HALF:] * inverse[s, h, j, HALF:] + ratio[s, h, j, HALF:] * down
            free[s, h, i, :HALF] = up
            free[s, h, j, HALF:] = down
            return up, down

        zeros = jnp.zeros((HALF, LANES), F32)
        return jnp.concatenate(loop(X, one, (zeros, zeros)), axis=0)

    wide = jnp.concatenate([absorb_now[0], absorb_now[1], jnp.zeros((LANES - 2 * X, 2 * LANES), F32)], axis=0)
    turned[...] = wide.T
    for h in range(HALVES):
        packed = turned[pl.ds(LANES * h, CYCLE, stride=OWN), :]
        for r in range(1, OWN):
            packed = packed + pltpu.roll(turned[pl.ds(LANES * h + r, CYCLE, stride=OWN), :], 2 * X * r, axis=1)
        for o in range(CYCLE):
            send_absorb[o, h : h + 1] = packed[o : o + 1]

    for h in range(HALVES):
        for s in range(STEPS):
            coefficients(absorb_now.at[s], h, inverse.at[s, h], ratio.at[s, h], unit.at[s, h])
        weights(inverse.at[1, h], ratio.at[1, h], weight.at[h])
    gained = []
    for s in range(STEPS):
        gain = jnp.where(first[s], decay[0:1], decay[1:2])
        gained.append(column(gain) * modes[...])
        left_comp[s] = jnp.concatenate(split(gained[s].T), axis=1)
    left_mid[...] = left_operand(
        jnp.dot(ordin[...], gained[0], preferred_element_type=F32, precision=lax.Precision.HIGHEST)
    )
    left_out[...] = left_operand(gained[1])
    outflows = [[], []]
    for h in range(HALVES):
        q_load[h].wait()

        def sources(i):
            value = jnp.concatenate(
                [q_in[h, pl.ds(2 * i, M, stride=X), :], q_in[h, pl.ds(2 * i + 1, M, stride=X), :]], axis=1
            )
            result = product(left_in[...], value)
            free[0, h, 2 * i] = result[:, :LANES]
            free[0, h, 2 * i + 1] = result[:, LANES:]

        loop(X // 2, sources)
        outflows[0].append(sweep(0, h))

        def sources_free(i, outflow):
            value = jnp.concatenate([free[0, h, 2 * i], free[0, h, 2 * i + 1]], axis=1)
            result = product(left_mid[...], value)
            return outflow + weight[h, 2 * i] * result[:, :LANES] + weight[h, 2 * i + 1] * result[:, LANES:]

        outflows[1].append(loop(X // 2, sources_free, jnp.zeros((M, LANES), F32)))
    for s in range(STEPS):
        by_line = jnp.concatenate(outflows[s], axis=0).T
        for o in range(CYCLE):
            send_out[s, o] = by_line[OWN * o : OWN * o + OWN]

    def remote(source, target, send_sem, recv_sem, place, section):
        pltpu.make_async_remote_copy(
            src_ref=source,
            dst_ref=target,
            send_sem=send_sem,
            recv_sem=recv_sem,
            device_id={"gx": place, "col": section},
            device_id_type=pl.DeviceIdType.MESH,
        ).start()

    pl.semaphore_wait(barrier, CYCLE + SECTIONS - 2)
    for p in far_places():
        remote(send_absorb.at[p], recv_absorb.at[me], absorb_send, absorb_recv, p, col)
    for p in far_places():
        remote(send_out.at[0, p], recv_out.at[0, me], out_send.at[0], out_recv.at[0], p, col)
    for p in far_places():
        remote(send_out.at[1, p], recv_out.at[1, me], out_send.at[1], out_recv.at[1], p, col)
    recv_absorb[me] = send_absorb[me]
    for s in range(STEPS):
        recv_out[s, me] = send_out[s, me]

    comp_load.wait()
    for s in range(STEPS):
        for h in range(HALVES):

            def widen(i):
                rows = pl.ds(8 * X * i, 8 * X)
                comp_wide[s, h, rows] = comp[s, rows, pl.ds(LANES * h, LANES)].astype(F32)

            loop(M // 8, widen)

            def to_ordinates(i):
                value = jnp.concatenate(
                    [
                        comp_wide[s, h, pl.ds(2 * i, M, stride=X), :],
                        comp_wide[s, h, pl.ds(2 * i + 1, M, stride=X), :],
                    ],
                    axis=1,
                ).astype(BF16)
                result = jnp.dot(left_comp[s], jnp.concatenate([value, value], axis=0), preferred_element_type=F32)
                comp_ordin[s, h, 2 * i] = result[:, :LANES]
                comp_ordin[s, h, 2 * i + 1] = result[:, LANES:]

            loop(X // 2, to_ordinates)

    wait_for(recv_absorb.at[pl.ds(0, CYCLE - 1)], absorb_recv)
    for h in range(HALVES):
        for p in range(CYCLE):
            own_wide[p : p + 1] = recv_absorb[p, h : h + 1]
        for r in range(OWN):
            part = own_wide[...]
            if r:
                part = pltpu.roll(part, LANES - 2 * X * r, axis=1)
            turned[pl.ds(LANES * h + r, CYCLE, stride=OWN), :] = part
        by_cell = turned[pl.ds(LANES * h, LANES)].T
        for s in range(STEPS):
            own_absorb[s, :, pl.ds(LANES * h, LANES)] = by_cell[X * s : X * s + X]
    whole = [[], []]
    for h in range(HALVES):
        whole[0].append(coefficients(own_absorb.at[0], h, None, None, own_unit.at[h]))
        whole[1].append(coefficients(own_absorb.at[1], h, own_inverse.at[h], own_ratio.at[h], None))
        weights(own_inverse.at[h], own_ratio.at[h], own_weight.at[h])
    for s in range(STEPS):
        own_factor[s] = jnp.concatenate(whole[s], axis=0).T

    lane = lax.broadcasted_iota(jnp.int32, (OWN, LANES), 1)
    upward = lax.rem(lane, M) < HALF
    ones, zeros = jnp.ones((OWN, LANES), F32), jnp.zeros((OWN, LANES), F32)

    def placed(slab, k):
        return jnp.where(upward, slab(k), slab(CYCLE - 1 - k))

    def rows_of(ref):
        return lambda k: ref[OWN * k : OWN * k + OWN]

    closing = []
    for s in range(STEPS):
        whole_unit = ones
        for k in range(CYCLE):
            prefix_unit[s, OWN * k : OWN * k + OWN] = whole_unit
            whole_unit = whole_unit * placed(rows_of(own_factor.at[s]), k)
        closing.append(1.0 - whole_unit)

    def solve(s, outflow):
        whole_free = zeros
        for k in range(CYCLE):
            prefix_free[OWN * k : OWN * k + OWN] = whole_free
            whole_free = placed(rows_of(own_factor.at[s]), k) * whole_free + placed(outflow, k)
        entry = whole_free / closing[s]
        for p in range(CYCLE):
            inflow = placed(rows_of(prefix_unit.at[s]), p) * entry + placed(rows_of(prefix_free), p)
            send_flow[s, p] = inflow
            if s == 0:
                own_flow[OWN * p : OWN * p + OWN] = inflow
        for p in far_places():
            remote(send_flow.at[s, p], recv_flow.at[s, me], flow_send.at[s], flow_recv.at[s], p, col)
        recv_flow[s, me] = send_flow[s, me]

    wait_for(recv_out.at[0, pl.ds(0, CYCLE - 1)], out_recv.at[0])
    solve(0, lambda p: recv_out[0, p])

    own_inflow = own_flow[...].T
    added = []
    for h in range(HALVES):
        inflow = own_inflow[M * h : M * h + M]

        def extra(i, outflow):
            value = jnp.concatenate([own_unit[h, 2 * i] * inflow, own_unit[h, 2 * i + 1] * inflow], axis=1)
            result = product(left_mid[...], value)
            return outflow + own_weight[h, 2 * i] * result[:, :LANES] + own_weight[h, 2 * i + 1] * result[:, LANES:]

        added.append(loop(X // 2, extra, jnp.zeros((M, LANES), F32)))
    own_extra[...] = jnp.concatenate(added, axis=0).T
    wait_for(recv_out.at[1, pl.ds(0, CYCLE - 1)], out_recv.at[1])
    solve(1, lambda p: recv_out[1, p] + rows_of(own_extra)(p))

    def inflows(s):
        wait_for(recv_flow.at[s, pl.ds(0, CYCLE - 1)], flow_recv.at[s])
        for o in range(CYCLE):
            flow[OWN * o : OWN * o + OWN] = recv_flow[s, o]
        both = flow[...].T
        return [both[M * h : M * h + M] for h in range(HALVES)]

    def to_sections(source, target, send_sem, recv_sem):
        for section in far_sections():
            remote(source, target, send_sem, recv_sem, me, section)

    inflow_first = inflows(0)
    for h in range(HALVES):
        inflow = inflow_first[h]

        def middle(i):
            solved = [free[0, h, 2 * i + j] + unit[0, h, 2 * i + j] * inflow for j in range(2)]
            for j in range(2):
                send_early[pl.ds(X * h + 2 * i + j, 1)] = jnp.sum(
                    solved[j] * comp_ordin[0, h, 2 * i + j], axis=0, keepdims=True
                )
            result = product(left_mid[...], jnp.concatenate(solved, axis=1))
            free[1, h, 2 * i] = result[:, :LANES]
            free[1, h, 2 * i + 1] = result[:, LANES:]

        loop(X // 2, middle)
    for s in range(STEPS):
        send_early[pl.ds(2 * X + 8 * s, 8)] = jnp.broadcast_to(labels[0, s].astype(F32), (8, LANES))
    to_sections(send_early, recv_early.at[col], early_send, early_recv)
    recv_early[col] = send_early[...]
    for h in range(HALVES):
        sweep(1, h)

    inflow_second = inflows(1)
    for h in range(HALVES):
        inflow = inflow_second[h]

        def last_density(i):
            solved = free[1, h, i] + unit[1, h, i] * inflow
            free[1, h, i] = solved
            send_late[h, pl.ds(i, 1)] = jnp.sum(solved * comp_ordin[1, h, i], axis=0, keepdims=True)

        loop(X, last_density)
        to_sections(send_late.at[h], recv_late.at[h, col], late_send.at[h], late_recv.at[h])
        recv_late[h, col] = send_late[h]
    q_store = [
        pltpu.make_async_copy(q_out.at[h], out_ref.at[:, pl.ds(LANES * h, LANES)], store_sem.at[h])
        for h in range(HALVES)
    ]
    for h in range(HALVES):

        def last(i):
            value = jnp.concatenate([free[1, h, 2 * i], free[1, h, 2 * i + 1]], axis=1)
            result = product(left_out[...], value)
            q_out[h, pl.ds(2 * i, M, stride=X), :] = result[:, :LANES]
            q_out[h, pl.ds(2 * i + 1, M, stride=X), :] = result[:, LANES:]

        loop(X // 2, last)
        q_store[h].start()

    wait_for(recv_early.at[pl.ds(0, SECTIONS - 1)], early_recv)

    def add_densities(carry, terms, s):
        def one(c, carry):
            total_a, total_b = carry
            label = recv_early[c, pl.ds(2 * X + 8 * s, 8)]
            is_a = jnp.concatenate([label, label], axis=0) == 0.0
            term = terms(c)
            return total_a + jnp.where(is_a, term, 0.0), total_b + jnp.where(is_a, 0.0, term)

        return loop(SECTIONS, one, carry)

    none = jnp.zeros((X, LANES), F32)
    early = [add_densities((none, none), lambda c, h=h: recv_early[c, pl.ds(X * h, X)], 0) for h in range(HALVES)]
    for h in range(HALVES):
        wait_for(recv_late.at[h, pl.ds(0, SECTIONS - 1)], late_recv.at[h])
        total_a, total_b = add_densities(early[h], lambda c, h=h: recv_late[h, c], 1)
        dens_ref[0, :, pl.ds(LANES * h, LANES)] = total_a
        dens_ref[1, :, pl.ds(LANES * h, LANES)] = total_b

    wait_for(send_absorb.at[pl.ds(0, CYCLE - 1)], absorb_send)
    for s in range(STEPS):
        wait_for(send_out.at[s, pl.ds(0, CYCLE - 1)], out_send.at[s])
        wait_for(send_flow.at[s, pl.ds(0, CYCLE - 1)], flow_send.at[s])
    wait_for(recv_early.at[pl.ds(0, SECTIONS - 1)], early_send)
    for h in range(HALVES):
        wait_for(recv_late.at[h, pl.ds(0, SECTIONS - 1)], late_send.at[h])
    for copy in q_store:
        copy.wait()


def store(q_ref, dens_ref, q_out, dens_out, sem):
    part = M * X // STORES
    copies = [pltpu.make_async_copy(dens_ref, dens_out, sem.at[STORES])]
    for i in range(STORES):
        rows = pl.ds(part * i, part)
        copies.append(pltpu.make_async_copy(q_ref.at[rows], q_out.at[rows], sem.at[i]))
    for copy in copies:
        copy.start()
    for copy in copies:
        copy.wait()


def body(propagator, complement, labels, absorption, to_ordinates, to_modes, upwind, mode_decay):
    rows, lines = M * X, HALVES * LANES
    dma = pltpu.SemaphoreType.DMA
    anywhere = pl.BlockSpec(memory_space=pl.ANY)
    left = pltpu.VMEM((M, 3 * M), BF16)
    half_cells = pltpu.VMEM((HALVES, X, M, LANES), F32)
    cells = pltpu.VMEM((STEPS, HALVES, X, M, LANES), F32)
    by_line = pltpu.VMEM((LANES, LANES), F32)
    both_by_line = pltpu.VMEM((STEPS, LANES, LANES), F32)
    flows = pltpu.VMEM((STEPS, CYCLE, OWN, LANES), F32)
    pairs = pltpu.VMEM((CYCLE, 2, LANES), F32)
    scratch = [
        pltpu.VMEM((HALVES, rows, LANES), F32),
        pltpu.VMEM((HALVES, rows, LANES), F32),
        pltpu.VMEM((STEPS, rows, lines), BF16),
        pltpu.SMEM((1, STEPS), jnp.int32),
        pltpu.VMEM((2, X, lines), F32),
        pltpu.VMEM((M, M), F32),
        pltpu.VMEM((M, M), F32),
        pltpu.VMEM((1, M), F32),
        pltpu.VMEM((2, M), F32),
        pltpu.VMEM((M, LANES), F32),
        pltpu.VMEM((STEPS, X, lines), F32),
        left,
        left,
        left,
        pltpu.VMEM((STEPS, M, 2 * M), BF16),
        cells,
        cells,
        cells,
        cells,
        half_cells,
        pltpu.VMEM((STEPS, HALVES, rows, LANES), F32),
        cells,
        pltpu.VMEM((HALVES * LANES, LANES), F32),
        pairs,
        pairs,
        pltpu.VMEM((CYCLE, LANES), F32),
        pltpu.VMEM((STEPS, X, lines), F32),
        half_cells,
        half_cells,
        half_cells,
        half_cells,
        flows,
        flows,
        both_by_line,
        both_by_line,
        by_line,
        by_line,
        by_line,
        flows,
        flows,
        by_line,
        pltpu.VMEM((3 * X, LANES), F32),
        pltpu.VMEM((SECTIONS, 3 * X, LANES), F32),
        pltpu.VMEM((HALVES, X, LANES), F32),
        pltpu.VMEM((HALVES, SECTIONS, X, LANES), F32),
        dma((6,)),
        dma((HALVES,)),
        dma,
        dma,
        dma,
        dma((STEPS,)),
        dma((STEPS,)),
        dma((STEPS,)),
        dma((STEPS,)),
        dma,
        dma,
        dma((HALVES,)),
        dma((HALVES,)),
        dma((HALVES,)),
    ]
    propagated, density = pl.pallas_call(
        kernel,
        out_shape=(
            jax.ShapeDtypeStruct((rows, lines), F32),
            jax.ShapeDtypeStruct((2, X, lines), F32),
        ),
        in_specs=[anywhere] * 8,
        out_specs=(anywhere, pl.BlockSpec(memory_space=pltpu.VMEM)),
        scratch_shapes=scratch,
        compiler_params=pltpu.CompilerParams(
            collective_id=0, has_side_effects=True, vmem_limit_bytes=48 * 1024 * 1024
        ),
        name="contour_steps",
    )(
        *(
            pltpu.with_memory_space_constraint(operand, pltpu.HBM)
            for operand in (
                propagator.reshape(rows, lines),
                complement.reshape(STEPS, rows, lines),
                labels,
                absorption,
                to_ordinates,
                to_modes,
                upwind.reshape(1, M),
                mode_decay,
            )
        )
    )
    propagated, density = pl.pallas_call(
        store,
        out_shape=(
            jax.ShapeDtypeStruct((rows, lines), F32),
            jax.ShapeDtypeStruct((2, X, lines), F32),
        ),
        in_specs=[anywhere] * 2,
        out_specs=(anywhere, anywhere),
        scratch_shapes=[dma((STORES + 1,))],
        compiler_params=pltpu.CompilerParams(vmem_limit_bytes=1024 * 1024),
        name="store_results",
    )(propagated, density)
    return propagated.reshape(1, M, X, lines), density


def solution(mesh):
    in_specs = (
        P("col", None, "gx", None),
        P("col", None, None, "gx", None),
        P("col", None),
        P(None, "gx", None),
        P(),
        P(),
        P(),
        P(),
    )
    out_specs = (P("col", None, "gx", None), P(None, "gx", None))
    return jax.shard_map(body, mesh=mesh, in_specs=in_specs, out_specs=out_specs, check_vma=False)
```

```python
import jax
import jax.numpy as jnp
from jax import lax
from jax.experimental import pallas as pl
from jax.experimental.pallas import tpu as pltpu
from jax.sharding import PartitionSpec as P

F32, BF16 = jnp.float32, jnp.bfloat16
M = 64
HALF = M // 2
X = 16
LANES = 128
HALVES = 2
STEPS = 2
CYCLE, SECTIONS = 32, 8
OWN = 8
OWNERS = LANES // OWN
BLOCKS = 2
RING_Z, RING_Y, RING_X = 8, 4, 4
FAR_Z, FAR_Y, FAR_X = (4, 3, 5, 2, 6, 1, 7, 0), (2, 1, 3, 0), (2, 1, 3, 0)
STORES = 2


def loop(count, step, carry=None):
    if carry is None:

        def plain(i, none):
            step(i)
            return none

        lax.fori_loop(0, count, plain, 0, unroll=True)
        return None
    return lax.fori_loop(0, count, step, carry, unroll=True)


def column(row):
    wide = jnp.broadcast_to(row, (M, M))
    here = lax.broadcasted_iota(jnp.int32, (M, M), 0) == lax.broadcasted_iota(jnp.int32, (M, M), 1)
    return jnp.sum(jnp.where(here, wide, 0.0), axis=1, keepdims=True)


def split(value):
    high = value.astype(BF16)
    low = (value - high.astype(F32)).astype(BF16)
    return high, low


def left_operand(weights):
    high, low = split(weights)
    return jnp.concatenate([high, high, low], axis=1)


def product(left, value):
    high, low = split(value)
    right = jnp.concatenate([high, low, high], axis=0)
    return jnp.dot(left, right, preferred_element_type=F32)


def wait_for(ref, sem):
    pltpu.make_async_copy(ref, ref, sem).wait()


def kernel(
    prop_ref,
    comp_ref,
    labels_ref,
    absorb_ref,
    ordin_ref,
    modes_ref,
    upwind_ref,
    decay_ref,
    out_ref,
    dens_ref,
    q_in,
    q_out,
    comp,
    labels,
    absorb,
    ordin,
    modes,
    upwind,
    decay,
    rate,
    absorb_now,
    left_in,
    left_mid,
    left_out,
    left_comp,
    mids,
    left_own,
    inverse,
    ratio,
    unit,
    free,
    weight,
    comp_wide,
    comp_ordin,
    turned,
    send_absorb,
    recv_absorb,
    wide_rows,
    own_absorb,
    own_inverse,
    own_ratio,
    own_unit,
    own_weight,
    send_out,
    recv_out,
    own_factor,
    prefix_unit,
    prefix_free,
    own_flow,
    own_extra,
    send_flow,
    recv_flow,
    send_label,
    recv_label,
    send_early,
    recv_early,
    send_late,
    recv_late,
    load_sem,
    q_sem,
    comp_sem,
    absorb_send,
    absorb_recv,
    out_send,
    out_recv,
    flow_send,
    flow_recv,
    label_send,
    label_recv,
    early_send,
    early_recv,
    late_send,
    late_recv,
    store_sem,
):
    me = lax.axis_index("gx")
    col = lax.axis_index("col")
    core = lax.rem(col, 2)
    my_z, my_y, my_x = me // RING_Y, lax.rem(me, RING_Y), col // 2
    is_owner = core == 1
    parity = lax.rem(my_z + my_y, 2)
    owns_here = jnp.logical_and(is_owner, parity == 1)
    owns_other = jnp.logical_and(is_owner, parity == 0)
    my_owner = 2 * my_z + my_y // 2
    owner_col = col - core + 1
    served_col = col - 1 + parity

    def far_places():
        for dz in FAR_Z:
            for dy in FAR_Y:
                yield RING_Y * lax.rem(my_z + dz, RING_Z) + lax.rem(my_y + dy, RING_Y), (dz, dy) == (0, 0)

    def far_owners():
        for dz in FAR_Z:
            for dh in (1, 0):
                z, h = lax.rem(my_z + dz, RING_Z), lax.rem(my_y // 2 + dh, 2)
                yield 2 * z + h, RING_Y * z + 2 * h + lax.rem(z + core, 2), (dz, dh) == (0, 0)

    def far_sections():
        for dx in FAR_X:
            for dc in range(2):
                if (dx, dc) != (0, 0):
                    yield 2 * lax.rem(my_x + dx, RING_X) + lax.rem(core + dc, 2)

    barrier = pltpu.get_barrier_semaphore()

    def greet(place, section):
        pl.semaphore_signal(
            barrier, inc=1, device_id={"gx": place, "col": section}, device_id_type=pl.DeviceIdType.MESH
        )

    @pl.when(owns_here)
    def _():
        for place, here in far_places():
            if not here:
                greet(place, col)

    @pl.when(owns_other)
    def _():
        for place, here in far_places():
            greet(place, served_col)

    @pl.when(jnp.logical_not(owns_here))
    def _():
        for o, place, near in far_owners():
            greet(place, owner_col)

    for section in far_sections():
        greet(me, section)
    greeted = jnp.where(owns_here, CYCLE - 1, jnp.where(owns_other, CYCLE + OWNERS, OWNERS)) + SECTIONS - 1

    small = [
        pltpu.make_async_copy(src, dst, load_sem.at[i])
        for i, (src, dst) in enumerate(
            (
                (absorb_ref, absorb),
                (upwind_ref, upwind),
                (labels_ref, labels),
                (ordin_ref, ordin),
                (modes_ref, modes),
                (decay_ref, decay),
            )
        )
    ]
    for copy in small:
        copy.start()
    q_load = [
        pltpu.make_async_copy(prop_ref.at[:, pl.ds(LANES * h, LANES)], q_in.at[h], q_sem.at[h])
        for h in range(HALVES)
    ]
    for copy in q_load:
        copy.start()
    comp_load = pltpu.make_async_copy(comp_ref, comp, comp_sem)
    comp_load.start()
    for copy in small:
        copy.wait()

    rate[...] = jnp.broadcast_to(column(upwind[...]), (M, LANES))
    first = [labels[0, s] == 0 for s in range(STEPS)]
    for s in range(STEPS):
        absorb_now[s] = jnp.where(first[s], absorb[0], absorb[1])
    left_in[...] = left_operand(ordin[...])

    def coefficients(rows, h, inverse, ratio, unit):
        def one(i, carry):
            up, down = carry
            lanes = pl.ds(LANES * h, LANES)
            j = X - 1 - i
            rate_up, rate_down = rate[:HALF], rate[HALF:]
            inverse_up = 1.0 / (1.0 + rate_up + rows[pl.ds(i, 1), lanes])
            inverse_down = 1.0 / (1.0 + rate_down + rows[pl.ds(j, 1), lanes])
            ratio_up = rate_up * inverse_up
            ratio_down = rate_down * inverse_down
            up = up * ratio_up
            down = down * ratio_down
            if inverse is not None:
                inverse[i, :HALF] = inverse_up
                inverse[j, HALF:] = inverse_down
                ratio[i, :HALF] = ratio_up
                ratio[j, HALF:] = ratio_down
            if unit is not None:
                unit[i, :HALF] = up
                unit[j, HALF:] = down
            return up, down

        ones = jnp.ones((HALF, LANES), F32)
        return jnp.concatenate(loop(X, one, (ones, ones)), axis=0)

    def weights(inverse, ratio, weight):
        def one(i, carry):
            up, down = carry
            j = X - 1 - i
            weight[j, :HALF] = inverse[j, :HALF] * up
            weight[i, HALF:] = inverse[i, HALF:] * down
            return up * ratio[j, :HALF], down * ratio[i, HALF:]

        ones = jnp.ones((HALF, LANES), F32)
        loop(X, one, (ones, ones))

    def sweep(s, h):
        def one(i, carry):
            up, down = carry
            j = X - 1 - i
            up = free[s, h, i, :HALF] * inverse[s, h, i, :HALF] + ratio[s, h, i, :HALF] * up
            down = free[s, h, j, HALF:] * inverse[s, h, j, HALF:] + ratio[s, h, j, HALF:] * down
            free[s, h, i, :HALF] = up
            free[s, h, j, HALF:] = down
            return up, down

        zeros = jnp.zeros((HALF, LANES), F32)
        return jnp.concatenate(loop(X, one, (zeros, zeros)), axis=0)

    wide = jnp.concatenate([absorb_now[0], absorb_now[1], jnp.zeros((LANES - 2 * X, 2 * LANES), F32)], axis=0)
    turned[...] = wide.T
    for h in range(HALVES):
        for j in range(2):
            base = LANES * h + 4 * j
            packed = turned[pl.ds(base, OWNERS, stride=OWN), :]
            for i in range(1, 4):
                packed = packed + pltpu.roll(turned[pl.ds(base + i, OWNERS, stride=OWN), :], 2 * X * i, axis=1)
            wide_rows[pl.ds(2 * h + j, OWNERS, stride=4), :] = packed
    for o in range(OWNERS):
        send_absorb[o] = wide_rows[4 * o : 4 * o + 4]

    for h in range(HALVES):
        for s in range(STEPS):
            coefficients(absorb_now.at[s], h, inverse.at[s, h], ratio.at[s, h], unit.at[s, h])
        weights(inverse.at[1, h], ratio.at[1, h], weight.at[h])
    gained = []
    for s in range(STEPS):
        gain = jnp.where(first[s], decay[0:1], decay[1:2])
        gained.append(column(gain) * modes[...])
        left_comp[s] = jnp.concatenate(split(gained[s].T), axis=1)
    for species in range(2):
        mids[species] = jnp.dot(
            ordin[...],
            column(decay[species : species + 1]) * modes[...],
            preferred_element_type=F32,
            precision=lax.Precision.HIGHEST,
        )
    left_mid[...] = left_operand(jnp.where(first[0], mids[0], mids[1]))
    send_label[...] = jnp.broadcast_to(labels[0, 0].astype(F32), (8, LANES))
    left_out[...] = left_operand(gained[1])
    outflows = [[], []]
    for h in range(HALVES):
        q_load[h].wait()

        def sources(i):
            value = jnp.concatenate(
                [q_in[h, pl.ds(2 * i, M, stride=X), :], q_in[h, pl.ds(2 * i + 1, M, stride=X), :]], axis=1
            )
            result = product(left_in[...], value)
            free[0, h, 2 * i] = result[:, :LANES]
            free[0, h, 2 * i + 1] = result[:, LANES:]

        loop(X // 2, sources)
        outflows[0].append(sweep(0, h))

        def sources_free(i, outflow):
            value = jnp.concatenate([free[0, h, 2 * i], free[0, h, 2 * i + 1]], axis=1)
            result = product(left_mid[...], value)
            return outflow + weight[h, 2 * i] * result[:, :LANES] + weight[h, 2 * i + 1] * result[:, LANES:]

        outflows[1].append(loop(X // 2, sources_free, jnp.zeros((M, LANES), F32)))
    for s in range(STEPS):
        send_out[s] = jnp.concatenate(outflows[s], axis=0).T.reshape(OWNERS, OWN, LANES)

    def remote(source, target, send_sem, recv_sem, place, section):
        pltpu.make_async_remote_copy(
            src_ref=source,
            dst_ref=target,
            send_sem=send_sem,
            recv_sem=recv_sem,
            device_id={"gx": place, "col": section},
            device_id_type=pl.DeviceIdType.MESH,
        ).start()

    def to_owners(source, target, send_sem, recv_sem):
        for o, place, near in far_owners():

            def send(o=o, place=place):
                remote(source.at[o], target.at[me], send_sem, recv_sem, place, owner_col)

            if near:
                pl.when(jnp.logical_not(owns_here))(send)
            else:
                send()

        @pl.when(owns_here)
        def _():
            target[me] = source[my_owner]

    def wait_for_slabs(ref, sem):
        @pl.when(owns_here)
        def _():
            wait_for(ref.at[pl.ds(0, CYCLE - 1)], sem)

        @pl.when(owns_other)
        def _():
            wait_for(ref, sem)

    def wait_for_owners(ref, sem):
        @pl.when(owns_here)
        def _():
            wait_for(ref.at[pl.ds(0, OWNERS - 1)], sem)

        @pl.when(jnp.logical_not(owns_here))
        def _():
            wait_for(ref, sem)

    pl.semaphore_wait(barrier, greeted)
    tells = jnp.logical_and(core == 0, parity == 0)

    @pl.when(tells)
    def _():
        remote(send_label, recv_label, label_send, label_recv, me, owner_col)

    @pl.when(owns_here)
    def _():
        recv_label[...] = send_label[...]

    to_owners(send_absorb, recv_absorb, absorb_send, absorb_recv)
    for s in range(STEPS):
        to_owners(send_out.at[s], recv_out.at[s], out_send.at[s], out_recv.at[s])

    comp_load.wait()
    for s in range(STEPS):
        for h in range(HALVES):

            def widen(i):
                rows = pl.ds(8 * X * i, 8 * X)
                comp_wide[s, h, rows] = comp[s, rows, pl.ds(LANES * h, LANES)].astype(F32)

            loop(M // 8, widen)

            def to_ordinates(i):
                value = jnp.concatenate(
                    [
                        comp_wide[s, h, pl.ds(2 * i, M, stride=X), :],
                        comp_wide[s, h, pl.ds(2 * i + 1, M, stride=X), :],
                    ],
                    axis=1,
                ).astype(BF16)
                result = jnp.dot(left_comp[s], jnp.concatenate([value, value], axis=0), preferred_element_type=F32)
                comp_ordin[s, h, 2 * i] = result[:, :LANES]
                comp_ordin[s, h, 2 * i + 1] = result[:, LANES:]

            loop(X // 2, to_ordinates)

    @pl.when(is_owner)
    def _():
        @pl.when(owns_other)
        def _():
            wait_for(recv_label, label_recv)

        first_own = jnp.broadcast_to(recv_label[0:1, :M], (M, M)) == 0.0
        left_own[...] = left_operand(jnp.where(first_own, mids[0], mids[1]))

        wait_for_slabs(recv_absorb, absorb_recv)
        for p in range(CYCLE):
            wide_rows[4 * p : 4 * p + 4] = recv_absorb[p]
        blocks = [(h, g) for h in range(HALVES) for g in range(BLOCKS)]
        for b, (h, g) in enumerate(blocks):
            for j in range(2):
                part = wide_rows[pl.ds(4 * OWNERS * g + 2 * h + j, OWNERS, stride=4), :]
                for i in range(4):
                    rolled = pltpu.roll(part, LANES - 2 * X * i, axis=1) if i else part
                    turned[pl.ds(LANES * (b % 2) + 4 * j + i, OWNERS, stride=OWN), :] = rolled
            by_cell = turned[pl.ds(LANES * (b % 2), LANES)].T
            for s in range(STEPS):
                own_absorb[s, :, pl.ds(LANES * b, LANES)] = by_cell[X * s : X * s + X]
        whole = [{}, {}]
        for b, block in enumerate(blocks):
            whole[0][block] = coefficients(own_absorb.at[0], b, None, None, own_unit.at[b])
            whole[1][block] = coefficients(own_absorb.at[1], b, own_inverse.at[b], own_ratio.at[b], None)
            weights(own_inverse.at[b], own_ratio.at[b], own_weight.at[b])
        for s in range(STEPS):
            for g in range(BLOCKS):
                own_factor[s, pl.ds(LANES * g, LANES)] = jnp.concatenate(
                    [whole[s][h, g] for h in range(HALVES)], axis=0
                ).T

        lane = lax.broadcasted_iota(jnp.int32, (OWN, LANES), 1)
        upward = lax.rem(lane, M) < HALF
        ones, zeros = jnp.ones((OWN, LANES), F32), jnp.zeros((OWN, LANES), F32)

        def placed(slab, k):
            return jnp.where(upward, slab(k), slab(CYCLE - 1 - k))

        def rows_of(ref):
            return lambda k: ref[OWN * k : OWN * k + OWN]

        closing = []
        for s in range(STEPS):
            whole_unit = ones
            for k in range(CYCLE):
                prefix_unit[s, OWN * k : OWN * k + OWN] = whole_unit
                whole_unit = whole_unit * placed(rows_of(own_factor.at[s]), k)
            closing.append(1.0 - whole_unit)

        def solve(s, outflow):
            whole_free = zeros
            for k in range(CYCLE):
                prefix_free[OWN * k : OWN * k + OWN] = whole_free
                whole_free = placed(rows_of(own_factor.at[s]), k) * whole_free + placed(outflow, k)
            entry = whole_free / closing[s]
            for p in range(CYCLE):
                inflow = placed(rows_of(prefix_unit.at[s]), p) * entry + placed(rows_of(prefix_free), p)
                send_flow[s, p] = inflow
                if s == 0:
                    own_flow[OWN * p : OWN * p + OWN] = inflow
            for p, here in far_places():

                def send(p=p):
                    remote(
                        send_flow.at[s, p], recv_flow.at[s, my_owner], flow_send.at[s], flow_recv.at[s], p, served_col
                    )

                if here:
                    pl.when(owns_other)(send)
                else:
                    send()

            @pl.when(owns_here)
            def _():
                recv_flow[s, my_owner] = send_flow[s, me]

        wait_for_slabs(recv_out.at[0], out_recv.at[0])
        solve(0, lambda p: recv_out[0, p])

        added = {}
        for g in range(BLOCKS):
            own_inflow = own_flow[pl.ds(LANES * g, LANES)].T
            for h in range(HALVES):
                b = BLOCKS * h + g
                inflow = own_inflow[M * h : M * h + M]

                def extra(i, outflow):
                    value = jnp.concatenate([own_unit[b, 2 * i] * inflow, own_unit[b, 2 * i + 1] * inflow], axis=1)
                    result = product(left_own[...], value)
                    return (
                        outflow + own_weight[b, 2 * i] * result[:, :LANES] + own_weight[b, 2 * i + 1] * result[:, LANES:]
                    )

                added[h] = loop(X // 2, extra, jnp.zeros((M, LANES), F32))
            own_extra[pl.ds(LANES * g, LANES)] = jnp.concatenate([added[h] for h in range(HALVES)], axis=0).T
        wait_for_slabs(recv_out.at[1], out_recv.at[1])
        solve(1, lambda p: recv_out[1, p] + rows_of(own_extra)(p))

    def inflows(s):
        wait_for_owners(recv_flow.at[s], flow_recv.at[s])
        both = recv_flow[s].reshape(LANES, LANES).T
        return [both[M * h : M * h + M] for h in range(HALVES)]

    def to_sections(source, target, send_sem, recv_sem):
        for section in far_sections():
            remote(source, target, send_sem, recv_sem, me, section)

    inflow_first = inflows(0)
    for h in range(HALVES):
        inflow = inflow_first[h]

        def middle(i):
            solved = [free[0, h, 2 * i + j] + unit[0, h, 2 * i + j] * inflow for j in range(2)]
            for j in range(2):
                send_early[pl.ds(X * h + 2 * i + j, 1)] = jnp.sum(
                    solved[j] * comp_ordin[0, h, 2 * i + j], axis=0, keepdims=True
                )
            result = product(left_mid[...], jnp.concatenate(solved, axis=1))
            free[1, h, 2 * i] = result[:, :LANES]
            free[1, h, 2 * i + 1] = result[:, LANES:]

        loop(X // 2, middle)
    for s in range(STEPS):
        send_early[pl.ds(2 * X + 8 * s, 8)] = jnp.broadcast_to(labels[0, s].astype(F32), (8, LANES))
    to_sections(send_early, recv_early.at[col], early_send, early_recv)
    recv_early[col] = send_early[...]
    for h in range(HALVES):
        sweep(1, h)

    inflow_second = inflows(1)
    for h in range(HALVES):
        inflow = inflow_second[h]

        def last_density(i):
            solved = free[1, h, i] + unit[1, h, i] * inflow
            free[1, h, i] = solved
            send_late[h, pl.ds(i, 1)] = jnp.sum(solved * comp_ordin[1, h, i], axis=0, keepdims=True)

        loop(X, last_density)
        to_sections(send_late.at[h], recv_late.at[h, col], late_send.at[h], late_recv.at[h])
        recv_late[h, col] = send_late[h]
    q_store = [
        pltpu.make_async_copy(q_out.at[h], out_ref.at[:, pl.ds(LANES * h, LANES)], store_sem.at[h])
        for h in range(HALVES)
    ]
    for h in range(HALVES):

        def last(i):
            value = jnp.concatenate([free[1, h, 2 * i], free[1, h, 2 * i + 1]], axis=1)
            result = product(left_out[...], value)
            q_out[h, pl.ds(2 * i, M, stride=X), :] = result[:, :LANES]
            q_out[h, pl.ds(2 * i + 1, M, stride=X), :] = result[:, LANES:]

        loop(X // 2, last)
        q_store[h].start()

    wait_for(recv_early.at[pl.ds(0, SECTIONS - 1)], early_recv)

    def add_densities(carry, terms, s):
        def one(c, carry):
            total_a, total_b = carry
            label = recv_early[c, pl.ds(2 * X + 8 * s, 8)]
            is_a = jnp.concatenate([label, label], axis=0) == 0.0
            term = terms(c)
            return total_a + jnp.where(is_a, term, 0.0), total_b + jnp.where(is_a, 0.0, term)

        return loop(SECTIONS, one, carry)

    none = jnp.zeros((X, LANES), F32)
    early = [add_densities((none, none), lambda c, h=h: recv_early[c, pl.ds(X * h, X)], 0) for h in range(HALVES)]
    for h in range(HALVES):
        wait_for(recv_late.at[h, pl.ds(0, SECTIONS - 1)], late_recv.at[h])
        total_a, total_b = add_densities(early[h], lambda c, h=h: recv_late[h, c], 1)
        dens_ref[0, :, pl.ds(LANES * h, LANES)] = total_a
        dens_ref[1, :, pl.ds(LANES * h, LANES)] = total_b

    @pl.when(tells)
    def _():
        wait_for(send_label, label_send)

    wait_for_owners(send_absorb, absorb_send)
    for s in range(STEPS):
        wait_for_owners(send_out.at[s], out_send.at[s])
        wait_for_slabs(send_flow.at[s], flow_send.at[s])
    wait_for(recv_early.at[pl.ds(0, SECTIONS - 1)], early_send)
    for h in range(HALVES):
        wait_for(recv_late.at[h, pl.ds(0, SECTIONS - 1)], late_send.at[h])
    for copy in q_store:
        copy.wait()


def store(q_ref, dens_ref, q_out, dens_out, sem):
    part = M * X // STORES
    copies = [pltpu.make_async_copy(dens_ref, dens_out, sem.at[STORES])]
    for i in range(STORES):
        rows = pl.ds(part * i, part)
        copies.append(pltpu.make_async_copy(q_ref.at[rows], q_out.at[rows], sem.at[i]))
    for copy in copies:
        copy.start()
    for copy in copies:
        copy.wait()


def body(propagator, complement, labels, absorption, to_ordinates, to_modes, upwind, mode_decay):
    rows, lines = M * X, HALVES * LANES
    dma = pltpu.SemaphoreType.DMA
    anywhere = pl.BlockSpec(memory_space=pl.ANY)
    left = pltpu.VMEM((M, 3 * M), BF16)
    half_cells = pltpu.VMEM((HALVES, X, M, LANES), F32)
    cells = pltpu.VMEM((STEPS, HALVES, X, M, LANES), F32)
    own_cells = pltpu.VMEM((HALVES * BLOCKS, X, M, LANES), F32)
    by_line = pltpu.VMEM((CYCLE * OWN, LANES), F32)
    both_by_line = pltpu.VMEM((STEPS, CYCLE * OWN, LANES), F32)
    by_owner = pltpu.VMEM((STEPS, OWNERS, OWN, LANES), F32)
    by_slab = pltpu.VMEM((STEPS, CYCLE, OWN, LANES), F32)
    scratch = [
        pltpu.VMEM((HALVES, rows, LANES), F32),
        pltpu.VMEM((HALVES, rows, LANES), F32),
        pltpu.VMEM((STEPS, rows, lines), BF16),
        pltpu.SMEM((1, STEPS), jnp.int32),
        pltpu.VMEM((2, X, lines), F32),
        pltpu.VMEM((M, M), F32),
        pltpu.VMEM((M, M), F32),
        pltpu.VMEM((1, M), F32),
        pltpu.VMEM((2, M), F32),
        pltpu.VMEM((M, LANES), F32),
        pltpu.VMEM((STEPS, X, lines), F32),
        left,
        left,
        left,
        pltpu.VMEM((STEPS, M, 2 * M), BF16),
        pltpu.VMEM((2, M, M), F32),
        left,
        cells,
        cells,
        cells,
        cells,
        half_cells,
        pltpu.VMEM((STEPS, HALVES, rows, LANES), F32),
        cells,
        pltpu.VMEM((HALVES * LANES, LANES), F32),
        pltpu.VMEM((OWNERS, 4, LANES), F32),
        pltpu.VMEM((CYCLE, 4, LANES), F32),
        pltpu.VMEM((4 * CYCLE, LANES), F32),
        pltpu.VMEM((STEPS, X, BLOCKS * lines), F32),
        own_cells,
        own_cells,
        own_cells,
        own_cells,
        by_owner,
        by_slab,
        both_by_line,
        both_by_line,
        by_line,
        by_line,
        by_line,
        by_slab,
        by_owner,
        pltpu.VMEM((8, LANES), F32),
        pltpu.VMEM((8, LANES), F32),
        pltpu.VMEM((3 * X, LANES), F32),
        pltpu.VMEM((SECTIONS, 3 * X, LANES), F32),
        pltpu.VMEM((HALVES, X, LANES), F32),
        pltpu.VMEM((HALVES, SECTIONS, X, LANES), F32),
        dma((6,)),
        dma((HALVES,)),
        dma,
        dma,
        dma,
        dma((STEPS,)),
        dma((STEPS,)),
        dma((STEPS,)),
        dma((STEPS,)),
        dma,
        dma,
        dma,
        dma,
        dma((HALVES,)),
        dma((HALVES,)),
        dma((HALVES,)),
    ]
    propagated, density = pl.pallas_call(
        kernel,
        out_shape=(
            jax.ShapeDtypeStruct((rows, lines), F32),
            jax.ShapeDtypeStruct((2, X, lines), F32),
        ),
        in_specs=[anywhere] * 8,
        out_specs=(anywhere, pl.BlockSpec(memory_space=pltpu.VMEM)),
        scratch_shapes=scratch,
        compiler_params=pltpu.CompilerParams(
            collective_id=0, has_side_effects=True, vmem_limit_bytes=48 * 1024 * 1024
        ),
        name="contour_steps",
    )(
        *(
            pltpu.with_memory_space_constraint(operand, pltpu.HBM)
            for operand in (
                propagator.reshape(rows, lines),
                complement.reshape(STEPS, rows, lines),
                labels,
                absorption,
                to_ordinates,
                to_modes,
                upwind.reshape(1, M),
                mode_decay,
            )
        )
    )
    propagated, density = pl.pallas_call(
        store,
        out_shape=(
            jax.ShapeDtypeStruct((rows, lines), F32),
            jax.ShapeDtypeStruct((2, X, lines), F32),
        ),
        in_specs=[anywhere] * 2,
        out_specs=(anywhere, anywhere),
        scratch_shapes=[dma((STORES + 1,))],
        compiler_params=pltpu.CompilerParams(vmem_limit_bytes=1024 * 1024),
        name="store_results",
    )(propagated, density)
    return propagated.reshape(1, M, X, lines), density


def solution(mesh):
    in_specs = (
        P("col", None, "gx", None),
        P("col", None, None, "gx", None),
        P("col", None),
        P(None, "gx", None),
        P(),
        P(),
        P(),
        P(),
    )
    out_specs = (P("col", None, "gx", None), P(None, "gx", None))
    return jax.shard_map(body, mesh=mesh, in_specs=in_specs, out_specs=out_specs, check_vma=False)
```

```python
import jax
import jax.numpy as jnp
from jax import lax
from jax.experimental import pallas as pl
from jax.experimental.pallas import tpu as pltpu
from jax.sharding import PartitionSpec as P

F32, BF16 = jnp.float32, jnp.bfloat16
M = 64
HALF = M // 2
X = 16
LANES = 128
HALVES = 2
STEPS = 2
CYCLE, SECTIONS = 32, 8
OWN = 8
OWNERS = LANES // OWN
BLOCKS = 2
RING_Z, RING_Y, RING_X = 8, 4, 4
FAR_Z, FAR_Y, FAR_X = (4, 3, 5, 2, 6, 1, 7, 0), (2, 1, 3, 0), (2, 1, 3, 0)
STORES = 2


def loop(count, step, carry=None):
    if carry is None:

        def plain(i, none):
            step(i)
            return none

        lax.fori_loop(0, count, plain, 0, unroll=True)
        return None
    return lax.fori_loop(0, count, step, carry, unroll=True)


def column(row):
    wide = jnp.broadcast_to(row, (M, M))
    here = lax.broadcasted_iota(jnp.int32, (M, M), 0) == lax.broadcasted_iota(jnp.int32, (M, M), 1)
    return jnp.sum(jnp.where(here, wide, 0.0), axis=1, keepdims=True)


def split(value):
    high = value.astype(BF16)
    low = (value - high.astype(F32)).astype(BF16)
    return high, low


def left_operand(weights):
    high, low = split(weights)
    return jnp.concatenate([high, high, low], axis=1)


def product(left, value):
    high, low = split(value)
    right = jnp.concatenate([high, low, high], axis=0)
    return jnp.dot(left, right, preferred_element_type=F32)


def wait_for(ref, sem):
    pltpu.make_async_copy(ref, ref, sem).wait()


def kernel(
    prop_ref,
    comp_ref,
    labels_ref,
    absorb_ref,
    ordin_ref,
    modes_ref,
    upwind_ref,
    decay_ref,
    out_ref,
    dens_ref,
    q_in,
    q_out,
    comp,
    labels,
    absorb,
    ordin,
    modes,
    upwind,
    decay,
    rate,
    absorb_now,
    left_in,
    left_mid,
    left_out,
    left_comp,
    mids,
    left_own,
    inverse,
    ratio,
    unit,
    free,
    weight,
    comp_wide,
    comp_ordin,
    turned,
    send_absorb,
    recv_absorb,
    wide_rows,
    own_absorb,
    own_inverse,
    own_ratio,
    own_unit,
    own_weight,
    send_out,
    recv_out,
    own_factor,
    prefix_unit,
    prefix_free,
    own_flow,
    own_extra,
    send_flow,
    recv_flow,
    send_label,
    recv_label,
    send_early,
    recv_early,
    send_late,
    recv_late,
    load_sem,
    q_sem,
    comp_sem,
    absorb_send,
    absorb_recv,
    out_send,
    out_recv,
    flow_send,
    flow_recv,
    label_send,
    label_recv,
    early_send,
    early_recv,
    late_send,
    late_recv,
    store_sem,
):
    me = lax.axis_index("gx")
    col = lax.axis_index("col")
    core = lax.rem(col, 2)
    my_z, my_y, my_x = me // RING_Y, lax.rem(me, RING_Y), col // 2
    is_owner = core == 1
    parity = lax.rem(my_z + my_y, 2)
    owns_here = jnp.logical_and(is_owner, parity == 1)
    owns_other = jnp.logical_and(is_owner, parity == 0)
    my_owner = 2 * my_z + my_y // 2
    owner_col = col - core + 1
    served_col = col - 1 + parity

    def far_places():
        for dz in FAR_Z:
            for dy in FAR_Y:
                yield RING_Y * lax.rem(my_z + dz, RING_Z) + lax.rem(my_y + dy, RING_Y), (dz, dy) == (0, 0)

    def far_owners():
        for dz in FAR_Z:
            for dh in (1, 0):
                z, h = lax.rem(my_z + dz, RING_Z), lax.rem(my_y // 2 + dh, 2)
                yield 2 * z + h, RING_Y * z + 2 * h + lax.rem(z + core, 2), (dz, dh) == (0, 0)

    def far_sections():
        for dx in FAR_X:
            for dc in range(2):
                if (dx, dc) != (0, 0):
                    yield 2 * lax.rem(my_x + dx, RING_X) + lax.rem(core + dc, 2)

    barrier = pltpu.get_barrier_semaphore()

    def greet(place, section):
        pl.semaphore_signal(
            barrier, inc=1, device_id={"gx": place, "col": section}, device_id_type=pl.DeviceIdType.MESH
        )

    @pl.when(owns_here)
    def _():
        for place, here in far_places():
            if not here:
                greet(place, col)

    @pl.when(owns_other)
    def _():
        for place, here in far_places():
            greet(place, served_col)

    @pl.when(jnp.logical_not(owns_here))
    def _():
        for o, place, near in far_owners():
            greet(place, owner_col)

    for section in far_sections():
        greet(me, section)
    greeted = jnp.where(owns_here, CYCLE - 1, jnp.where(owns_other, CYCLE + OWNERS, OWNERS)) + SECTIONS - 1

    small = [
        pltpu.make_async_copy(src, dst, load_sem.at[i])
        for i, (src, dst) in enumerate(
            (
                (absorb_ref, absorb),
                (upwind_ref, upwind),
                (labels_ref, labels),
                (ordin_ref, ordin),
                (modes_ref, modes),
                (decay_ref, decay),
            )
        )
    ]
    for copy in small:
        copy.start()
    q_load = [
        pltpu.make_async_copy(prop_ref.at[:, pl.ds(LANES * h, LANES)], q_in.at[h], q_sem.at[h])
        for h in range(HALVES)
    ]
    for copy in q_load:
        copy.start()
    comp_load = pltpu.make_async_copy(comp_ref, comp, comp_sem)
    comp_load.start()
    for copy in small:
        copy.wait()

    rate[...] = jnp.broadcast_to(column(upwind[...]), (M, LANES))
    first = [labels[0, s] == 0 for s in range(STEPS)]
    for s in range(STEPS):
        absorb_now[s] = jnp.where(first[s], absorb[0], absorb[1])
    left_in[...] = left_operand(ordin[...])

    def coefficients(rows, h, inverse, ratio, unit):
        def one(i, carry):
            up, down = carry
            lanes = pl.ds(LANES * h, LANES)
            j = X - 1 - i
            rate_up, rate_down = rate[:HALF], rate[HALF:]
            inverse_up = 1.0 / (1.0 + rate_up + rows[pl.ds(i, 1), lanes])
            inverse_down = 1.0 / (1.0 + rate_down + rows[pl.ds(j, 1), lanes])
            ratio_up = rate_up * inverse_up
            ratio_down = rate_down * inverse_down
            up = up * ratio_up
            down = down * ratio_down
            if inverse is not None:
                inverse[i, :HALF] = inverse_up
                inverse[j, HALF:] = inverse_down
                ratio[i, :HALF] = ratio_up
                ratio[j, HALF:] = ratio_down
            if unit is not None:
                unit[i, :HALF] = up
                unit[j, HALF:] = down
            return up, down

        ones = jnp.ones((HALF, LANES), F32)
        return jnp.concatenate(loop(X, one, (ones, ones)), axis=0)

    def weights(inverse, ratio, weight):
        def one(i, carry):
            up, down = carry
            j = X - 1 - i
            weight[j, :HALF] = inverse[j, :HALF] * up
            weight[i, HALF:] = inverse[i, HALF:] * down
            return up * ratio[j, :HALF], down * ratio[i, HALF:]

        ones = jnp.ones((HALF, LANES), F32)
        loop(X, one, (ones, ones))

    def sweep(s, h):
        def one(i, carry):
            up, down = carry
            j = X - 1 - i
            up = free[s, h, i, :HALF] * inverse[s, h, i, :HALF] + ratio[s, h, i, :HALF] * up
            down = free[s, h, j, HALF:] * inverse[s, h, j, HALF:] + ratio[s, h, j, HALF:] * down
            free[s, h, i, :HALF] = up
            free[s, h, j, HALF:] = down
            return up, down

        zeros = jnp.zeros((HALF, LANES), F32)
        return jnp.concatenate(loop(X, one, (zeros, zeros)), axis=0)

    wide = jnp.concatenate([absorb_now[0], absorb_now[1], jnp.zeros((LANES - 2 * X, 2 * LANES), F32)], axis=0)
    turned[...] = wide.T
    for h in range(HALVES):
        for j in range(2):
            base = LANES * h + 4 * j
            packed = turned[pl.ds(base, OWNERS, stride=OWN), :]
            for i in range(1, 4):
                packed = packed + pltpu.roll(turned[pl.ds(base + i, OWNERS, stride=OWN), :], 2 * X * i, axis=1)
            wide_rows[pl.ds(2 * h + j, OWNERS, stride=4), :] = packed
    for o in range(OWNERS):
        send_absorb[o] = wide_rows[4 * o : 4 * o + 4]

    for h in range(HALVES):
        for s in range(STEPS):
            coefficients(absorb_now.at[s], h, inverse.at[s, h], ratio.at[s, h], unit.at[s, h])
        weights(inverse.at[1, h], ratio.at[1, h], weight.at[h])
    gained = []
    for s in range(STEPS):
        gain = jnp.where(first[s], decay[0:1], decay[1:2])
        gained.append(column(gain) * modes[...])
        left_comp[s] = jnp.concatenate(split(gained[s].T), axis=1)
    for species in range(2):
        mids[species] = jnp.dot(
            ordin[...],
            column(decay[species : species + 1]) * modes[...],
            preferred_element_type=F32,
            precision=lax.Precision.HIGHEST,
        )
    left_mid[...] = left_operand(jnp.where(first[0], mids[0], mids[1]))
    for s in range(STEPS):
        send_label[s : s + 1] = jnp.broadcast_to(labels[0, s].astype(F32), (1, LANES))
    send_label[STEPS:] = jnp.zeros((8 - STEPS, LANES), F32)
    left_out[...] = left_operand(gained[1])
    outflows = [[], []]
    for h in range(HALVES):
        q_load[h].wait()

        def sources(i):
            value = jnp.concatenate(
                [q_in[h, pl.ds(2 * i, M, stride=X), :], q_in[h, pl.ds(2 * i + 1, M, stride=X), :]], axis=1
            )
            result = product(left_in[...], value)
            free[0, h, 2 * i] = result[:, :LANES]
            free[0, h, 2 * i + 1] = result[:, LANES:]

        loop(X // 2, sources)
        outflows[0].append(sweep(0, h))

        def sources_free(i, outflow):
            value = jnp.concatenate([free[0, h, 2 * i], free[0, h, 2 * i + 1]], axis=1)
            result = product(left_mid[...], value)
            return outflow + weight[h, 2 * i] * result[:, :LANES] + weight[h, 2 * i + 1] * result[:, LANES:]

        outflows[1].append(loop(X // 2, sources_free, jnp.zeros((M, LANES), F32)))
    for s in range(STEPS):
        send_out[s] = jnp.concatenate(outflows[s], axis=0).T.reshape(OWNERS, OWN, LANES)

    def remote(source, target, send_sem, recv_sem, place, section):
        pltpu.make_async_remote_copy(
            src_ref=source,
            dst_ref=target,
            send_sem=send_sem,
            recv_sem=recv_sem,
            device_id={"gx": place, "col": section},
            device_id_type=pl.DeviceIdType.MESH,
        ).start()

    def to_owners(source, target, send_sem, recv_sem):
        for o, place, near in far_owners():

            def send(o=o, place=place):
                remote(source.at[o], target.at[me], send_sem, recv_sem, place, owner_col)

            if near:
                pl.when(jnp.logical_not(owns_here))(send)
            else:
                send()

        @pl.when(owns_here)
        def _():
            target[me] = source[my_owner]

    def wait_for_slabs(ref, sem):
        @pl.when(owns_here)
        def _():
            wait_for(ref.at[pl.ds(0, CYCLE - 1)], sem)

        @pl.when(owns_other)
        def _():
            wait_for(ref, sem)

    def wait_for_owners(ref, sem):
        @pl.when(owns_here)
        def _():
            wait_for(ref.at[pl.ds(0, OWNERS - 1)], sem)

        @pl.when(jnp.logical_not(owns_here))
        def _():
            wait_for(ref, sem)

    pl.semaphore_wait(barrier, greeted)
    to_owners(send_absorb, recv_absorb, absorb_send, absorb_recv)
    for s in range(STEPS):
        to_owners(send_out.at[s], recv_out.at[s], out_send.at[s], out_recv.at[s])

    def to_sections(source, target, send_sem, recv_sem):
        for section in far_sections():
            remote(source, target, send_sem, recv_sem, me, section)

    to_sections(send_label, recv_label.at[col], label_send, label_recv)
    recv_label[col] = send_label[...]

    comp_load.wait()
    for s in range(STEPS):
        for h in range(HALVES):

            def widen(i):
                rows = pl.ds(8 * X * i, 8 * X)
                comp_wide[s, h, rows] = comp[s, rows, pl.ds(LANES * h, LANES)].astype(F32)

            loop(M // 8, widen)

            def to_ordinates(i):
                value = jnp.concatenate(
                    [
                        comp_wide[s, h, pl.ds(2 * i, M, stride=X), :],
                        comp_wide[s, h, pl.ds(2 * i + 1, M, stride=X), :],
                    ],
                    axis=1,
                ).astype(BF16)
                result = jnp.dot(left_comp[s], jnp.concatenate([value, value], axis=0), preferred_element_type=F32)
                comp_ordin[s, h, 2 * i] = result[:, :LANES]
                comp_ordin[s, h, 2 * i + 1] = result[:, LANES:]

            loop(X // 2, to_ordinates)

    wait_for(recv_label.at[pl.ds(0, SECTIONS - 1)], label_recv)

    @pl.when(is_owner)
    def _():
        first_own = jnp.broadcast_to(recv_label[served_col, 0:1, :M], (M, M)) == 0.0
        left_own[...] = left_operand(jnp.where(first_own, mids[0], mids[1]))

        wait_for_slabs(recv_absorb, absorb_recv)
        for p in range(CYCLE):
            wide_rows[4 * p : 4 * p + 4] = recv_absorb[p]
        blocks = [(h, g) for h in range(HALVES) for g in range(BLOCKS)]
        for b, (h, g) in enumerate(blocks):
            for j in range(2):
                part = wide_rows[pl.ds(4 * OWNERS * g + 2 * h + j, OWNERS, stride=4), :]
                for i in range(4):
                    rolled = pltpu.roll(part, LANES - 2 * X * i, axis=1) if i else part
                    turned[pl.ds(LANES * (b % 2) + 4 * j + i, OWNERS, stride=OWN), :] = rolled
            by_cell = turned[pl.ds(LANES * (b % 2), LANES)].T
            for s in range(STEPS):
                own_absorb[s, :, pl.ds(LANES * b, LANES)] = by_cell[X * s : X * s + X]
        whole = [{}, {}]
        for b, block in enumerate(blocks):
            whole[0][block] = coefficients(own_absorb.at[0], b, None, None, own_unit.at[b])
            whole[1][block] = coefficients(own_absorb.at[1], b, own_inverse.at[b], own_ratio.at[b], None)
            weights(own_inverse.at[b], own_ratio.at[b], own_weight.at[b])
        for s in range(STEPS):
            for g in range(BLOCKS):
                own_factor[s, pl.ds(LANES * g, LANES)] = jnp.concatenate(
                    [whole[s][h, g] for h in range(HALVES)], axis=0
                ).T

        lane = lax.broadcasted_iota(jnp.int32, (OWN, LANES), 1)
        upward = lax.rem(lane, M) < HALF
        ones, zeros = jnp.ones((OWN, LANES), F32), jnp.zeros((OWN, LANES), F32)

        def placed(slab, k):
            return jnp.where(upward, slab(k), slab(CYCLE - 1 - k))

        def rows_of(ref):
            return lambda k: ref[OWN * k : OWN * k + OWN]

        closing = []
        for s in range(STEPS):
            whole_unit = ones
            for k in range(CYCLE):
                prefix_unit[s, OWN * k : OWN * k + OWN] = whole_unit
                whole_unit = whole_unit * placed(rows_of(own_factor.at[s]), k)
            closing.append(1.0 - whole_unit)

        def solve(s, outflow):
            whole_free = zeros
            for k in range(CYCLE):
                prefix_free[OWN * k : OWN * k + OWN] = whole_free
                whole_free = placed(rows_of(own_factor.at[s]), k) * whole_free + placed(outflow, k)
            entry = whole_free / closing[s]
            for p in range(CYCLE):
                inflow = placed(rows_of(prefix_unit.at[s]), p) * entry + placed(rows_of(prefix_free), p)
                send_flow[s, p] = inflow
                if s == 0:
                    own_flow[OWN * p : OWN * p + OWN] = inflow
            for p, here in far_places():

                def send(p=p):
                    remote(
                        send_flow.at[s, p], recv_flow.at[s, my_owner], flow_send.at[s], flow_recv.at[s], p, served_col
                    )

                if here:
                    pl.when(owns_other)(send)
                else:
                    send()

            @pl.when(owns_here)
            def _():
                recv_flow[s, my_owner] = send_flow[s, me]

        wait_for_slabs(recv_out.at[0], out_recv.at[0])
        solve(0, lambda p: recv_out[0, p])

        added = {}
        for g in range(BLOCKS):
            own_inflow = own_flow[pl.ds(LANES * g, LANES)].T
            for h in range(HALVES):
                b = BLOCKS * h + g
                inflow = own_inflow[M * h : M * h + M]

                def extra(i, outflow):
                    value = jnp.concatenate([own_unit[b, 2 * i] * inflow, own_unit[b, 2 * i + 1] * inflow], axis=1)
                    result = product(left_own[...], value)
                    return (
                        outflow + own_weight[b, 2 * i] * result[:, :LANES] + own_weight[b, 2 * i + 1] * result[:, LANES:]
                    )

                added[h] = loop(X // 2, extra, jnp.zeros((M, LANES), F32))
            own_extra[pl.ds(LANES * g, LANES)] = jnp.concatenate([added[h] for h in range(HALVES)], axis=0).T
        wait_for_slabs(recv_out.at[1], out_recv.at[1])
        solve(1, lambda p: recv_out[1, p] + rows_of(own_extra)(p))

    def inflows(s):
        wait_for_owners(recv_flow.at[s], flow_recv.at[s])
        both = recv_flow[s].reshape(LANES, LANES).T
        return [both[M * h : M * h + M] for h in range(HALVES)]

    inflow_first = inflows(0)
    for h in range(HALVES):
        inflow = inflow_first[h]

        def middle(i):
            solved = [free[0, h, 2 * i + j] + unit[0, h, 2 * i + j] * inflow for j in range(2)]
            for j in range(2):
                send_early[pl.ds(X * h + 2 * i + j, 1)] = jnp.sum(
                    solved[j] * comp_ordin[0, h, 2 * i + j], axis=0, keepdims=True
                )
            result = product(left_mid[...], jnp.concatenate(solved, axis=1))
            free[1, h, 2 * i] = result[:, :LANES]
            free[1, h, 2 * i + 1] = result[:, LANES:]

        loop(X // 2, middle)
    to_sections(send_early, recv_early.at[col], early_send, early_recv)
    recv_early[col] = send_early[...]
    for h in range(HALVES):
        sweep(1, h)

    inflow_second = inflows(1)
    for h in range(HALVES):
        inflow = inflow_second[h]

        def last_density(i):
            solved = free[1, h, i] + unit[1, h, i] * inflow
            free[1, h, i] = solved
            send_late[h, pl.ds(i, 1)] = jnp.sum(solved * comp_ordin[1, h, i], axis=0, keepdims=True)

        loop(X, last_density)
    to_sections(send_late, recv_late.at[col], late_send, late_recv)
    recv_late[col] = send_late[...]
    q_store = [
        pltpu.make_async_copy(q_out.at[h], out_ref.at[:, pl.ds(LANES * h, LANES)], store_sem.at[h])
        for h in range(HALVES)
    ]
    for h in range(HALVES):

        def last(i):
            value = jnp.concatenate([free[1, h, 2 * i], free[1, h, 2 * i + 1]], axis=1)
            result = product(left_out[...], value)
            q_out[h, pl.ds(2 * i, M, stride=X), :] = result[:, :LANES]
            q_out[h, pl.ds(2 * i + 1, M, stride=X), :] = result[:, LANES:]

        loop(X // 2, last)
        q_store[h].start()

    wait_for(recv_early.at[pl.ds(0, SECTIONS - 1)], early_recv)

    def add_densities(carry, terms, s):
        def one(c, carry):
            total_a, total_b = carry
            is_a = jnp.broadcast_to(recv_label[c, s : s + 1], (X, LANES)) == 0.0
            term = terms(c)
            return total_a + jnp.where(is_a, term, 0.0), total_b + jnp.where(is_a, 0.0, term)

        return loop(SECTIONS, one, carry)

    none = jnp.zeros((X, LANES), F32)
    early = [add_densities((none, none), lambda c, h=h: recv_early[c, pl.ds(X * h, X)], 0) for h in range(HALVES)]
    for h in range(HALVES):
        if h == 0:
            wait_for(recv_late.at[pl.ds(0, SECTIONS - 1)], late_recv)
        total_a, total_b = add_densities(early[h], lambda c, h=h: recv_late[c, h], 1)
        dens_ref[0, :, pl.ds(LANES * h, LANES)] = total_a
        dens_ref[1, :, pl.ds(LANES * h, LANES)] = total_b

    wait_for(recv_label.at[pl.ds(0, SECTIONS - 1)], label_send)
    wait_for_owners(send_absorb, absorb_send)
    for s in range(STEPS):
        wait_for_owners(send_out.at[s], out_send.at[s])
        wait_for_slabs(send_flow.at[s], flow_send.at[s])
    wait_for(recv_early.at[pl.ds(0, SECTIONS - 1)], early_send)
    wait_for(recv_late.at[pl.ds(0, SECTIONS - 1)], late_send)
    for copy in q_store:
        copy.wait()


def store(q_ref, dens_ref, q_out, dens_out, sem):
    part = M * X // STORES
    copies = [pltpu.make_async_copy(dens_ref, dens_out, sem.at[STORES])]
    for i in range(STORES):
        rows = pl.ds(part * i, part)
        copies.append(pltpu.make_async_copy(q_ref.at[rows], q_out.at[rows], sem.at[i]))
    for copy in copies:
        copy.start()
    for copy in copies:
        copy.wait()


def body(propagator, complement, labels, absorption, to_ordinates, to_modes, upwind, mode_decay):
    rows, lines = M * X, HALVES * LANES
    dma = pltpu.SemaphoreType.DMA
    anywhere = pl.BlockSpec(memory_space=pl.ANY)
    left = pltpu.VMEM((M, 3 * M), BF16)
    half_cells = pltpu.VMEM((HALVES, X, M, LANES), F32)
    cells = pltpu.VMEM((STEPS, HALVES, X, M, LANES), F32)
    own_cells = pltpu.VMEM((HALVES * BLOCKS, X, M, LANES), F32)
    by_line = pltpu.VMEM((CYCLE * OWN, LANES), F32)
    both_by_line = pltpu.VMEM((STEPS, CYCLE * OWN, LANES), F32)
    by_owner = pltpu.VMEM((STEPS, OWNERS, OWN, LANES), F32)
    by_slab = pltpu.VMEM((STEPS, CYCLE, OWN, LANES), F32)
    scratch = [
        pltpu.VMEM((HALVES, rows, LANES), F32),
        pltpu.VMEM((HALVES, rows, LANES), F32),
        pltpu.VMEM((STEPS, rows, lines), BF16),
        pltpu.SMEM((1, STEPS), jnp.int32),
        pltpu.VMEM((2, X, lines), F32),
        pltpu.VMEM((M, M), F32),
        pltpu.VMEM((M, M), F32),
        pltpu.VMEM((1, M), F32),
        pltpu.VMEM((2, M), F32),
        pltpu.VMEM((M, LANES), F32),
        pltpu.VMEM((STEPS, X, lines), F32),
        left,
        left,
        left,
        pltpu.VMEM((STEPS, M, 2 * M), BF16),
        pltpu.VMEM((2, M, M), F32),
        left,
        cells,
        cells,
        cells,
        cells,
        half_cells,
        pltpu.VMEM((STEPS, HALVES, rows, LANES), F32),
        cells,
        pltpu.VMEM((HALVES * LANES, LANES), F32),
        pltpu.VMEM((OWNERS, 4, LANES), F32),
        pltpu.VMEM((CYCLE, 4, LANES), F32),
        pltpu.VMEM((4 * CYCLE, LANES), F32),
        pltpu.VMEM((STEPS, X, BLOCKS * lines), F32),
        own_cells,
        own_cells,
        own_cells,
        own_cells,
        by_owner,
        by_slab,
        both_by_line,
        both_by_line,
        by_line,
        by_line,
        by_line,
        by_slab,
        by_owner,
        pltpu.VMEM((8, LANES), F32),
        pltpu.VMEM((SECTIONS, 8, LANES), F32),
        pltpu.VMEM((HALVES * X, LANES), F32),
        pltpu.VMEM((SECTIONS, HALVES * X, LANES), F32),
        pltpu.VMEM((HALVES, X, LANES), F32),
        pltpu.VMEM((SECTIONS, HALVES, X, LANES), F32),
        dma((6,)),
        dma((HALVES,)),
        dma,
        dma,
        dma,
        dma((STEPS,)),
        dma((STEPS,)),
        dma((STEPS,)),
        dma((STEPS,)),
        dma,
        dma,
        dma,
        dma,
        dma,
        dma,
        dma((HALVES,)),
    ]
    propagated, density = pl.pallas_call(
        kernel,
        out_shape=(
            jax.ShapeDtypeStruct((rows, lines), F32),
            jax.ShapeDtypeStruct((2, X, lines), F32),
        ),
        in_specs=[anywhere] * 8,
        out_specs=(anywhere, pl.BlockSpec(memory_space=pltpu.VMEM)),
        scratch_shapes=scratch,
        compiler_params=pltpu.CompilerParams(
            collective_id=0, has_side_effects=True, vmem_limit_bytes=48 * 1024 * 1024
        ),
        name="contour_steps",
    )(
        *(
            pltpu.with_memory_space_constraint(operand, pltpu.HBM)
            for operand in (
                propagator.reshape(rows, lines),
                complement.reshape(STEPS, rows, lines),
                labels,
                absorption,
                to_ordinates,
                to_modes,
                upwind.reshape(1, M),
                mode_decay,
            )
        )
    )
    propagated, density = pl.pallas_call(
        store,
        out_shape=(
            jax.ShapeDtypeStruct((rows, lines), F32),
            jax.ShapeDtypeStruct((2, X, lines), F32),
        ),
        in_specs=[anywhere] * 2,
        out_specs=(anywhere, anywhere),
        scratch_shapes=[dma((STORES + 1,))],
        compiler_params=pltpu.CompilerParams(vmem_limit_bytes=1024 * 1024),
        name="store_results",
    )(propagated, density)
    return propagated.reshape(1, M, X, lines), density


def solution(mesh):
    in_specs = (
        P("col", None, "gx", None),
        P("col", None, None, "gx", None),
        P("col", None),
        P(None, "gx", None),
        P(),
        P(),
        P(),
        P(),
    )
    out_specs = (P("col", None, "gx", None), P(None, "gx", None))
    return jax.shard_map(body, mesh=mesh, in_specs=in_specs, out_specs=out_specs, check_vma=False)
```

```python
import jax
import jax.numpy as jnp
from jax import lax
from jax.experimental import pallas as pl
from jax.experimental.pallas import tpu as pltpu
from jax.sharding import PartitionSpec as P

F32, BF16 = jnp.float32, jnp.bfloat16
M = 64
HALF = M // 2
X = 16
LANES = 128
HALVES = 2
STEPS = 2
CYCLE, SECTIONS = 32, 8
OWN = 8
OWNERS = LANES // OWN
BLOCKS = 2
RING_Z, RING_Y, RING_X = 8, 4, 4
FAR_Z, FAR_Y, FAR_X = (4, 3, 5, 2, 6, 1, 7, 0), (2, 1, 3, 0), (2, 1, 3, 0)
STORES = 2


def loop(count, step, carry=None):
    if carry is None:

        def plain(i, none):
            step(i)
            return none

        lax.fori_loop(0, count, plain, 0, unroll=True)
        return None
    return lax.fori_loop(0, count, step, carry, unroll=True)


def column(row):
    wide = jnp.broadcast_to(row, (M, M))
    here = lax.broadcasted_iota(jnp.int32, (M, M), 0) == lax.broadcasted_iota(jnp.int32, (M, M), 1)
    return jnp.sum(jnp.where(here, wide, 0.0), axis=1, keepdims=True)


def split(value):
    high = value.astype(BF16)
    low = (value - high.astype(F32)).astype(BF16)
    return high, low


def left_operand(weights):
    high, low = split(weights)
    return jnp.concatenate([high, high, low], axis=1)


def product(left, value):
    high, low = split(value)
    right = jnp.concatenate([high, low, high], axis=0)
    return jnp.dot(left, right, preferred_element_type=F32)


def wait_for(ref, sem):
    pltpu.make_async_copy(ref, ref, sem).wait()


def kernel(
    prop_ref,
    comp_ref,
    labels_ref,
    absorb_ref,
    ordin_ref,
    modes_ref,
    upwind_ref,
    decay_ref,
    out_ref,
    dens_ref,
    q_in,
    q_out,
    comp,
    labels,
    absorb,
    ordin,
    modes,
    upwind,
    decay,
    rate,
    absorb_now,
    left_in,
    left_mid,
    left_out,
    left_comp,
    mids,
    left_own,
    inverse,
    ratio,
    unit,
    free,
    weight,
    comp_wide,
    comp_ordin,
    turned,
    send_absorb,
    recv_absorb,
    wide_rows,
    own_absorb,
    own_inverse,
    own_ratio,
    own_unit,
    own_weight,
    send_out,
    recv_out,
    own_factor,
    prefix_unit,
    prefix_free,
    own_flow,
    own_extra,
    send_flow,
    recv_flow,
    send_label,
    recv_label,
    send_early,
    recv_early,
    send_late,
    recv_late,
    load_sem,
    q_sem,
    comp_sem,
    absorb_send,
    absorb_recv,
    out_send,
    out_recv,
    flow_send,
    flow_recv,
    label_send,
    label_recv,
    early_send,
    early_recv,
    late_send,
    late_recv,
    store_sem,
):
    me = lax.axis_index("gx")
    col = lax.axis_index("col")
    core = lax.rem(col, 2)
    my_z, my_y, my_x = me // RING_Y, lax.rem(me, RING_Y), col // 2
    is_owner = core == 1
    parity = lax.rem(my_z + my_y, 2)
    owns_here = jnp.logical_and(is_owner, parity == 1)
    owns_other = jnp.logical_and(is_owner, parity == 0)
    my_owner = 2 * my_z + my_y // 2
    owner_col = col - core + 1
    served_col = col - 1 + parity

    def far_places():
        for dz in FAR_Z:
            for dy in FAR_Y:
                yield RING_Y * lax.rem(my_z + dz, RING_Z) + lax.rem(my_y + dy, RING_Y), (dz, dy) == (0, 0)

    def far_owners():
        for dz in FAR_Z:
            for dh in (1, 0):
                z, h = lax.rem(my_z + dz, RING_Z), lax.rem(my_y // 2 + dh, 2)
                yield 2 * z + h, RING_Y * z + 2 * h + lax.rem(z + core, 2), (dz, dh) == (0, 0)

    def far_sections():
        for dx in FAR_X:
            for dc in range(2):
                if (dx, dc) != (0, 0):
                    yield 2 * lax.rem(my_x + dx, RING_X) + lax.rem(core + dc, 2)

    barrier = pltpu.get_barrier_semaphore()

    def greet(place, section):
        pl.semaphore_signal(
            barrier, inc=1, device_id={"gx": place, "col": section}, device_id_type=pl.DeviceIdType.MESH
        )

    @pl.when(owns_here)
    def _():
        for place, here in far_places():
            if not here:
                greet(place, col)

    @pl.when(owns_other)
    def _():
        for place, here in far_places():
            greet(place, served_col)

    @pl.when(jnp.logical_not(owns_here))
    def _():
        for o, place, near in far_owners():
            greet(place, owner_col)

    for section in far_sections():
        greet(me, section)
    greeted = jnp.where(owns_here, CYCLE - 1, jnp.where(owns_other, CYCLE + OWNERS, OWNERS)) + SECTIONS - 1

    small = [
        pltpu.make_async_copy(src, dst, load_sem.at[i])
        for i, (src, dst) in enumerate(
            (
                (absorb_ref, absorb),
                (upwind_ref, upwind),
                (labels_ref, labels),
                (ordin_ref, ordin),
                (modes_ref, modes),
                (decay_ref, decay),
            )
        )
    ]
    for copy in small:
        copy.start()
    q_load = [
        pltpu.make_async_copy(prop_ref.at[:, pl.ds(LANES * h, LANES)], q_in.at[h], q_sem.at[h])
        for h in range(HALVES)
    ]
    for copy in q_load:
        copy.start()
    comp_load = pltpu.make_async_copy(comp_ref, comp, comp_sem)
    comp_load.start()
    for copy in small:
        copy.wait()

    rate[...] = jnp.broadcast_to(column(upwind[...]), (M, LANES))
    first = [labels[0, s] == 0 for s in range(STEPS)]
    for s in range(STEPS):
        absorb_now[s] = jnp.where(first[s], absorb[0], absorb[1])
    left_in[...] = left_operand(ordin[...])

    def coefficients(rows, h, inverse, ratio, unit):
        def one(i, carry):
            up, down = carry
            lanes = pl.ds(LANES * h, LANES)
            j = X - 1 - i
            rate_up, rate_down = rate[:HALF], rate[HALF:]
            inverse_up = 1.0 / (1.0 + rate_up + rows[pl.ds(i, 1), lanes])
            inverse_down = 1.0 / (1.0 + rate_down + rows[pl.ds(j, 1), lanes])
            ratio_up = rate_up * inverse_up
            ratio_down = rate_down * inverse_down
            up = up * ratio_up
            down = down * ratio_down
            if inverse is not None:
                inverse[i, :HALF] = inverse_up
                inverse[j, HALF:] = inverse_down
                ratio[i, :HALF] = ratio_up
                ratio[j, HALF:] = ratio_down
            if unit is not None:
                unit[i, :HALF] = up
                unit[j, HALF:] = down
            return up, down

        ones = jnp.ones((HALF, LANES), F32)
        return jnp.concatenate(loop(X, one, (ones, ones)), axis=0)

    def weights(inverse, ratio, weight):
        def one(i, carry):
            up, down = carry
            j = X - 1 - i
            weight[j, :HALF] = inverse[j, :HALF] * up
            weight[i, HALF:] = inverse[i, HALF:] * down
            return up * ratio[j, :HALF], down * ratio[i, HALF:]

        ones = jnp.ones((HALF, LANES), F32)
        loop(X, one, (ones, ones))

    def sweep(s, h):
        def one(i, carry):
            up, down = carry
            j = X - 1 - i
            up = free[s, h, i, :HALF] * inverse[s, h, i, :HALF] + ratio[s, h, i, :HALF] * up
            down = free[s, h, j, HALF:] * inverse[s, h, j, HALF:] + ratio[s, h, j, HALF:] * down
            free[s, h, i, :HALF] = up
            free[s, h, j, HALF:] = down
            return up, down

        zeros = jnp.zeros((HALF, LANES), F32)
        return jnp.concatenate(loop(X, one, (zeros, zeros)), axis=0)

    wide = jnp.concatenate([absorb_now[0], absorb_now[1], jnp.zeros((LANES - 2 * X, 2 * LANES), F32)], axis=0)
    turned[...] = wide.T
    for h in range(HALVES):
        for j in range(2):
            base = LANES * h + 4 * j
            packed = turned[pl.ds(base, OWNERS, stride=OWN), :]
            for i in range(1, 4):
                packed = packed + pltpu.roll(turned[pl.ds(base + i, OWNERS, stride=OWN), :], 2 * X * i, axis=1)
            wide_rows[pl.ds(2 * h + j, OWNERS, stride=4), :] = packed
    for o in range(OWNERS):
        send_absorb[o] = wide_rows[4 * o : 4 * o + 4]

    for h in range(HALVES):
        for s in range(STEPS):
            coefficients(absorb_now.at[s], h, inverse.at[s, h], ratio.at[s, h], unit.at[s, h])
        weights(inverse.at[1, h], ratio.at[1, h], weight.at[h])
    gained = []
    for s in range(STEPS):
        gain = jnp.where(first[s], decay[0:1], decay[1:2])
        gained.append(column(gain) * modes[...])
        left_comp[s] = jnp.concatenate(split(gained[s].T), axis=1)
    for species in range(2):
        mids[species] = jnp.dot(
            ordin[...],
            column(decay[species : species + 1]) * modes[...],
            preferred_element_type=F32,
            precision=lax.Precision.HIGHEST,
        )
    left_mid[...] = left_operand(jnp.where(first[0], mids[0], mids[1]))
    for s in range(STEPS):
        send_label[s : s + 1] = jnp.broadcast_to(labels[0, s].astype(F32), (1, LANES))
    send_label[STEPS:] = jnp.zeros((8 - STEPS, LANES), F32)
    left_out[...] = left_operand(gained[1])
    outflows = [[], []]
    for h in range(HALVES):
        q_load[h].wait()

        def sources(i):
            value = jnp.concatenate(
                [q_in[h, pl.ds(2 * i, M, stride=X), :], q_in[h, pl.ds(2 * i + 1, M, stride=X), :]], axis=1
            )
            result = product(left_in[...], value)
            free[0, h, 2 * i] = result[:, :LANES]
            free[0, h, 2 * i + 1] = result[:, LANES:]

        loop(X // 2, sources)
        outflows[0].append(sweep(0, h))

        def sources_free(i, outflow):
            value = jnp.concatenate([free[0, h, 2 * i], free[0, h, 2 * i + 1]], axis=1)
            result = product(left_mid[...], value)
            return outflow + weight[h, 2 * i] * result[:, :LANES] + weight[h, 2 * i + 1] * result[:, LANES:]

        outflows[1].append(loop(X // 2, sources_free, jnp.zeros((M, LANES), F32)))
    for s in range(STEPS):
        send_out[s] = jnp.concatenate(outflows[s], axis=0).T.reshape(OWNERS, OWN, LANES)

    def remote(source, target, send_sem, recv_sem, place, section):
        pltpu.make_async_remote_copy(
            src_ref=source,
            dst_ref=target,
            send_sem=send_sem,
            recv_sem=recv_sem,
            device_id={"gx": place, "col": section},
            device_id_type=pl.DeviceIdType.MESH,
        ).start()

    def to_owners(source, target, send_sem, recv_sem):
        for o, place, near in far_owners():

            def send(o=o, place=place):
                remote(source.at[o], target.at[me], send_sem, recv_sem, place, owner_col)

            if near:
                pl.when(jnp.logical_not(owns_here))(send)
            else:
                send()

        @pl.when(owns_here)
        def _():
            target[me] = source[my_owner]

    def wait_for_slabs(ref, sem):
        @pl.when(owns_here)
        def _():
            wait_for(ref.at[pl.ds(0, CYCLE - 1)], sem)

        @pl.when(owns_other)
        def _():
            wait_for(ref, sem)

    def wait_for_owners(ref, sem):
        @pl.when(owns_here)
        def _():
            wait_for(ref.at[pl.ds(0, OWNERS - 1)], sem)

        @pl.when(jnp.logical_not(owns_here))
        def _():
            wait_for(ref, sem)

    pl.semaphore_wait(barrier, greeted)
    to_owners(send_absorb, recv_absorb, absorb_send, absorb_recv)
    for s in range(STEPS):
        to_owners(send_out.at[s], recv_out.at[s], out_send.at[s], out_recv.at[s])

    def to_sections(source, target, send_sem, recv_sem):
        for section in far_sections():
            remote(source, target, send_sem, recv_sem, me, section)

    to_sections(send_label, recv_label.at[col], label_send, label_recv)
    recv_label[col] = send_label[...]

    comp_load.wait()
    for s in range(STEPS):
        for h in range(HALVES):

            def widen(i):
                rows = pl.ds(8 * X * i, 8 * X)
                comp_wide[s, h, rows] = comp[s, rows, pl.ds(LANES * h, LANES)].astype(F32)

            loop(M // 8, widen)

            def to_ordinates(i):
                value = jnp.concatenate(
                    [
                        comp_wide[s, h, pl.ds(2 * i, M, stride=X), :],
                        comp_wide[s, h, pl.ds(2 * i + 1, M, stride=X), :],
                    ],
                    axis=1,
                ).astype(BF16)
                result = jnp.dot(left_comp[s], jnp.concatenate([value, value], axis=0), preferred_element_type=F32)
                comp_ordin[s, h, 2 * i] = result[:, :LANES]
                comp_ordin[s, h, 2 * i + 1] = result[:, LANES:]

            loop(X // 2, to_ordinates)

    wait_for(recv_label.at[pl.ds(0, SECTIONS - 1)], label_recv)

    @pl.when(is_owner)
    def _():
        first_own = jnp.broadcast_to(recv_label[served_col, 0:1, :M], (M, M)) == 0.0
        left_own[...] = left_operand(jnp.where(first_own, mids[0], mids[1]))

        wait_for_slabs(recv_absorb, absorb_recv)
        for p in range(CYCLE):
            wide_rows[4 * p : 4 * p + 4] = recv_absorb[p]
        blocks = [(h, g) for h in range(HALVES) for g in range(BLOCKS)]
        for b, (h, g) in enumerate(blocks):
            for j in range(2):
                part = wide_rows[pl.ds(4 * OWNERS * g + 2 * h + j, OWNERS, stride=4), :]
                for i in range(4):
                    rolled = pltpu.roll(part, LANES - 2 * X * i, axis=1) if i else part
                    turned[pl.ds(LANES * (b % 2) + 4 * j + i, OWNERS, stride=OWN), :] = rolled
            by_cell = turned[pl.ds(LANES * (b % 2), LANES)].T
            for s in range(STEPS):
                own_absorb[s, :, pl.ds(LANES * b, LANES)] = by_cell[X * s : X * s + X]
        whole = [{}, {}]
        for b, block in enumerate(blocks):
            whole[0][block] = coefficients(own_absorb.at[0], b, None, None, own_unit.at[b])
            whole[1][block] = coefficients(own_absorb.at[1], b, own_inverse.at[b], own_ratio.at[b], None)
            weights(own_inverse.at[b], own_ratio.at[b], own_weight.at[b])
        for s in range(STEPS):
            for g in range(BLOCKS):
                own_factor[s, pl.ds(LANES * g, LANES)] = jnp.concatenate(
                    [whole[s][h, g] for h in range(HALVES)], axis=0
                ).T

        lane = lax.broadcasted_iota(jnp.int32, (OWN, LANES), 1)
        upward = lax.rem(lane, M) < HALF
        ones, zeros = jnp.ones((OWN, LANES), F32), jnp.zeros((OWN, LANES), F32)

        def placed(slab, k):
            return jnp.where(upward, slab(k), slab(CYCLE - 1 - k))

        def rows_of(ref):
            return lambda k: ref[OWN * k : OWN * k + OWN]

        closing = []
        for s in range(STEPS):
            whole_unit = ones
            for k in range(CYCLE):
                prefix_unit[s, OWN * k : OWN * k + OWN] = whole_unit
                whole_unit = whole_unit * placed(rows_of(own_factor.at[s]), k)
            closing.append(1.0 - whole_unit)

        def solve(s, outflow):
            whole_free = zeros
            for k in range(CYCLE):
                prefix_free[OWN * k : OWN * k + OWN] = whole_free
                whole_free = placed(rows_of(own_factor.at[s]), k) * whole_free + placed(outflow, k)
            entry = whole_free / closing[s]
            for p in range(CYCLE):
                inflow = placed(rows_of(prefix_unit.at[s]), p) * entry + placed(rows_of(prefix_free), p)
                send_flow[s, p] = inflow
                if s == 0:
                    own_flow[OWN * p : OWN * p + OWN] = inflow
            for p, here in far_places():

                def send(p=p):
                    remote(
                        send_flow.at[s, p], recv_flow.at[s, my_owner], flow_send.at[s], flow_recv.at[s], p, served_col
                    )

                if here:
                    pl.when(owns_other)(send)
                else:
                    send()

            @pl.when(owns_here)
            def _():
                recv_flow[s, my_owner] = send_flow[s, me]

        wait_for_slabs(recv_out.at[0], out_recv.at[0])
        solve(0, lambda p: recv_out[0, p])

        added = {}
        for g in range(BLOCKS):
            own_inflow = own_flow[pl.ds(LANES * g, LANES)].T
            for h in range(HALVES):
                b = BLOCKS * h + g
                inflow = own_inflow[M * h : M * h + M]

                def extra(i, outflow):
                    value = jnp.concatenate([own_unit[b, 2 * i] * inflow, own_unit[b, 2 * i + 1] * inflow], axis=1)
                    result = product(left_own[...], value)
                    return (
                        outflow + own_weight[b, 2 * i] * result[:, :LANES] + own_weight[b, 2 * i + 1] * result[:, LANES:]
                    )

                added[h] = loop(X // 2, extra, jnp.zeros((M, LANES), F32))
            own_extra[pl.ds(LANES * g, LANES)] = jnp.concatenate([added[h] for h in range(HALVES)], axis=0).T
        wait_for_slabs(recv_out.at[1], out_recv.at[1])
        solve(1, lambda p: recv_out[1, p] + rows_of(own_extra)(p))

    def inflows(s):
        wait_for_owners(recv_flow.at[s], flow_recv.at[s])
        both = recv_flow[s].reshape(LANES, LANES).T
        return [both[M * h : M * h + M] for h in range(HALVES)]

    inflow_first = inflows(0)
    for h in range(HALVES):
        inflow = inflow_first[h]

        def first_density(i):
            solved = free[0, h, i] + unit[0, h, i] * inflow
            free[0, h, i] = solved
            send_early[pl.ds(X * h + i, 1)] = jnp.sum(solved * comp_ordin[0, h, i], axis=0, keepdims=True)

        loop(X, first_density)
    to_sections(send_early, recv_early.at[col], early_send, early_recv)
    recv_early[col] = send_early[...]
    for h in range(HALVES):

        def middle(i):
            value = jnp.concatenate([free[0, h, 2 * i], free[0, h, 2 * i + 1]], axis=1)
            result = product(left_mid[...], value)
            free[1, h, 2 * i] = result[:, :LANES]
            free[1, h, 2 * i + 1] = result[:, LANES:]

        loop(X // 2, middle)
    for h in range(HALVES):
        sweep(1, h)

    inflow_second = inflows(1)
    for h in range(HALVES):
        inflow = inflow_second[h]

        def last_density(i):
            solved = free[1, h, i] + unit[1, h, i] * inflow
            free[1, h, i] = solved
            send_late[h, pl.ds(i, 1)] = jnp.sum(solved * comp_ordin[1, h, i], axis=0, keepdims=True)

        loop(X, last_density)
    to_sections(send_late, recv_late.at[col], late_send, late_recv)
    recv_late[col] = send_late[...]
    q_store = [
        pltpu.make_async_copy(q_out.at[h], out_ref.at[:, pl.ds(LANES * h, LANES)], store_sem.at[h])
        for h in range(HALVES)
    ]
    for h in range(HALVES):

        def last(i):
            value = jnp.concatenate([free[1, h, 2 * i], free[1, h, 2 * i + 1]], axis=1)
            result = product(left_out[...], value)
            q_out[h, pl.ds(2 * i, M, stride=X), :] = result[:, :LANES]
            q_out[h, pl.ds(2 * i + 1, M, stride=X), :] = result[:, LANES:]

        loop(X // 2, last)
        q_store[h].start()

    wait_for(recv_early.at[pl.ds(0, SECTIONS - 1)], early_recv)

    def add_densities(carry, terms, s):
        def one(c, carry):
            total_a, total_b = carry
            is_a = jnp.broadcast_to(recv_label[c, s : s + 1], (X, LANES)) == 0.0
            term = terms(c)
            return total_a + jnp.where(is_a, term, 0.0), total_b + jnp.where(is_a, 0.0, term)

        return loop(SECTIONS, one, carry)

    none = jnp.zeros((X, LANES), F32)
    early = [add_densities((none, none), lambda c, h=h: recv_early[c, pl.ds(X * h, X)], 0) for h in range(HALVES)]
    for h in range(HALVES):
        if h == 0:
            wait_for(recv_late.at[pl.ds(0, SECTIONS - 1)], late_recv)
        total_a, total_b = add_densities(early[h], lambda c, h=h: recv_late[c, h], 1)
        dens_ref[0, :, pl.ds(LANES * h, LANES)] = total_a
        dens_ref[1, :, pl.ds(LANES * h, LANES)] = total_b

    wait_for(recv_label.at[pl.ds(0, SECTIONS - 1)], label_send)
    wait_for_owners(send_absorb, absorb_send)
    for s in range(STEPS):
        wait_for_owners(send_out.at[s], out_send.at[s])
        wait_for_slabs(send_flow.at[s], flow_send.at[s])
    wait_for(recv_early.at[pl.ds(0, SECTIONS - 1)], early_send)
    wait_for(recv_late.at[pl.ds(0, SECTIONS - 1)], late_send)
    for copy in q_store:
        copy.wait()


def store(q_ref, dens_ref, q_out, dens_out, sem):
    part = M * X // STORES
    copies = [pltpu.make_async_copy(dens_ref, dens_out, sem.at[STORES])]
    for i in range(STORES):
        rows = pl.ds(part * i, part)
        copies.append(pltpu.make_async_copy(q_ref.at[rows], q_out.at[rows], sem.at[i]))
    for copy in copies:
        copy.start()
    for copy in copies:
        copy.wait()


def body(propagator, complement, labels, absorption, to_ordinates, to_modes, upwind, mode_decay):
    rows, lines = M * X, HALVES * LANES
    dma = pltpu.SemaphoreType.DMA
    anywhere = pl.BlockSpec(memory_space=pl.ANY)
    left = pltpu.VMEM((M, 3 * M), BF16)
    half_cells = pltpu.VMEM((HALVES, X, M, LANES), F32)
    cells = pltpu.VMEM((STEPS, HALVES, X, M, LANES), F32)
    own_cells = pltpu.VMEM((HALVES * BLOCKS, X, M, LANES), F32)
    by_line = pltpu.VMEM((CYCLE * OWN, LANES), F32)
    both_by_line = pltpu.VMEM((STEPS, CYCLE * OWN, LANES), F32)
    by_owner = pltpu.VMEM((STEPS, OWNERS, OWN, LANES), F32)
    by_slab = pltpu.VMEM((STEPS, CYCLE, OWN, LANES), F32)
    scratch = [
        pltpu.VMEM((HALVES, rows, LANES), F32),
        pltpu.VMEM((HALVES, rows, LANES), F32),
        pltpu.VMEM((STEPS, rows, lines), BF16),
        pltpu.SMEM((1, STEPS), jnp.int32),
        pltpu.VMEM((2, X, lines), F32),
        pltpu.VMEM((M, M), F32),
        pltpu.VMEM((M, M), F32),
        pltpu.VMEM((1, M), F32),
        pltpu.VMEM((2, M), F32),
        pltpu.VMEM((M, LANES), F32),
        pltpu.VMEM((STEPS, X, lines), F32),
        left,
        left,
        left,
        pltpu.VMEM((STEPS, M, 2 * M), BF16),
        pltpu.VMEM((2, M, M), F32),
        left,
        cells,
        cells,
        cells,
        cells,
        half_cells,
        pltpu.VMEM((STEPS, HALVES, rows, LANES), F32),
        cells,
        pltpu.VMEM((HALVES * LANES, LANES), F32),
        pltpu.VMEM((OWNERS, 4, LANES), F32),
        pltpu.VMEM((CYCLE, 4, LANES), F32),
        pltpu.VMEM((4 * CYCLE, LANES), F32),
        pltpu.VMEM((STEPS, X, BLOCKS * lines), F32),
        own_cells,
        own_cells,
        own_cells,
        own_cells,
        by_owner,
        by_slab,
        both_by_line,
        both_by_line,
        by_line,
        by_line,
        by_line,
        by_slab,
        by_owner,
        pltpu.VMEM((8, LANES), F32),
        pltpu.VMEM((SECTIONS, 8, LANES), F32),
        pltpu.VMEM((HALVES * X, LANES), F32),
        pltpu.VMEM((SECTIONS, HALVES * X, LANES), F32),
        pltpu.VMEM((HALVES, X, LANES), F32),
        pltpu.VMEM((SECTIONS, HALVES, X, LANES), F32),
        dma((6,)),
        dma((HALVES,)),
        dma,
        dma,
        dma,
        dma((STEPS,)),
        dma((STEPS,)),
        dma((STEPS,)),
        dma((STEPS,)),
        dma,
        dma,
        dma,
        dma,
        dma,
        dma,
        dma((HALVES,)),
    ]
    propagated, density = pl.pallas_call(
        kernel,
        out_shape=(
            jax.ShapeDtypeStruct((rows, lines), F32),
            jax.ShapeDtypeStruct((2, X, lines), F32),
        ),
        in_specs=[anywhere] * 8,
        out_specs=(anywhere, pl.BlockSpec(memory_space=pltpu.VMEM)),
        scratch_shapes=scratch,
        compiler_params=pltpu.CompilerParams(
            collective_id=0, has_side_effects=True, vmem_limit_bytes=48 * 1024 * 1024
        ),
        name="contour_steps",
    )(
        *(
            pltpu.with_memory_space_constraint(operand, pltpu.HBM)
            for operand in (
                propagator.reshape(rows, lines),
                complement.reshape(STEPS, rows, lines),
                labels,
                absorption,
                to_ordinates,
                to_modes,
                upwind.reshape(1, M),
                mode_decay,
            )
        )
    )
    propagated, density = pl.pallas_call(
        store,
        out_shape=(
            jax.ShapeDtypeStruct((rows, lines), F32),
            jax.ShapeDtypeStruct((2, X, lines), F32),
        ),
        in_specs=[anywhere] * 2,
        out_specs=(anywhere, anywhere),
        scratch_shapes=[dma((STORES + 1,))],
        compiler_params=pltpu.CompilerParams(vmem_limit_bytes=1024 * 1024),
        name="store_results",
    )(propagated, density)
    return propagated.reshape(1, M, X, lines), density


def solution(mesh):
    in_specs = (
        P("col", None, "gx", None),
        P("col", None, None, "gx", None),
        P("col", None),
        P(None, "gx", None),
        P(),
        P(),
        P(),
        P(),
    )
    out_specs = (P("col", None, "gx", None), P(None, "gx", None))
    return jax.shard_map(body, mesh=mesh, in_specs=in_specs, out_specs=out_specs, check_vma=False)
```

```python
import jax
import jax.numpy as jnp
from jax import lax
from jax.experimental import pallas as pl
from jax.experimental.pallas import tpu as pltpu
from jax.sharding import PartitionSpec as P

F32, BF16 = jnp.float32, jnp.bfloat16
M = 64
HALF = M // 2
X = 16
LANES = 128
HALVES = 2
STEPS = 2
CYCLE, SECTIONS = 32, 8
OWN = 8
OWNERS = LANES // OWN
BLOCKS = 2
RING_Z, RING_Y, RING_X = 8, 4, 4
FAR_Z, FAR_Y, FAR_X = (4, 3, 5, 2, 6, 1, 7, 0), (2, 1, 3, 0), (2, 1, 3, 0)
STORES = 1


def loop(count, step, carry=None):
    if carry is None:

        def plain(i, none):
            step(i)
            return none

        lax.fori_loop(0, count, plain, 0, unroll=True)
        return None
    return lax.fori_loop(0, count, step, carry, unroll=True)


def column(row):
    wide = jnp.broadcast_to(row, (M, M))
    here = lax.broadcasted_iota(jnp.int32, (M, M), 0) == lax.broadcasted_iota(jnp.int32, (M, M), 1)
    return jnp.sum(jnp.where(here, wide, 0.0), axis=1, keepdims=True)


def split(value):
    high = value.astype(BF16)
    low = (value - high.astype(F32)).astype(BF16)
    return high, low


def left_operand(weights):
    high, low = split(weights)
    return jnp.concatenate([high, high, low], axis=1)


def product(left, value):
    high, low = split(value)
    right = jnp.concatenate([high, low, high], axis=0)
    return jnp.dot(left, right, preferred_element_type=F32)


def wait_for(ref, sem):
    pltpu.make_async_copy(ref, ref, sem).wait()


def kernel(
    prop_ref,
    comp_ref,
    labels_ref,
    absorb_ref,
    ordin_ref,
    modes_ref,
    upwind_ref,
    decay_ref,
    out_ref,
    dens_ref,
    q_in,
    q_out,
    comp,
    labels,
    absorb,
    ordin,
    modes,
    upwind,
    decay,
    rate,
    absorb_now,
    left_in,
    left_mid,
    left_out,
    left_comp,
    mids,
    left_own,
    inverse,
    ratio,
    unit,
    free,
    weight,
    comp_wide,
    comp_ordin,
    turned,
    send_absorb,
    recv_absorb,
    wide_rows,
    own_absorb,
    own_inverse,
    own_ratio,
    own_unit,
    own_weight,
    send_out,
    recv_out,
    own_factor,
    prefix_unit,
    prefix_free,
    own_flow,
    own_extra,
    send_flow,
    recv_flow,
    send_label,
    recv_label,
    send_early,
    recv_early,
    send_late,
    recv_late,
    load_sem,
    q_sem,
    comp_sem,
    absorb_send,
    absorb_recv,
    out_send,
    out_recv,
    flow_send,
    flow_recv,
    label_send,
    label_recv,
    early_send,
    early_recv,
    late_send,
    late_recv,
    store_sem,
):
    me = lax.axis_index("gx")
    col = lax.axis_index("col")
    core = lax.rem(col, 2)
    my_z, my_y, my_x = me // RING_Y, lax.rem(me, RING_Y), col // 2
    is_owner = core == 1
    parity = lax.rem(my_z + my_y, 2)
    owns_here = jnp.logical_and(is_owner, parity == 1)
    owns_other = jnp.logical_and(is_owner, parity == 0)
    my_owner = 2 * my_z + my_y // 2
    owner_col = col - core + 1
    served_col = col - 1 + parity

    def far_places():
        for dz in FAR_Z:
            for dy in FAR_Y:
                yield RING_Y * lax.rem(my_z + dz, RING_Z) + lax.rem(my_y + dy, RING_Y), (dz, dy) == (0, 0)

    def far_owners():
        for dz in FAR_Z:
            for dh in (1, 0):
                z, h = lax.rem(my_z + dz, RING_Z), lax.rem(my_y // 2 + dh, 2)
                yield 2 * z + h, RING_Y * z + 2 * h + lax.rem(z + core, 2), (dz, dh) == (0, 0)

    def far_sections():
        for dx in FAR_X:
            for dc in range(2):
                if (dx, dc) != (0, 0):
                    yield 2 * lax.rem(my_x + dx, RING_X) + lax.rem(core + dc, 2)

    barrier = pltpu.get_barrier_semaphore()

    def greet(place, section):
        pl.semaphore_signal(
            barrier, inc=1, device_id={"gx": place, "col": section}, device_id_type=pl.DeviceIdType.MESH
        )

    @pl.when(owns_here)
    def _():
        for place, here in far_places():
            if not here:
                greet(place, col)

    @pl.when(owns_other)
    def _():
        for place, here in far_places():
            greet(place, served_col)

    @pl.when(jnp.logical_not(owns_here))
    def _():
        for o, place, near in far_owners():
            greet(place, owner_col)

    for section in far_sections():
        greet(me, section)
    greeted = jnp.where(owns_here, CYCLE - 1, jnp.where(owns_other, CYCLE + OWNERS, OWNERS)) + SECTIONS - 1

    small = [
        pltpu.make_async_copy(src, dst, load_sem.at[i])
        for i, (src, dst) in enumerate(
            (
                (absorb_ref, absorb),
                (upwind_ref, upwind),
                (labels_ref, labels),
                (ordin_ref, ordin),
                (modes_ref, modes),
                (decay_ref, decay),
            )
        )
    ]
    for copy in small:
        copy.start()
    q_load = [
        pltpu.make_async_copy(prop_ref.at[:, pl.ds(LANES * h, LANES)], q_in.at[h], q_sem.at[h])
        for h in range(HALVES)
    ]
    for copy in q_load:
        copy.start()
    comp_load = pltpu.make_async_copy(comp_ref, comp, comp_sem)
    comp_load.start()
    for copy in small:
        copy.wait()

    rate[...] = jnp.broadcast_to(column(upwind[...]), (M, LANES))
    first = [labels[0, s] == 0 for s in range(STEPS)]
    for s in range(STEPS):
        absorb_now[s] = jnp.where(first[s], absorb[0], absorb[1])
    left_in[...] = left_operand(ordin[...])

    def coefficients(rows, h, inverse, ratio, unit):
        def one(i, carry):
            up, down = carry
            lanes = pl.ds(LANES * h, LANES)
            j = X - 1 - i
            rate_up, rate_down = rate[:HALF], rate[HALF:]
            inverse_up = 1.0 / (1.0 + rate_up + rows[pl.ds(i, 1), lanes])
            inverse_down = 1.0 / (1.0 + rate_down + rows[pl.ds(j, 1), lanes])
            ratio_up = rate_up * inverse_up
            ratio_down = rate_down * inverse_down
            up = up * ratio_up
            down = down * ratio_down
            if inverse is not None:
                inverse[i, :HALF] = inverse_up
                inverse[j, HALF:] = inverse_down
                ratio[i, :HALF] = ratio_up
                ratio[j, HALF:] = ratio_down
            if unit is not None:
                unit[i, :HALF] = up
                unit[j, HALF:] = down
            return up, down

        ones = jnp.ones((HALF, LANES), F32)
        return jnp.concatenate(loop(X, one, (ones, ones)), axis=0)

    def weights(inverse, ratio, weight):
        def one(i, carry):
            up, down = carry
            j = X - 1 - i
            weight[j, :HALF] = inverse[j, :HALF] * up
            weight[i, HALF:] = inverse[i, HALF:] * down
            return up * ratio[j, :HALF], down * ratio[i, HALF:]

        ones = jnp.ones((HALF, LANES), F32)
        loop(X, one, (ones, ones))

    def sweep(s, h):
        def one(i, carry):
            up, down = carry
            j = X - 1 - i
            up = free[s, h, i, :HALF] * inverse[s, h, i, :HALF] + ratio[s, h, i, :HALF] * up
            down = free[s, h, j, HALF:] * inverse[s, h, j, HALF:] + ratio[s, h, j, HALF:] * down
            free[s, h, i, :HALF] = up
            free[s, h, j, HALF:] = down
            return up, down

        zeros = jnp.zeros((HALF, LANES), F32)
        return jnp.concatenate(loop(X, one, (zeros, zeros)), axis=0)

    wide = jnp.concatenate([absorb_now[0], absorb_now[1], jnp.zeros((LANES - 2 * X, 2 * LANES), F32)], axis=0)
    turned[...] = wide.T
    for h in range(HALVES):
        for j in range(2):
            base = LANES * h + 4 * j
            packed = turned[pl.ds(base, OWNERS, stride=OWN), :]
            for i in range(1, 4):
                packed = packed + pltpu.roll(turned[pl.ds(base + i, OWNERS, stride=OWN), :], 2 * X * i, axis=1)
            wide_rows[pl.ds(2 * h + j, OWNERS, stride=4), :] = packed
    for o in range(OWNERS):
        send_absorb[o] = wide_rows[4 * o : 4 * o + 4]

    for h in range(HALVES):
        for s in range(STEPS):
            coefficients(absorb_now.at[s], h, inverse.at[s, h], ratio.at[s, h], unit.at[s, h])
        weights(inverse.at[1, h], ratio.at[1, h], weight.at[h])
    gained = []
    for s in range(STEPS):
        gain = jnp.where(first[s], decay[0:1], decay[1:2])
        gained.append(column(gain) * modes[...])
        left_comp[s] = jnp.concatenate(split(gained[s].T), axis=1)
    for species in range(2):
        mids[species] = jnp.dot(
            ordin[...],
            column(decay[species : species + 1]) * modes[...],
            preferred_element_type=F32,
            precision=lax.Precision.HIGHEST,
        )
    left_mid[...] = left_operand(jnp.where(first[0], mids[0], mids[1]))
    for s in range(STEPS):
        send_label[s : s + 1] = jnp.broadcast_to(labels[0, s].astype(F32), (1, LANES))
    send_label[STEPS:] = jnp.zeros((8 - STEPS, LANES), F32)
    left_out[...] = left_operand(gained[1])
    outflows = [[], []]
    for h in range(HALVES):
        q_load[h].wait()

        def sources(i):
            value = jnp.concatenate(
                [q_in[h, pl.ds(2 * i, M, stride=X), :], q_in[h, pl.ds(2 * i + 1, M, stride=X), :]], axis=1
            )
            result = product(left_in[...], value)
            free[0, h, 2 * i] = result[:, :LANES]
            free[0, h, 2 * i + 1] = result[:, LANES:]

        loop(X // 2, sources)
        outflows[0].append(sweep(0, h))

        def sources_free(i, outflow):
            value = jnp.concatenate([free[0, h, 2 * i], free[0, h, 2 * i + 1]], axis=1)
            result = product(left_mid[...], value)
            return outflow + weight[h, 2 * i] * result[:, :LANES] + weight[h, 2 * i + 1] * result[:, LANES:]

        outflows[1].append(loop(X // 2, sources_free, jnp.zeros((M, LANES), F32)))
    for s in range(STEPS):
        send_out[s] = jnp.concatenate(outflows[s], axis=0).T.reshape(OWNERS, OWN, LANES)

    def remote(source, target, send_sem, recv_sem, place, section):
        pltpu.make_async_remote_copy(
            src_ref=source,
            dst_ref=target,
            send_sem=send_sem,
            recv_sem=recv_sem,
            device_id={"gx": place, "col": section},
            device_id_type=pl.DeviceIdType.MESH,
        ).start()

    def to_owners(source, target, send_sem, recv_sem):
        for o, place, near in far_owners():

            def send(o=o, place=place):
                remote(source.at[o], target.at[me], send_sem, recv_sem, place, owner_col)

            if near:
                pl.when(jnp.logical_not(owns_here))(send)
            else:
                send()

        @pl.when(owns_here)
        def _():
            target[me] = source[my_owner]

    def wait_for_slabs(ref, sem):
        @pl.when(owns_here)
        def _():
            wait_for(ref.at[pl.ds(0, CYCLE - 1)], sem)

        @pl.when(owns_other)
        def _():
            wait_for(ref, sem)

    def wait_for_owners(ref, sem):
        @pl.when(owns_here)
        def _():
            wait_for(ref.at[pl.ds(0, OWNERS - 1)], sem)

        @pl.when(jnp.logical_not(owns_here))
        def _():
            wait_for(ref, sem)

    pl.semaphore_wait(barrier, greeted)
    to_owners(send_absorb, recv_absorb, absorb_send, absorb_recv)
    for s in range(STEPS):
        to_owners(send_out.at[s], recv_out.at[s], out_send.at[s], out_recv.at[s])

    def to_sections(source, target, send_sem, recv_sem):
        for section in far_sections():
            remote(source, target, send_sem, recv_sem, me, section)

    to_sections(send_label, recv_label.at[col], label_send, label_recv)
    recv_label[col] = send_label[...]

    comp_load.wait()
    for s in range(STEPS):
        for h in range(HALVES):

            def widen(i):
                rows = pl.ds(8 * X * i, 8 * X)
                comp_wide[s, h, rows] = comp[s, rows, pl.ds(LANES * h, LANES)].astype(F32)

            loop(M // 8, widen)

            def to_ordinates(i):
                value = jnp.concatenate(
                    [
                        comp_wide[s, h, pl.ds(2 * i, M, stride=X), :],
                        comp_wide[s, h, pl.ds(2 * i + 1, M, stride=X), :],
                    ],
                    axis=1,
                ).astype(BF16)
                result = jnp.dot(left_comp[s], jnp.concatenate([value, value], axis=0), preferred_element_type=F32)
                comp_ordin[s, h, 2 * i] = result[:, :LANES]
                comp_ordin[s, h, 2 * i + 1] = result[:, LANES:]

            loop(X // 2, to_ordinates)

    wait_for(recv_label.at[pl.ds(0, SECTIONS - 1)], label_recv)

    @pl.when(is_owner)
    def _():
        first_own = jnp.broadcast_to(recv_label[served_col, 0:1, :M], (M, M)) == 0.0
        left_own[...] = left_operand(jnp.where(first_own, mids[0], mids[1]))

        wait_for_slabs(recv_absorb, absorb_recv)
        for p in range(CYCLE):
            wide_rows[4 * p : 4 * p + 4] = recv_absorb[p]
        blocks = [(h, g) for h in range(HALVES) for g in range(BLOCKS)]
        for b, (h, g) in enumerate(blocks):
            for j in range(2):
                part = wide_rows[pl.ds(4 * OWNERS * g + 2 * h + j, OWNERS, stride=4), :]
                for i in range(4):
                    rolled = pltpu.roll(part, LANES - 2 * X * i, axis=1) if i else part
                    turned[pl.ds(LANES * (b % 2) + 4 * j + i, OWNERS, stride=OWN), :] = rolled
            by_cell = turned[pl.ds(LANES * (b % 2), LANES)].T
            for s in range(STEPS):
                own_absorb[s, :, pl.ds(LANES * b, LANES)] = by_cell[X * s : X * s + X]
        whole = [{}, {}]
        for b, block in enumerate(blocks):
            whole[0][block] = coefficients(own_absorb.at[0], b, None, None, own_unit.at[b])
            whole[1][block] = coefficients(own_absorb.at[1], b, own_inverse.at[b], own_ratio.at[b], None)
            weights(own_inverse.at[b], own_ratio.at[b], own_weight.at[b])
        for s in range(STEPS):
            for g in range(BLOCKS):
                own_factor[s, pl.ds(LANES * g, LANES)] = jnp.concatenate(
                    [whole[s][h, g] for h in range(HALVES)], axis=0
                ).T

        lane = lax.broadcasted_iota(jnp.int32, (OWN, LANES), 1)
        upward = lax.rem(lane, M) < HALF
        ones, zeros = jnp.ones((OWN, LANES), F32), jnp.zeros((OWN, LANES), F32)

        def placed(slab, k):
            return jnp.where(upward, slab(k), slab(CYCLE - 1 - k))

        def rows_of(ref):
            return lambda k: ref[OWN * k : OWN * k + OWN]

        closing = []
        for s in range(STEPS):
            whole_unit = ones
            for k in range(CYCLE):
                prefix_unit[s, OWN * k : OWN * k + OWN] = whole_unit
                whole_unit = whole_unit * placed(rows_of(own_factor.at[s]), k)
            closing.append(1.0 - whole_unit)

        def solve(s, outflow):
            whole_free = zeros
            for k in range(CYCLE):
                prefix_free[OWN * k : OWN * k + OWN] = whole_free
                whole_free = placed(rows_of(own_factor.at[s]), k) * whole_free + placed(outflow, k)
            entry = whole_free / closing[s]
            for p in range(CYCLE):
                inflow = placed(rows_of(prefix_unit.at[s]), p) * entry + placed(rows_of(prefix_free), p)
                send_flow[s, p] = inflow
                if s == 0:
                    own_flow[OWN * p : OWN * p + OWN] = inflow
            for p, here in far_places():

                def send(p=p):
                    remote(
                        send_flow.at[s, p], recv_flow.at[s, my_owner], flow_send.at[s], flow_recv.at[s], p, served_col
                    )

                if here:
                    pl.when(owns_other)(send)
                else:
                    send()

            @pl.when(owns_here)
            def _():
                recv_flow[s, my_owner] = send_flow[s, me]

        wait_for_slabs(recv_out.at[0], out_recv.at[0])
        solve(0, lambda p: recv_out[0, p])

        added = {}
        for g in range(BLOCKS):
            own_inflow = own_flow[pl.ds(LANES * g, LANES)].T
            for h in range(HALVES):
                b = BLOCKS * h + g
                inflow = own_inflow[M * h : M * h + M]

                def extra(i, outflow):
                    value = jnp.concatenate([own_unit[b, 2 * i] * inflow, own_unit[b, 2 * i + 1] * inflow], axis=1)
                    result = product(left_own[...], value)
                    return (
                        outflow + own_weight[b, 2 * i] * result[:, :LANES] + own_weight[b, 2 * i + 1] * result[:, LANES:]
                    )

                added[h] = loop(X // 2, extra, jnp.zeros((M, LANES), F32))
            own_extra[pl.ds(LANES * g, LANES)] = jnp.concatenate([added[h] for h in range(HALVES)], axis=0).T
        wait_for_slabs(recv_out.at[1], out_recv.at[1])
        solve(1, lambda p: recv_out[1, p] + rows_of(own_extra)(p))

    def inflows(s):
        wait_for_owners(recv_flow.at[s], flow_recv.at[s])
        both = recv_flow[s].reshape(LANES, LANES).T
        return [both[M * h : M * h + M] for h in range(HALVES)]

    inflow_first = inflows(0)
    for h in range(HALVES):
        inflow = inflow_first[h]

        def first_density(i):
            solved = free[0, h, i] + unit[0, h, i] * inflow
            free[0, h, i] = solved
            send_early[pl.ds(X * h + i, 1)] = jnp.sum(solved * comp_ordin[0, h, i], axis=0, keepdims=True)

        loop(X, first_density)
    to_sections(send_early, recv_early.at[col], early_send, early_recv)
    recv_early[col] = send_early[...]
    for h in range(HALVES):

        def middle(i):
            value = jnp.concatenate([free[0, h, 2 * i], free[0, h, 2 * i + 1]], axis=1)
            result = product(left_mid[...], value)
            free[1, h, 2 * i] = result[:, :LANES]
            free[1, h, 2 * i + 1] = result[:, LANES:]

        loop(X // 2, middle)
    for h in range(HALVES):
        sweep(1, h)

    inflow_second = inflows(1)
    for h in range(HALVES):
        inflow = inflow_second[h]

        def last_density(i):
            solved = free[1, h, i] + unit[1, h, i] * inflow
            free[1, h, i] = solved
            send_late[h, pl.ds(i, 1)] = jnp.sum(solved * comp_ordin[1, h, i], axis=0, keepdims=True)

        loop(X, last_density)
    to_sections(send_late, recv_late.at[col], late_send, late_recv)
    recv_late[col] = send_late[...]
    q_store = [
        pltpu.make_async_copy(q_out.at[h], out_ref.at[:, pl.ds(LANES * h, LANES)], store_sem.at[h])
        for h in range(HALVES)
    ]
    for h in range(HALVES):

        def last(i):
            value = jnp.concatenate([free[1, h, 2 * i], free[1, h, 2 * i + 1]], axis=1)
            result = product(left_out[...], value)
            q_out[h, pl.ds(2 * i, M, stride=X), :] = result[:, :LANES]
            q_out[h, pl.ds(2 * i + 1, M, stride=X), :] = result[:, LANES:]

        loop(X // 2, last)
        q_store[h].start()

    wait_for(recv_early.at[pl.ds(0, SECTIONS - 1)], early_recv)

    def add_densities(carry, terms, s):
        def one(c, carry):
            total_a, total_b = carry
            is_a = jnp.broadcast_to(recv_label[c, s : s + 1], (X, LANES)) == 0.0
            term = terms(c)
            return total_a + jnp.where(is_a, term, 0.0), total_b + jnp.where(is_a, 0.0, term)

        return loop(SECTIONS, one, carry)

    none = jnp.zeros((X, LANES), F32)
    early = [add_densities((none, none), lambda c, h=h: recv_early[c, pl.ds(X * h, X)], 0) for h in range(HALVES)]
    for h in range(HALVES):
        if h == 0:
            wait_for(recv_late.at[pl.ds(0, SECTIONS - 1)], late_recv)
        total_a, total_b = add_densities(early[h], lambda c, h=h: recv_late[c, h], 1)
        dens_ref[0, :, pl.ds(LANES * h, LANES)] = total_a
        dens_ref[1, :, pl.ds(LANES * h, LANES)] = total_b

    wait_for(recv_label.at[pl.ds(0, SECTIONS - 1)], label_send)
    wait_for_owners(send_absorb, absorb_send)
    for s in range(STEPS):
        wait_for_owners(send_out.at[s], out_send.at[s])
        wait_for_slabs(send_flow.at[s], flow_send.at[s])
    wait_for(recv_early.at[pl.ds(0, SECTIONS - 1)], early_send)
    wait_for(recv_late.at[pl.ds(0, SECTIONS - 1)], late_send)
    for copy in q_store:
        copy.wait()


def store(q_ref, dens_ref, q_out, dens_out, sem):
    part = M * X // STORES
    copies = [pltpu.make_async_copy(dens_ref, dens_out, sem.at[STORES])]
    for i in range(STORES):
        rows = pl.ds(part * i, part)
        copies.append(pltpu.make_async_copy(q_ref.at[rows], q_out.at[rows], sem.at[i]))
    for copy in copies:
        copy.start()
    for copy in copies:
        copy.wait()


def body(propagator, complement, labels, absorption, to_ordinates, to_modes, upwind, mode_decay):
    rows, lines = M * X, HALVES * LANES
    dma = pltpu.SemaphoreType.DMA
    anywhere = pl.BlockSpec(memory_space=pl.ANY)
    left = pltpu.VMEM((M, 3 * M), BF16)
    half_cells = pltpu.VMEM((HALVES, X, M, LANES), F32)
    cells = pltpu.VMEM((STEPS, HALVES, X, M, LANES), F32)
    own_cells = pltpu.VMEM((HALVES * BLOCKS, X, M, LANES), F32)
    by_line = pltpu.VMEM((CYCLE * OWN, LANES), F32)
    both_by_line = pltpu.VMEM((STEPS, CYCLE * OWN, LANES), F32)
    by_owner = pltpu.VMEM((STEPS, OWNERS, OWN, LANES), F32)
    by_slab = pltpu.VMEM((STEPS, CYCLE, OWN, LANES), F32)
    scratch = [
        pltpu.VMEM((HALVES, rows, LANES), F32),
        pltpu.VMEM((HALVES, rows, LANES), F32),
        pltpu.VMEM((STEPS, rows, lines), BF16),
        pltpu.SMEM((1, STEPS), jnp.int32),
        pltpu.VMEM((2, X, lines), F32),
        pltpu.VMEM((M, M), F32),
        pltpu.VMEM((M, M), F32),
        pltpu.VMEM((1, M), F32),
        pltpu.VMEM((2, M), F32),
        pltpu.VMEM((M, LANES), F32),
        pltpu.VMEM((STEPS, X, lines), F32),
        left,
        left,
        left,
        pltpu.VMEM((STEPS, M, 2 * M), BF16),
        pltpu.VMEM((2, M, M), F32),
        left,
        cells,
        cells,
        cells,
        cells,
        half_cells,
        pltpu.VMEM((STEPS, HALVES, rows, LANES), F32),
        cells,
        pltpu.VMEM((HALVES * LANES, LANES), F32),
        pltpu.VMEM((OWNERS, 4, LANES), F32),
        pltpu.VMEM((CYCLE, 4, LANES), F32),
        pltpu.VMEM((4 * CYCLE, LANES), F32),
        pltpu.VMEM((STEPS, X, BLOCKS * lines), F32),
        own_cells,
        own_cells,
        own_cells,
        own_cells,
        by_owner,
        by_slab,
        both_by_line,
        both_by_line,
        by_line,
        by_line,
        by_line,
        by_slab,
        by_owner,
        pltpu.VMEM((8, LANES), F32),
        pltpu.VMEM((SECTIONS, 8, LANES), F32),
        pltpu.VMEM((HALVES * X, LANES), F32),
        pltpu.VMEM((SECTIONS, HALVES * X, LANES), F32),
        pltpu.VMEM((HALVES, X, LANES), F32),
        pltpu.VMEM((SECTIONS, HALVES, X, LANES), F32),
        dma((6,)),
        dma((HALVES,)),
        dma,
        dma,
        dma,
        dma((STEPS,)),
        dma((STEPS,)),
        dma((STEPS,)),
        dma((STEPS,)),
        dma,
        dma,
        dma,
        dma,
        dma,
        dma,
        dma((HALVES,)),
    ]
    propagated, density = pl.pallas_call(
        kernel,
        out_shape=(
            jax.ShapeDtypeStruct((rows, lines), F32),
            jax.ShapeDtypeStruct((2, X, lines), F32),
        ),
        in_specs=[anywhere] * 8,
        out_specs=(anywhere, pl.BlockSpec(memory_space=pltpu.VMEM)),
        scratch_shapes=scratch,
        compiler_params=pltpu.CompilerParams(
            collective_id=0, has_side_effects=True, vmem_limit_bytes=48 * 1024 * 1024
        ),
        name="contour_steps",
    )(
        *(
            pltpu.with_memory_space_constraint(operand, pltpu.HBM)
            for operand in (
                propagator.reshape(rows, lines),
                complement.reshape(STEPS, rows, lines),
                labels,
                absorption,
                to_ordinates,
                to_modes,
                upwind.reshape(1, M),
                mode_decay,
            )
        )
    )
    propagated, density = pl.pallas_call(
        store,
        out_shape=(
            jax.ShapeDtypeStruct((rows, lines), F32),
            jax.ShapeDtypeStruct((2, X, lines), F32),
        ),
        in_specs=[anywhere] * 2,
        out_specs=(anywhere, anywhere),
        scratch_shapes=[dma((STORES + 1,))],
        compiler_params=pltpu.CompilerParams(vmem_limit_bytes=1024 * 1024),
        name="store_results",
    )(propagated, density)
    return propagated.reshape(1, M, X, lines), density


def solution(mesh):
    in_specs = (
        P("col", None, "gx", None),
        P("col", None, None, "gx", None),
        P("col", None),
        P(None, "gx", None),
        P(),
        P(),
        P(),
        P(),
    )
    out_specs = (P("col", None, "gx", None), P(None, "gx", None))
    return jax.shard_map(body, mesh=mesh, in_specs=in_specs, out_specs=out_specs, check_vma=False)
```
